32 devices in a mesh: ctx: 4 (over x, core), fsdp: 8 (over z, y).
Axes of the slice: x: 2, y: 2, z: 4, core: 2. Of those that a mesh axis runs over, the one named last changes fastest.
Arguments:
- tokens: bfloat16 [8, 1024, 1024], P('fsdp', 'ctx'), may hold values from -6 to 6
- teacher: bfloat16 [8, 1024, 1024], P('fsdp', 'ctx'), may hold values from -6 to 6
- segment_ids: int32 [8, 1024], P('fsdp'), may hold values from 0 to 5, as said below
- valid_mask: int32 [8, 1024], P('fsdp', 'ctx'), may hold values from 0 to 1, as said below
- gain_in: bfloat16 [1024], P('fsdp'), may hold values from 0.5 to 1.5
- w_in: bfloat16 [1024, 3352], P('fsdp'), may hold values from -0.1875 to 0.1875
- conv_w: bfloat16 [4, 1792], P(None, 'fsdp'), may hold values from -3 to 3
- conv_b: bfloat16 [1792], P('fsdp'), may hold values from -3 to 3
- dt_bias: float32 [24], replicated, may hold values from -2 to 1
- a_log: float32 [24], replicated, may hold values from -10.4 to -3
- d_skip: float32 [24], replicated, may hold values from 0.5 to 1.5
- gain_m: bfloat16 [1536], P('fsdp'), may hold values from 0.5 to 1.5
- w_out: bfloat16 [1536, 1024], P('fsdp'), may hold values from -0.15625 to 0.15625
- w_qkv: bfloat16 [1024, 768], P('fsdp'), may hold values from -0.1875 to 0.1875
- w_o: bfloat16 [512, 1024], P('fsdp'), may hold values from -3.5 to 3.5
- gain_ffn: bfloat16 [1024], P('fsdp'), may hold values from 0.5 to 1.5
- w_gate: bfloat16 [1024, 2048], P('fsdp'), may hold values from -0.1875 to 0.1875
- w_up: bfloat16 [1024, 2048], P('fsdp'), may hold values from -0.1875 to 0.1875
- w_down: bfloat16 [2048, 1024], P('fsdp'), may hold values from -0.125 to 0.125
Outputs:
- loss: float32 [], replicated
- layer_out: float32 [8, 1024, 1024], P('fsdp', 'ctx')
- grad_tokens: float32 [8, 1024, 1024], P('fsdp', 'ctx')
- grad_gain_in: float32 [1024], P('fsdp')
- grad_w_in: float32 [1024, 3352], P('fsdp')
- grad_conv_w: float32 [4, 1792], P(None, 'fsdp')
- grad_conv_b: float32 [1792], P('fsdp')
- grad_dt_bias: float32 [24], replicated
- grad_a_log: float32 [24], replicated
- grad_d_skip: float32 [24], replicated
- grad_gain_m: float32 [1536], P('fsdp')
- grad_w_out: float32 [1536, 1024], P('fsdp')
- grad_w_qkv: float32 [1024, 768], P('fsdp')
- grad_w_o: float32 [512, 1024], P('fsdp')
- grad_gain_ffn: float32 [1024], P('fsdp')
- grad_w_gate: float32 [1024, 2048], P('fsdp')
- grad_w_up: float32 [1024, 2048], P('fsdp')
- grad_w_down: float32 [2048, 1024], P('fsdp')
The draws below stay inside these ranges and needn't reach their ends.
Inputs may be any that keep to these rules, and one draw needn't show every extreme that they name: `segment_ids`: segment numbers start at 0 in each sequence and rise by one at each document's first token; every document but the last of a sequence has 200 to 2000 tokens, the last one at most 2000; in the first sequence every document but the last has exactly 200 tokens. `valid_mask`: the first token of every sequence is valid.
All inputs are finite; a program needn't handle non-finite values.
Results may differ from the reference program's by a relative error of at most 0.019.
Values may be sent and summed in bfloat16 or wider, within the bound.
No kernel may reach another device: no remote copies, remote signals or barrier semaphores. Data moves between devices by JAX's collectives and lax.ppermute only.
A program may use at most 192 MiB of HBM per device.

```python
import jax
import jax.numpy as jnp
from jax import lax

D = 1024
MH = 24
HP = 64
NS = 128
KW = 4
QH = 8
KVH = 2
HD = 64
FF = 2048
SPAN = 128
DOC_MIN = 200
DOC_MAX = 2000
TOK_DEV = 256
LEN = 1024
SEQS = 8
TOKENS = 8192
DI = 1536
CONVCH = 1792


def draw_segment_ids(key, part):
    docs = LEN // DOC_MIN + 1
    sizes = jax.random.randint(key, (SEQS, docs), DOC_MIN, DOC_MAX + 1)
    first_row = (jnp.arange(SEQS, dtype=jnp.int32) == 0)[:, None]
    sizes = jnp.where(first_row, jnp.int32(DOC_MIN), sizes).astype(jnp.int32)
    ends = jnp.cumsum(sizes, axis=1)
    positions = jnp.arange(LEN, dtype=jnp.int32)
    return jnp.sum((ends[:, None, :] <= positions[None, :, None]).astype(jnp.int32), axis=2).astype(jnp.int32)


def draw_valid_mask(key, part):
    total = SEQS * LEN
    index = jnp.arange(total, dtype=jnp.int32).reshape(SEQS, LEN)
    limit = 1024 + 2048 * index // total
    rolls = jax.random.randint(key, (SEQS, LEN), 0, 4096)
    leading = (jnp.arange(LEN, dtype=jnp.int32) == 0)[None, :]
    return ((rolls < limit) | leading).astype(jnp.int32)


def shard_levels(key, shape, pieces, least, high):
    def one(position, parts):
        draws = jax.random.uniform(jax.random.fold_in(jax.random.fold_in(key, 6), position), (parts,), jnp.float32, least / len(pieces), high / len(pieces))
        return jnp.repeat(jnp.exp(draws), shape[position] // parts).reshape((-1,) + (1,) * (len(shape) - position - 1))

    level = one(*pieces[0])
    for cut in pieces[1:]:
        level = level * one(*cut)
    return level


def scatter_about(key, dims, deviation, reach, cuts=(), held_as=jnp.bfloat16):
    loudness = shard_levels(key, dims, cuts, -0.22, 0.18) if cuts else 1.0
    drawn = jax.random.normal(key, dims, jnp.float32) * deviation * loudness
    return jnp.minimum(jnp.maximum(drawn, -reach), reach).astype(held_as)


def setup_inputs(seed: int = 0) -> dict:
    key_of = jax.random.split(jax.random.key(seed), 20)
    tokens = scatter_about(key_of[0], (SEQS, LEN, D), 1.0, 6.0, ((0, 8), (1, 4)))
    teacher = scatter_about(key_of[1], (SEQS, LEN, D), 1.0, 6.0, ((0, 8), (1, 4)))
    segment_ids = draw_segment_ids(jax.random.fold_in(key_of[19], 71), 0)
    valid_mask = draw_valid_mask(jax.random.fold_in(key_of[19], 71), 0)
    gain_in = jnp.clip(1.0 + 0.1 * jax.random.normal(key_of[4], (D,), jnp.float32), 0.5, 1.5).astype(jnp.bfloat16)
    w_in = scatter_about(key_of[5], (D, 2 * DI + 2 * NS + MH), D ** -0.5, 0.1875, ((0, 8),))
    conv_w = scatter_about(key_of[6], (KW, CONVCH), KW ** -0.5, 3.0, ((1, 8),))
    conv_b = scatter_about(key_of[7], (CONVCH,), 0.5, 3.0, ((0, 8),))
    dt_bias = jnp.clip(jax.random.uniform(key_of[8], (MH,), jnp.float32, -2.0, 1.0), -2.0, 1.0)
    a_log = jnp.clip(jax.random.uniform(key_of[9], (MH,), jnp.float32, -10.4, -3.0), -10.4, -3.0)
    d_skip = jnp.clip(jax.random.uniform(key_of[10], (MH,), jnp.float32, 0.5, 1.5), 0.5, 1.5)
    gain_m = jnp.clip(1.0 + 0.1 * jax.random.normal(key_of[11], (DI,), jnp.float32), 0.5, 1.5).astype(jnp.bfloat16)
    w_out = scatter_about(key_of[12], (DI, D), DI ** -0.5, 0.15625, ((0, 8),))
    w_qkv = scatter_about(key_of[13], (D, (QH + 2 * KVH) * HD), D ** -0.5, 0.1875, ((0, 8),))
    w_o = scatter_about(key_of[14], (QH * HD, D), 3 ** -0.5, 3.5, ((0, 8),))
    gain_ffn = jnp.clip(1.0 + 0.1 * jax.random.normal(key_of[15], (D,), jnp.float32), 0.5, 1.5).astype(jnp.bfloat16)
    w_gate = scatter_about(key_of[16], (D, FF), D ** -0.5, 0.1875, ((0, 8),))
    w_up = scatter_about(key_of[17], (D, FF), D ** -0.5, 0.1875, ((0, 8),))
    w_down = scatter_about(key_of[18], (FF, D), FF ** -0.5, 0.125, ((0, 8),))
    return dict(tokens=tokens, teacher=teacher, segment_ids=segment_ids, valid_mask=valid_mask, gain_in=gain_in, w_in=w_in, conv_w=conv_w, conv_b=conv_b, dt_bias=dt_bias, a_log=a_log, d_skip=d_skip, gain_m=gain_m, w_out=w_out, w_qkv=w_qkv, w_o=w_o, gain_ffn=gain_ffn, w_gate=w_gate, w_up=w_up, w_down=w_down)


EPSILON = 1e-05
ROPE_BASE = 100000000000.0
MASKED = -1e+30

@jax.custom_vjp
def low(v):
    return lax.optimization_barrier(v.astype(jnp.bfloat16)).astype(jnp.float32)

@jax.custom_vjp
def low_back(v):
    return v

def low_keep(v):
    return (low(v), None)

def low_pass(kept, grad):
    return (grad,)

def back_keep(v):
    return (v, None)

def back_low(kept, grad):
    return (low(grad),)
low.defvjp(low_keep, low_pass)
low_back.defvjp(back_keep, back_low)

def high_dot(left, right):
    return jnp.dot(left, right, precision=lax.Precision.HIGHEST, preferred_element_type=jnp.float32)

def norm_rows(values, gain):
    return values * lax.rsqrt(lax.optimization_barrier(jnp.mean(values * values, axis=-1, keepdims=True)) + EPSILON) * gain

def rotary(values, positions):
    half = values.shape[-1] // 2
    freq = ROPE_BASE ** (-(jnp.arange(half, dtype=jnp.float32) * 2.0 / values.shape[-1]))
    angle = positions.astype(jnp.float32)[:, None] * freq[None, :]
    cosine = jnp.cos(angle)[:, None, :]
    sine = jnp.sin(angle)[:, None, :]
    first_half = values[..., :half]
    second_half = values[..., half:]
    return jnp.concatenate([first_half * cosine - second_half * sine, second_half * cosine + first_half * sine], axis=-1)

def conv_silu(extended, seg_ext, kernel, kernel_bias):
    width = kernel.shape[0]
    count_rows = extended.shape[0] - width + 1
    last_seg = seg_ext[width - 1:]
    total = kernel_bias[None, :] + jnp.zeros((count_rows, kernel.shape[1]), jnp.float32)
    for tap in range(width):
        same = (seg_ext[tap:tap + count_rows] == last_seg).astype(jnp.float32)
        total = total + kernel[tap][None, :] * extended[tap:tap + count_rows] * same[:, None]
    return jax.nn.silu(total)

def state_space(x_in, b_in, c_in, step_size, log_decay, segment, seg_before):
    count_rows = x_in.shape[0]
    blocks = count_rows // SPAN

    def split(values):
        return values.reshape((blocks, SPAN) + values.shape[1:])
    inputs = (split(x_in), split(b_in), split(c_in), split(step_size), split(log_decay), split(segment))
    lower = jnp.tril(jnp.ones((SPAN, SPAN), bool))

    def step(carry, block):
        state, decay, last_seg = carry
        x_blk, b_blk, c_blk, step_blk, decay_blk, seg_blk = block
        running = jnp.cumsum(decay_blk, axis=0)
        same = ((seg_blk[:, None] == seg_blk[None, :]) & lower)[:, :, None]
        gap = jnp.where(same, running[:, None, :] - running[None, :, :], 0.0)
        decay_matrix = jnp.where(same, jnp.exp(gap), 0.0)
        gram = jnp.dot(c_blk, b_blk.T, precision=lax.Precision.HIGHEST, preferred_element_type=jnp.float32)
        mixing = gram[:, :, None] * decay_matrix * step_blk[None, :, :]
        inside = jnp.einsum('tsh,shp->thp', mixing, x_blk, precision=lax.Precision.HIGHEST, preferred_element_type=jnp.float32)
        keep = (seg_blk == last_seg).astype(jnp.float32)
        carry_weight = jnp.exp(running) * keep[:, None]
        from_state = jnp.einsum('tn,hpn->thp', c_blk, state, precision=lax.Precision.HIGHEST, preferred_element_type=jnp.float32)
        end_seg = seg_blk[-1]
        tail = (seg_blk == end_seg).astype(jnp.float32)
        end_weight = jnp.exp(running[-1][None, :] - running) * tail[:, None] * step_blk
        local = jnp.einsum('sh,shp,sn->hpn', end_weight, x_blk, b_blk, precision=lax.Precision.HIGHEST, preferred_element_type=jnp.float32)
        link = jnp.exp(running[-1]) * (end_seg == last_seg).astype(jnp.float32)
        new_state = link[:, None, None] * state + local
        return ((new_state, decay * link, end_seg), inside + from_state * carry_weight[:, :, None])
    init = (jnp.zeros((MH, HP, NS), jnp.float32), jnp.ones((MH,), jnp.float32), seg_before)
    (state, decay, _), outputs = lax.scan(jax.checkpoint(step), init, inputs)
    return (outputs.reshape(x_in.shape), decay, state)

def attention(query, keys, values, segment, positions):
    group = QH // KVH
    scale = HD ** (-0.5)

    def one_block(item):
        q_blk, q_seg, q_pos = item
        q_grouped = q_blk.reshape(q_blk.shape[0], KVH, group, HD)
        scores = low_back(jnp.einsum('tkgd,skd->kgts', q_grouped, keys, precision=lax.Precision.HIGHEST, preferred_element_type=jnp.float32) * scale)
        allowed = (q_seg[:, None] == segment[None, :]) & (positions[None, :] <= q_pos[:, None])
        scores = jnp.where(allowed, scores, MASKED)
        top = lax.optimization_barrier(jnp.max(scores, axis=-1, keepdims=True))
        expo = jnp.exp(scores - top)
        probs = low(expo / lax.optimization_barrier(jnp.sum(expo, axis=-1, keepdims=True)))
        out = jnp.einsum('kgts,skd->tkgd', probs, values, precision=lax.Precision.HIGHEST, preferred_element_type=jnp.float32)
        return out.reshape(out.shape[0], QH * HD)
    blocks = LEN // TOK_DEV
    items = (query.reshape(blocks, TOK_DEV, QH, HD), segment.reshape(blocks, TOK_DEV), positions.reshape(blocks, TOK_DEV))
    return lax.map(jax.checkpoint(one_block), items).reshape(LEN, QH * HD)

def layer(resid, segment, positions, params):
    gain_in, w_in, conv_w, conv_b, dt_bias, a_log, d_skip, gain_m, w_out, w_qkv, w_o, gain_ffn, w_gate, w_up, w_down = params
    ssm_width = MH * HP
    normed = low(norm_rows(resid, gain_in))
    proj = low_back(high_dot(normed, w_in))
    gate_ssm = proj[:, :ssm_width]
    conv_in = proj[:, ssm_width:ssm_width + CONVCH]
    step_raw = proj[:, ssm_width + CONVCH:]
    extended = jnp.concatenate([jnp.zeros((KW - 1, CONVCH), jnp.float32), conv_in], axis=0)
    seg_ext = jnp.concatenate([jnp.full((KW - 1,), -1, jnp.int32), segment], axis=0)
    activated = conv_silu(extended, seg_ext, conv_w, conv_b)
    x_ssm = low(activated[:, :ssm_width]).reshape(LEN, MH, HP)
    b_ssm = low(activated[:, ssm_width:ssm_width + NS])
    c_ssm = low(activated[:, ssm_width + NS:])
    step_size = jax.nn.softplus(step_raw + dt_bias)
    log_decay = -step_size * jnp.exp(a_log)
    ssm_y, _, _ = state_space(x_ssm, b_ssm, c_ssm, step_size, log_decay, segment, jnp.array(-1, jnp.int32))
    ssm_y = ssm_y + d_skip[None, :, None] * x_ssm
    mamba_low = low(norm_rows(ssm_y.reshape(LEN, ssm_width) * jax.nn.silu(gate_ssm), gain_m))
    mamba_out = low_back(high_dot(mamba_low, w_out))
    qkv = low_back(high_dot(normed, w_qkv))
    q_width = QH * HD
    kv_width = KVH * HD
    query = low(rotary(qkv[:, :q_width].reshape(LEN, QH, HD), positions))
    keys = low(rotary(qkv[:, q_width:q_width + kv_width].reshape(LEN, KVH, HD), positions))
    values = low(qkv[:, q_width + kv_width:].reshape(LEN, KVH, HD))
    attended = low_back(low(attention(query, keys, values, segment, positions)))
    attn_out = low_back(high_dot(attended, w_o))
    mixed = resid + mamba_out + attn_out
    normed2 = low(norm_rows(mixed, gain_ffn))
    gate_val = low_back(high_dot(normed2, w_gate))
    up_val = low_back(high_dot(normed2, w_up))
    product = low(jax.nn.silu(gate_val) * up_val)
    return mixed + low_back(high_dot(product, w_down))

def reference(tokens, teacher, segment_ids, valid_mask, gain_in, w_in, conv_w, conv_b, dt_bias, a_log, d_skip, gain_m, w_out, w_qkv, w_o, gain_ffn, w_gate, w_up, w_down):
    params = tuple((p.astype(jnp.float32) for p in (gain_in, w_in, conv_w, conv_b, dt_bias, a_log, d_skip, gain_m, w_out, w_qkv, w_o, gain_ffn, w_gate, w_up, w_down)))
    resid = tokens.astype(jnp.float32)
    target = teacher.astype(jnp.float32)
    valid = valid_mask.astype(jnp.float32)
    count = jnp.sum(valid)
    positions = jnp.arange(LEN, dtype=jnp.int32)

    def whole(inputs, *weights):

        def one_seq(item):
            seq_in, seq_seg = item
            return layer(seq_in, seq_seg, positions, weights)
        outputs = lax.map(jax.checkpoint(one_seq), (inputs, segment_ids))
        diff = outputs - target
        scaled = TOKENS * jnp.sum(valid[..., None] * diff * diff) / (2.0 * count)
        return (scaled, outputs)
    scaled, pull, outputs = jax.vjp(whole, resid, *params, has_aux=True)
    grads = pull(jnp.ones((), jnp.float32))
    loss = scaled / TOKENS
    return (loss, outputs, grads[0], grads[1], grads[2], grads[3], grads[4], grads[5], grads[6], grads[7], grads[8], grads[9], grads[10], grads[11], grads[12], grads[13], grads[14], grads[15])
```

```python
import functools

import jax
import jax.numpy as jnp
from jax import lax
from jax.experimental import pallas as pl
from jax.experimental.pallas import tpu as pltpu
from jax.sharding import PartitionSpec as P

MH = 24
HP = 64
NS = 128
KW = 4
QH = 8
KVH = 2
HD = 64
SPAN = 128
QBLK = 256

EPSILON = 1e-05
ROPE_BASE = 100000000000.0
MASKED = -1e30

F32 = jnp.float32
BF16 = jnp.bfloat16
HIGH = lax.Precision.HIGHEST


def nn(left, right, precision=None):
    return lax.dot_general(
        left, right, (((1,), (0,)), ((), ())), precision=precision, preferred_element_type=F32
    )


def nt(left, right):
    return lax.dot_general(left, right, (((1,), (1,)), ((), ())), preferred_element_type=F32)


def tn(left, right):
    return lax.dot_general(left, right, (((0,), (0,)), ((), ())), preferred_element_type=F32)


def decays(seg_c, seg_r, loga_c, loga_r, before, end):
    row = lax.broadcasted_iota(jnp.int32, (SPAN, SPAN), 0)
    col = lax.broadcasted_iota(jnp.int32, (SPAN, SPAN), 1)
    lower = row >= col
    same = (seg_c == seg_r) & lower
    run_c = nn(lower.astype(F32), loga_c, HIGH)
    run_r = nn(loga_r, (row <= col).astype(F32), HIGH)
    keep = (seg_c == before).astype(F32)
    tail = (seg_c == end).astype(F32)
    return lower, same, run_c, run_r, keep, tail


def ssm_fwd_kernel(
    heads, ends, skip, act, dt_c, loga_c, dt_r, loga_r, seg_c, seg_r, y_ref, st_ref, state
):
    step = pl.program_id(0)

    @pl.when(step == 0)
    def _():
        state[...] = jnp.zeros_like(state)

    before, end = ends[step], ends[step + 1]
    link = (before == end).astype(F32)
    _, same, run_c, run_r, keep, tail = decays(
        seg_c[...], seg_r[...], loga_c[...], loga_r[...], before, end
    )
    width = heads * HP
    b_in = act[:, width : width + NS]
    c_in = act[:, width + NS : width + 2 * NS]
    gram = nt(c_in, b_in)
    for h in range(heads):
        lanes = slice(h * HP, (h + 1) * HP)
        x_in = act[:, lanes]
        own_c = run_c[:, h : h + 1]
        last = own_c[SPAN - 1 :, :]
        decay = jnp.where(same, jnp.exp(own_c - run_r[h : h + 1, :]), 0.0)
        mixing = (gram * decay * dt_r[h : h + 1, :]).astype(BF16)
        prior = state[h]
        st_ref[0, h] = prior
        x_wide = x_in.astype(F32)
        y_out = nn(mixing, x_in) + nt(c_in, prior.astype(BF16)) * (jnp.exp(own_c) * keep)
        y_ref[:, lanes] = y_out + skip[h] * x_wide
        weight = jnp.exp(last - own_c) * tail * dt_c[:, h : h + 1]
        state[h] = (jnp.exp(last) * link) * prior + tn((x_wide * weight).astype(BF16), b_in)


def ssm_bwd_kernel(
    heads,
    ends,
    skip,
    act,
    dt_c,
    loga_c,
    dt_r,
    loga_r,
    seg_c,
    seg_r,
    st_ref,
    gy_ref,
    gact_ref,
    gcol_ref,
    grow_ref,
    gstate,
):
    step = pl.num_programs(0) - 1 - pl.program_id(0)

    @pl.when(pl.program_id(0) == 0)
    def _():
        gstate[...] = jnp.zeros_like(gstate)

    before, end = ends[step], ends[step + 1]
    link = (before == end).astype(F32)
    lower, same, run_c, run_r, keep, tail = decays(
        seg_c[...], seg_r[...], loga_c[...], loga_r[...], before, end
    )
    width = heads * HP
    b_in = act[:, width : width + NS]
    c_in = act[:, width + NS : width + 2 * NS]
    gram = nt(c_in, b_in)
    g_gram = jnp.zeros((SPAN, SPAN), F32)
    g_b = jnp.zeros((SPAN, NS), F32)
    g_c = jnp.zeros((SPAN, NS), F32)
    for h in range(heads):
        lanes = slice(h * HP, (h + 1) * HP)
        x_in = act[:, lanes]
        x_wide = x_in.astype(F32)
        gy = gy_ref[:, lanes]
        gy_low = gy.astype(BF16)
        own_c = run_c[:, h : h + 1]
        last = own_c[SPAN - 1 :, :]
        dt_row = dt_r[h : h + 1, :]
        decay = jnp.where(same, jnp.exp(own_c - run_r[h : h + 1, :]), 0.0)
        prior = st_ref[0, h]
        prior_low = prior.astype(BF16)
        after = gstate[h]
        after_low = after.astype(BF16)
        carry_w = jnp.exp(own_c) * keep
        tail_w = jnp.exp(last - own_c) * tail
        end_w = tail_w * dt_c[:, h : h + 1]
        mixing = (gram * decay * dt_row).astype(BF16)
        g_mix = nt(gy_low, x_in) * decay
        g_gram_h = g_mix * dt_row
        g_gram = g_gram + g_gram_h
        inner = g_gram_h * gram
        g_dt_row = jnp.sum(g_mix * gram, axis=0, keepdims=True)
        from_state = nt(b_in, after_low)
        g_x = tn(mixing, gy_low) + from_state * end_w
        gact_ref[:, lanes] = g_x + skip[h] * gy
        g_carry = jnp.sum(gy * nt(c_in, prior_low), axis=1, keepdims=True)
        g_tail = jnp.sum(x_wide * from_state, axis=1, keepdims=True)
        g_link = jnp.exp(last) * link
        total_last = jnp.sum(g_tail * end_w, axis=0, keepdims=True) + g_link * jnp.sum(
            jnp.sum(after * prior, axis=1, keepdims=True), axis=0, keepdims=True
        )
        g_run_c = jnp.sum(inner, axis=1, keepdims=True) + g_carry * carry_w - g_tail * end_w
        at_last = lax.broadcasted_iota(jnp.int32, (SPAN, 1), 0) == SPAN - 1
        gcol_ref[:, h : h + 1] = g_run_c + jnp.where(at_last, total_last, 0.0)
        gcol_ref[:, heads + h : heads + h + 1] = g_tail * tail_w
        grow_ref[h : h + 1, :] = jnp.sum(inner, axis=0, keepdims=True)
        grow_ref[heads + h : heads + h + 1, :] = g_dt_row
        weighted = (gy * carry_w).astype(BF16)
        g_c = g_c + nn(weighted, prior_low)
        g_b = g_b + nn((x_wide * end_w).astype(BF16), after_low)
        gstate[h] = g_link * after + tn(weighted, c_in)
    g_gram_low = g_gram.astype(BF16)
    gact_ref[:, width : width + NS] = g_b + tn(g_gram_low, c_in)
    gact_ref[:, width + NS :] = g_c + nn(g_gram_low, b_in)


def ssm_specs(heads, width, at):
    return [
        pl.BlockSpec(memory_space=pltpu.SMEM),
        pl.BlockSpec(memory_space=pltpu.SMEM),
        pl.BlockSpec((SPAN, width + 2 * NS), lambda i: (at(i), 0)),
        pl.BlockSpec((SPAN, heads), lambda i: (at(i), 0)),
        pl.BlockSpec((SPAN, heads), lambda i: (at(i), 0)),
        pl.BlockSpec((heads, SPAN), lambda i: (0, at(i))),
        pl.BlockSpec((heads, SPAN), lambda i: (0, at(i))),
        pl.BlockSpec((SPAN, 1), lambda i: (at(i), 0)),
        pl.BlockSpec((1, SPAN), lambda i: (0, at(i))),
    ]


def ssm_forward(heads, inputs):
    length = inputs[2].shape[0]
    steps = length // SPAN
    width = heads * HP
    return pl.pallas_call(
        functools.partial(ssm_fwd_kernel, heads),
        grid=(steps,),
        in_specs=ssm_specs(heads, width, lambda i: i),
        out_specs=[
            pl.BlockSpec((SPAN, width), lambda i: (i, 0)),
            pl.BlockSpec((1, heads, HP, NS), lambda i: (i, 0, 0, 0)),
        ],
        out_shape=[
            jax.ShapeDtypeStruct((length, width), F32),
            jax.ShapeDtypeStruct((steps, heads, HP, NS), F32),
        ],
        scratch_shapes=[pltpu.VMEM((heads, HP, NS), F32)],
        compiler_params=pltpu.CompilerParams(vmem_limit_bytes=32 * 1024 * 1024),
        cost_estimate=pl.CostEstimate(flops=10**9, bytes_accessed=10**7, transcendentals=10**6),
        name="ssm_forward",
    )(*inputs)


def ssm_backward(heads, inputs, states, gy):
    length = inputs[2].shape[0]
    steps = length // SPAN
    width = heads * HP

    def at(i):
        return steps - 1 - i

    return pl.pallas_call(
        functools.partial(ssm_bwd_kernel, heads),
        grid=(steps,),
        in_specs=ssm_specs(heads, width, at)
        + [
            pl.BlockSpec((1, heads, HP, NS), lambda i: (at(i), 0, 0, 0)),
            pl.BlockSpec((SPAN, width), lambda i: (at(i), 0)),
        ],
        out_specs=[
            pl.BlockSpec((SPAN, width + 2 * NS), lambda i: (at(i), 0)),
            pl.BlockSpec((SPAN, 2 * heads), lambda i: (at(i), 0)),
            pl.BlockSpec((2 * heads, SPAN), lambda i: (0, at(i))),
        ],
        out_shape=[
            jax.ShapeDtypeStruct((length, width + 2 * NS), F32),
            jax.ShapeDtypeStruct((length, 2 * heads), F32),
            jax.ShapeDtypeStruct((2 * heads, length), F32),
        ],
        scratch_shapes=[pltpu.VMEM((heads, HP, NS), F32)],
        compiler_params=pltpu.CompilerParams(vmem_limit_bytes=32 * 1024 * 1024),
        cost_estimate=pl.CostEstimate(flops=3 * 10**9, bytes_accessed=10**7, transcendentals=10**6),
        name="ssm_backward",
    )(*inputs, states, gy)


def allowed_keys(index, reach, seg_c, seg_r):
    row = lax.broadcasted_iota(jnp.int32, (QBLK, reach), 0) + index * QBLK
    col = lax.broadcasted_iota(jnp.int32, (QBLK, reach), 1)
    return (seg_c[...] == seg_r[:, :reach]) & (col <= row)


def attn_fwd_kernel(heads, blocks, q_ref, k_ref, v_ref, seg_c, seg_r, out_ref, lse_ref):
    for index in range(blocks):

        @pl.when(pl.program_id(0) == index)
        def _(index=index):
            reach = (index + 1) * QBLK
            allowed = allowed_keys(index, reach, seg_c, seg_r)
            keys = k_ref[:reach, :]
            values = v_ref[:reach, :]
            for h in range(heads):
                lanes = slice(h * HD, (h + 1) * HD)
                scores = nt(q_ref[:, lanes], keys) * (HD**-0.5)
                scores = jnp.where(allowed, scores, MASKED)
                top = jnp.max(scores, axis=1, keepdims=True)
                expo = jnp.exp(scores - top)
                total = jnp.sum(expo, axis=1, keepdims=True)
                probs = (expo * (1.0 / total)).astype(BF16)
                out_ref[:, lanes] = nn(probs, values).astype(BF16)
                lse_ref[:, h : h + 1] = top + jnp.log(total)


def attn_bwd_kernel(
    heads, blocks, q_ref, k_ref, v_ref, seg_c, seg_r, lse_ref, go_ref, gq_ref, gk_ref, gv_ref
):
    @pl.when(pl.program_id(0) == 0)
    def _():
        gk_ref[...] = jnp.zeros_like(gk_ref)
        gv_ref[...] = jnp.zeros_like(gv_ref)

    for index in range(blocks):

        @pl.when(pl.program_id(0) == index)
        def _(index=index):
            reach = (index + 1) * QBLK
            allowed = allowed_keys(index, reach, seg_c, seg_r)
            keys = k_ref[:reach, :]
            values = v_ref[:reach, :]
            for h in range(heads):
                lanes = slice(h * HD, (h + 1) * HD)
                query = q_ref[:, lanes]
                g_out = go_ref[:, lanes]
                scores = nt(query, keys) * (HD**-0.5)
                probs = jnp.where(allowed, jnp.exp(scores - lse_ref[:, h : h + 1]), 0.0)
                g_probs = nt(g_out, values)
                delta = jnp.sum(probs * g_probs, axis=1, keepdims=True)
                g_scores = (probs * (g_probs - delta)).astype(BF16)
                gq_ref[:, lanes] = nn(g_scores, keys) * (HD**-0.5)
                gk_ref[:reach, :] += tn(g_scores, query) * (HD**-0.5)
                gv_ref[:reach, :] += tn(probs.astype(BF16), g_out)


def attn_specs(heads, length):
    return [
        pl.BlockSpec((QBLK, heads * HD), lambda i: (i, 0)),
        pl.BlockSpec((length, HD), lambda i: (0, 0)),
        pl.BlockSpec((length, HD), lambda i: (0, 0)),
        pl.BlockSpec((QBLK, 1), lambda i: (i, 0)),
        pl.BlockSpec((1, length), lambda i: (0, 0)),
    ]


def attn_forward(heads, inputs):
    length = inputs[0].shape[0]
    blocks = length // QBLK
    return pl.pallas_call(
        functools.partial(attn_fwd_kernel, heads, blocks),
        grid=(blocks,),
        in_specs=attn_specs(heads, length),
        out_specs=[
            pl.BlockSpec((QBLK, heads * HD), lambda i: (i, 0)),
            pl.BlockSpec((QBLK, heads), lambda i: (i, 0)),
        ],
        out_shape=[
            jax.ShapeDtypeStruct((length, heads * HD), BF16),
            jax.ShapeDtypeStruct((length, heads), F32),
        ],
        compiler_params=pltpu.CompilerParams(vmem_limit_bytes=32 * 1024 * 1024),
        cost_estimate=pl.CostEstimate(flops=10**9, bytes_accessed=10**7, transcendentals=10**6),
        name="attn_forward",
    )(*inputs)


def attn_backward(heads, inputs, lse, g_out):
    length = inputs[0].shape[0]
    blocks = length // QBLK
    return pl.pallas_call(
        functools.partial(attn_bwd_kernel, heads, blocks),
        grid=(blocks,),
        in_specs=attn_specs(heads, length)
        + [
            pl.BlockSpec((QBLK, heads), lambda i: (i, 0)),
            pl.BlockSpec((QBLK, heads * HD), lambda i: (i, 0)),
        ],
        out_specs=[
            pl.BlockSpec((QBLK, heads * HD), lambda i: (i, 0)),
            pl.BlockSpec((length, HD), lambda i: (0, 0)),
            pl.BlockSpec((length, HD), lambda i: (0, 0)),
        ],
        out_shape=[
            jax.ShapeDtypeStruct((length, heads * HD), F32),
            jax.ShapeDtypeStruct((length, HD), F32),
            jax.ShapeDtypeStruct((length, HD), F32),
        ],
        compiler_params=pltpu.CompilerParams(vmem_limit_bytes=32 * 1024 * 1024),
        cost_estimate=pl.CostEstimate(flops=3 * 10**9, bytes_accessed=10**7, transcendentals=10**6),
        name="attn_backward",
    )(*inputs, lse, g_out)


class Net:
    def __init__(self):
        self.n = lax.axis_size("ctx")
        self.m = lax.axis_size("fsdp")
        self.c = lax.axis_index("ctx")
        self.f = lax.axis_index("fsdp")
        self.direct = self.n == 4 and self.m == 8
        self.x, self.core = self.c // 2, self.c % 2
        self.z, self.y = self.f // 2, self.f % 2

    def flip(self, value, axis, bit):
        size = lax.axis_size(axis)
        return lax.ppermute(value, axis, [(i, i ^ bit) for i in range(size)])

    def shift_z(self, value, by):
        return lax.ppermute(value, "fsdp", [(i, (i + 2 * by) % self.m) for i in range(self.m)])

    def spread(self, block, share_x=False):
        if not self.direct:
            if share_x:
                block = lax.all_gather(block, "ctx", axis=0, tiled=False)
                half = self.n // 2
                block = block.reshape((half, 2) + block.shape[1:])
                block = lax.dynamic_index_in_dim(block, self.core, 1, False)
                block = block.reshape((half * block.shape[1],) + block.shape[2:])
            return lax.all_gather(block, "fsdp", axis=0, tiled=False)
        parts, places = [], []
        for k in range(4):
            got = self.shift_z(block, k) if k else block
            z_from = (self.z - k) % 4
            for other in range(2):
                piece = self.flip(got, "fsdp", 1) if other else got
                place = 2 * z_from + (self.y ^ other)
                if share_x:
                    parts.append(piece)
                    places.append(2 * place + self.x)
                    parts.append(self.flip(piece, "ctx", 2))
                    places.append(2 * place + 1 - self.x)
                else:
                    parts.append(piece)
                    places.append(place)
        out = put(parts, places)
        if share_x:
            out = out.reshape((8, 2 * block.shape[0]) + block.shape[1:])
        return out

    def collect(self, sums, share_x=False, kind=BF16):
        if not self.direct:
            out = lax.psum_scatter(sums.astype(kind), "fsdp", scatter_dimension=0, tiled=False)
            if share_x:
                half = self.n // 2
                groups = [[i * 2 + k for i in range(half)] for k in range(2)]
                out = lax.psum_scatter(
                    out, "ctx", scatter_dimension=0, axis_index_groups=groups, tiled=True
                )
            return out
        low = sums.astype(kind)
        if share_x:
            low = low.reshape((8, 2, low.shape[1] // 2) + low.shape[2:])
            away = lax.dynamic_index_in_dim(low, 1 - self.x, 1, False)
            here = lax.dynamic_index_in_dim(low, self.x, 1, False)
            low = (here.astype(F32) + self.flip(away, "ctx", 2).astype(F32)).astype(kind)
        low = low.reshape((4, 2) + low.shape[1:])
        away = lax.dynamic_index_in_dim(low, 1 - self.y, 1, False)
        here = lax.dynamic_index_in_dim(low, self.y, 1, False)
        both = (here.astype(F32) + self.flip(away, "fsdp", 1).astype(F32)).astype(kind)
        total = lax.dynamic_index_in_dim(both, self.z, 0, False).astype(F32)
        for k in range(1, 4):
            block = lax.dynamic_index_in_dim(both, (self.z + k) % 4, 0, False)
            total = total + self.shift_z(block, k).astype(F32)
        return total.astype(kind)

    def total(self, value):
        if not self.direct:
            return lax.psum(value, ("ctx", "fsdp"))
        value = self.ctx_sum(value)
        value = value + self.flip(value, "fsdp", 1)
        return value + sum(self.shift_z(value, k) for k in range(1, 4))

    def ctx_all(self, value):
        if not self.direct:
            return lax.all_gather(value, "ctx", axis=0, tiled=False)
        mate = self.flip(value, "ctx", 1)
        across = self.flip(value, "ctx", 2)
        far = self.flip(across, "ctx", 1)
        return put([value, mate, across, far], [self.c, self.c ^ 1, self.c ^ 2, self.c ^ 3])

    def ctx_sum(self, value):
        if not self.direct:
            return lax.psum(value, "ctx")
        value = value + self.flip(value, "ctx", 1)
        return value + self.flip(value, "ctx", 2)

    def ctx_collect(self, parts):
        if not self.direct:
            low = lax.psum_scatter(parts.astype(BF16), "ctx", scatter_dimension=0, tiled=False)
            return low.astype(F32)
        pairs = parts.reshape((2, 2) + parts.shape[1:])
        pairs = lax.dynamic_index_in_dim(pairs, 1 - self.core, 1, False), (
            lax.dynamic_index_in_dim(pairs, self.core, 1, False)
        )

        def half(which):
            away = lax.dynamic_index_in_dim(pairs[0], which, 0, False).astype(BF16)
            here = lax.dynamic_index_in_dim(pairs[1], which, 0, False)
            return here.astype(F32) + self.flip(away, "ctx", 1).astype(F32)

        across = self.flip(half(1 - self.x).astype(BF16), "ctx", 2)
        return half(self.x) + across.astype(F32)

    def ctx_swap(self, parts):
        if not self.direct:
            return lax.all_to_all(parts, "ctx", 0, 0, tiled=True)
        got = [lax.dynamic_index_in_dim(parts, self.c, 0, False)]
        for bit in range(1, 4):
            block = lax.dynamic_index_in_dim(parts, self.c ^ bit, 0, False)
            got.append(self.flip(block, "ctx", bit))
        return put(got, [self.c ^ bit for bit in range(4)])


def put_kernel(count, places, *refs):
    parts, out = refs[:count], refs[count]
    for i in range(count):

        @pl.when(pl.program_id(0) == i)
        def _(i=i):
            out[0] = parts[i][...]


def put(parts, places):
    count = len(parts)
    shape = parts[0].shape
    zeros = (0,) * len(shape)
    places = jnp.stack([jnp.asarray(p, jnp.int32) for p in places])
    size = parts[0].size * parts[0].dtype.itemsize
    return pl.pallas_call(
        functools.partial(put_kernel, count),
        grid_spec=pltpu.PrefetchScalarGridSpec(
            num_scalar_prefetch=1,
            grid=(count,),
            in_specs=[pl.BlockSpec(shape, lambda i, at: zeros)] * count,
            out_specs=pl.BlockSpec((1,) + shape, lambda i, at: (at[i],) + zeros),
        ),
        out_shape=jax.ShapeDtypeStruct((count,) + shape, parts[0].dtype),
        compiler_params=pltpu.CompilerParams(vmem_limit_bytes=40 * 1024 * 1024),
        cost_estimate=pl.CostEstimate(
            flops=0, bytes_accessed=2 * count * size, transcendentals=0
        ),
        name="put",
    )(places, *parts)


def rms_scale(values):
    return lax.rsqrt(jnp.mean(values * values, axis=-1, keepdims=True) + EPSILON)


def rms_back(values, gain, scale, grad):
    scaled = grad * gain
    inner = jnp.mean(values * scaled, axis=-1, keepdims=True)
    return scale * scaled - values * (scale * scale * scale * inner), jnp.sum(
        grad * values * scale, axis=0
    )


def turn(values, cosine, sine):
    half = values.shape[-1] // 2
    first, second = values[..., :half], values[..., half:]
    return jnp.concatenate(
        [first * cosine - second * sine, second * cosine + first * sine], axis=-1
    )


def columns_of(w, start, size):
    return lax.dynamic_slice_in_dim(w, start, size, 1)


def per_device(
    tokens,
    teacher,
    segment_ids,
    valid_mask,
    gain_in,
    w_in,
    conv_w,
    conv_b,
    dt_bias,
    a_log,
    d_skip,
    gain_m,
    w_out,
    w_qkv,
    w_o,
    gain_ffn,
    w_gate,
    w_up,
    w_down,
):
    net = Net()
    n, m, c, f = net.n, net.m, net.c, net.f
    rows, dim = tokens.shape[1:]
    length = segment_ids.shape[1]
    shard = w_in.shape[0]
    wide = MH * HP
    conv_full = wide + 2 * NS
    heads = MH // n
    q_heads = QH // n
    width = heads * HP
    conv_width = width + 2 * NS
    q_width = q_heads * HD
    group = QH // KVH
    kv_at = (c * q_heads) // group
    ff = w_gate.shape[1]
    ff_shard = w_down.shape[0]
    ff_part = ff_shard // 2
    seg = segment_ids[0]
    seg_c, seg_r = seg[:, None], seg[None, :]
    ends = jnp.concatenate([jnp.full((1,), -1, jnp.int32), seg[SPAN - 1 :: SPAN]])

    def lay(values):
        values = values.reshape((-1, values.shape[-1]))
        room = -values.shape[1] % 128
        return jnp.pad(values, ((0, 0), (0, room))).reshape(-1, 128)

    def lay_all(pieces, dtype):
        laid = [lay(p) for p in pieces]
        used = sum(p.shape[0] for p in laid)
        return jnp.concatenate(laid + [jnp.zeros((-used % 16, 128), dtype)], axis=0)

    def unlay(small, start, lead, size):
        room = size + -size % 128
        count = lead * room // 128
        return small[..., start : start + count, :].reshape(small.shape[:-2] + (lead, room))[
            ..., :size
        ]

    shapes = [(1, shard), (1, shard), (1, w_out.shape[0]), (1, conv_b.shape[0])]
    shapes += [(KW, conv_b.shape[0]), (MH, shard)]
    starts = [0]
    for lead, size in shapes:
        starts.append(starts[-1] + lead * (size + -size % 128) // 128)
    small = net.spread(
        lay_all(
            [
                gain_in[None],
                gain_ffn[None],
                gain_m[None],
                conv_b[None],
                conv_w,
                w_in[:, wide + conv_full :].T,
            ],
            BF16,
        )
    )
    cuts = [
        jnp.transpose(unlay(small, start, *shape), (1, 0, 2)).reshape(shape[0], -1)
        for start, shape in zip(starts, shapes)
    ]
    gain_input = cuts[0][0].astype(F32)
    gain_second = cuts[1][0].astype(F32)
    gain_mamba = lax.dynamic_slice_in_dim(cuts[2][0], c * width, width).astype(F32)

    def conv_cut(values):
        own = lax.dynamic_slice_in_dim(values, c * width, width, values.ndim - 1)
        return jnp.concatenate([own, values[..., wide:]], axis=-1)

    bias = conv_cut(cuts[3][0].astype(F32))
    taps = conv_cut(cuts[4].astype(F32))
    w_step = lax.dynamic_slice_in_dim(cuts[5], c * heads, heads, 0)
    step_bias = lax.dynamic_slice_in_dim(dt_bias, c * heads, heads)
    decay_log = lax.dynamic_slice_in_dim(a_log, c * heads, heads)
    skip = lax.dynamic_slice_in_dim(d_skip, c * heads, heads)

    all_tokens = net.ctx_all(tokens[0]).reshape(length, dim)
    first = jnp.concatenate(
        [
            columns_of(w_in, c * width, width),
            columns_of(w_in, wide + c * width, width),
            w_in[:, 2 * wide : 2 * wide + 2 * NS],
            columns_of(w_qkv, c * q_width, q_width),
            columns_of(w_qkv, QH * HD + kv_at * HD, HD),
            columns_of(w_qkv, (QH + KVH) * HD + kv_at * HD, HD),
        ],
        axis=1,
    )
    w_first = net.spread(first).reshape(dim, first.shape[1])
    quarter = dim // n
    both_out = jnp.concatenate([w_out, w_o], axis=0)
    out_rows = both_out.shape[0]
    own_out = columns_of(both_out, c * quarter, quarter)
    per = m // n
    spread_out = net.spread(own_out)
    swapped = net.ctx_swap(spread_out.reshape((n, per) + own_out.shape))
    w_outs = jnp.transpose(swapped, (1, 2, 0, 3)).reshape(per, out_rows, dim)
    mamba_rows = w_out.shape[0]
    w_mamba = w_outs[:, :mamba_rows].reshape(per * mamba_rows, dim)
    w_attn = w_outs[:, mamba_rows:].reshape(per * (out_rows - mamba_rows), dim)

    def ff_cut(w):
        w = w.reshape(shard, m, 2, ff_part)
        return lax.dynamic_index_in_dim(w, net.core, 2, False).reshape(shard, m * ff_part)

    halves = n // 2
    gate_up = jnp.concatenate([ff_cut(w_gate), ff_cut(w_up)], axis=1)
    gu_rows = shard // halves
    gate_up = lax.dynamic_slice_in_dim(gate_up, net.x * gu_rows, gu_rows, 0)
    w_gu = net.spread(gate_up, share_x=True).reshape(dim, ff)
    down = lax.dynamic_slice_in_dim(w_down, net.core * ff_part, ff_part, 0)
    d_rows = ff_part // halves
    down = lax.dynamic_slice_in_dim(down, net.x * d_rows, d_rows, 0)
    w_dn = net.spread(down, share_x=True).reshape(m * ff_part, dim)

    valid = valid_mask[0].astype(F32)
    count = net.total(jnp.full((8, 128), jnp.sum(valid), F32))[0, 0]
    resid_all = all_tokens.astype(F32)
    normed = (resid_all * rms_scale(resid_all) * gain_input).astype(BF16)
    proj = nn(normed, w_first)
    gate_z = proj[:, :width]
    conv_in = proj[:, width : width + conv_width]
    qkv = proj[:, width + conv_width :]
    step_raw = nt(normed, w_step) + step_bias
    dt = jax.nn.softplus(step_raw)
    rate = jnp.exp(decay_log)
    loga = -dt * rate

    def same_back(by):
        ahead = jnp.concatenate([jnp.full((by,), -1, jnp.int32), seg[: length - by]])
        return (ahead == seg).astype(F32)[:, None]

    def behind(values, by):
        if by == 0:
            return values
        return jnp.concatenate(
            [jnp.zeros((by,) + values.shape[1:], values.dtype), values[: length - by]]
        )

    def before(values, by):
        if by == 0:
            return values
        return jnp.concatenate([values[by:], jnp.zeros((by,) + values.shape[1:], values.dtype)])

    pre = bias[None, :]
    for tap in range(KW):
        by = KW - 1 - tap
        term = taps[tap][None, :] * behind(conv_in, by)
        pre = pre + (term * same_back(by) if by else term)
    act = jax.nn.silu(pre).astype(BF16)
    ssm_in = (ends, skip, act, dt, loga, dt.T, loga.T, seg_c, seg_r)
    ssm_y, states = ssm_forward(heads, ssm_in)
    gated = ssm_y * jax.nn.silu(gate_z)
    square = net.ctx_sum(jnp.sum(gated * gated, axis=1))

    half = HD // 2
    freq = ROPE_BASE ** (-(jnp.arange(half, dtype=F32) * 2.0 / HD))
    angle = jnp.arange(length, dtype=jnp.int32).astype(F32)[:, None] * freq[None, :]
    cosine, sine = jnp.cos(angle), jnp.sin(angle)
    q_rot = turn(qkv[:, :q_width].reshape(length, q_heads, HD), cosine[:, None], sine[:, None])
    query = q_rot.astype(BF16).reshape(length, q_width)
    keys = turn(qkv[:, q_width : q_width + HD], cosine, sine).astype(BF16)
    values = qkv[:, q_width + HD : q_width + 2 * HD].astype(BF16)
    attn_in = (query, keys, values, seg_c, seg_r)
    attended, lse = attn_forward(q_heads, attn_in)
    scale_m = lax.rsqrt(square / wide + EPSILON)[:, None]
    ym = (gated * scale_m * gain_mamba).astype(BF16)
    outs = nn(ym, w_mamba) + nn(attended, w_attn)
    mixed = tokens[0].astype(F32) + net.ctx_collect(outs.reshape(n, rows, dim))

    scale2 = rms_scale(mixed)
    normed2 = (mixed * scale2 * gain_second).astype(BF16)
    mate = [(i, i ^ 1) for i in range(n)]
    both = jnp.concatenate([normed2, lax.ppermute(normed2, "ctx", mate)], axis=0)
    gu = nn(both, w_gu)
    gate_v, up_v = gu[:, : ff // 2], gu[:, ff // 2 :]
    sig = jax.nn.sigmoid(gate_v)
    product = (gate_v * sig * up_v).astype(BF16)
    down_out = nn(product, w_dn)
    from_mate = lax.ppermute(down_out[rows:].astype(BF16), "ctx", mate)
    layer_out = mixed + down_out[:rows] + from_mate.astype(F32)
    diff = layer_out - teacher[0].astype(F32)
    squared = jnp.sum(valid[:, None] * diff * diff)
    token_total = length * m * tokens.shape[0]
    grad_out = token_total * valid[:, None] * diff / count

    gb = grad_out.astype(BF16)
    gb_both = jnp.concatenate([gb, lax.ppermute(gb, "ctx", mate)], axis=0)
    g_prod = nt(gb_both, w_dn)
    g_gate = (g_prod * up_v * (sig * (1.0 + gate_v * (1.0 - sig)))).astype(BF16)
    g_up = (g_prod * gate_v * sig).astype(BF16)
    g_gu = jnp.concatenate([g_gate, g_up], axis=1)
    g_n2 = nt(g_gu, w_gu)
    from_mate = lax.ppermute(g_n2[rows:].astype(BF16), "ctx", mate)
    grad_n2 = g_n2[:rows] + from_mate.astype(F32)
    grad_down = net.collect(tn(product, gb_both).reshape(m, ff_part, dim), share_x=True)
    grad_gu = net.collect(tn(both, g_gu).reshape(m, shard, ff), share_x=True)
    part, grad_gain_second = rms_back(mixed, gain_second, scale2, grad_n2)
    grad_mixed = grad_out + part
    gm = net.ctx_all(grad_mixed.astype(BF16)).reshape(length, dim)

    g_ym = nt(gm, w_mamba)
    g_ob = nt(gm, w_attn).astype(BF16)
    sig_z = jax.nn.sigmoid(gate_z)
    scaled = g_ym * gain_mamba
    inner = net.ctx_sum(jnp.sum(gated * scaled, axis=1))[:, None] / wide
    grad_gain_mamba = jnp.sum(g_ym * gated * scale_m, axis=0)
    g_query, g_keys, g_values = attn_backward(q_heads, attn_in, lse, g_ob)
    g_qkv = jnp.concatenate(
        [
            turn(g_query.reshape(length, q_heads, HD), cosine[:, None], -sine[:, None]).reshape(
                length, q_width
            ),
            turn(g_keys, cosine, -sine),
            g_values,
        ],
        axis=1,
    ).astype(BF16)
    g_gated = scale_m * scaled - gated * (scale_m * scale_m * scale_m * inner)
    g_ssm = g_gated * gate_z * sig_z
    g_z = (g_gated * ssm_y * (sig_z * (1.0 + gate_z * (1.0 - sig_z)))).astype(BF16)
    x_wide = act[:, :width].astype(F32)
    grad_skip = jnp.sum((g_ssm * x_wide).reshape(length, heads, HP), axis=(0, 2))
    g_act, g_col, g_row = ssm_backward(heads, ssm_in, states, g_ssm)
    g_run = g_col[:, :heads] - g_row[:heads].T
    g_run = g_run.reshape(length // SPAN, SPAN, heads)
    g_loga = lax.cumsum(g_run, axis=1, reverse=True).reshape(length, heads)
    g_dt = g_col[:, heads:] + g_row[heads:].T - g_loga * rate
    grad_decay_log = jnp.sum(g_loga * loga, axis=0)
    g_step = g_dt * jax.nn.sigmoid(step_raw)
    grad_step_bias = jnp.sum(g_step, axis=0)
    sig_pre = jax.nn.sigmoid(pre)
    g_pre = g_act * (sig_pre * (1.0 + pre * (1.0 - sig_pre)))
    grad_bias = jnp.sum(g_pre, axis=0)
    grad_taps = []
    g_conv = jnp.zeros_like(g_pre)
    for tap in range(KW):
        by = KW - 1 - tap
        masked = g_pre * same_back(by) if by else g_pre
        grad_taps.append(jnp.sum(masked * behind(conv_in, by), axis=0))
        g_conv = g_conv + taps[tap][None, :] * before(masked, by)
    grad_taps = jnp.stack(grad_taps)
    g_first = jnp.concatenate([g_z, g_conv.astype(BF16), g_qkv], axis=1)
    g_step_low = g_step.astype(BF16)
    grad_first = net.collect(tn(normed, g_first).reshape(m, shard, first.shape[1]))
    g_normed = nt(g_first, w_first) + nn(g_step_low, w_step)
    grad_normed = net.ctx_collect(g_normed.reshape(n, rows, dim))
    resid = tokens[0].astype(F32)
    part, grad_gain_input = rms_back(resid, gain_input, rms_scale(resid), grad_normed)
    grad_tokens = grad_mixed + part
    grad_w_step = tn(g_step_low, normed)

    g_outs = jnp.concatenate(
        [
            tn(ym, gm).reshape(per, mamba_rows, dim),
            tn(attended, gm).reshape(per, out_rows - mamba_rows, dim),
        ],
        axis=1,
    ).astype(BF16)
    g_outs = jnp.transpose(g_outs.reshape(per, out_rows, n, quarter), (2, 0, 1, 3))
    grad_outs = net.collect(net.ctx_swap(g_outs).reshape(m, out_rows, quarter))

    def to_wide(values, at, size):
        out = jnp.zeros(values.shape[:-1] + (size,), F32)
        return lax.dynamic_update_slice_in_dim(out, values, at, values.ndim - 1)

    def conv_wide(values):
        return jnp.concatenate(
            [to_wide(values[..., :width], c * width, wide), values[..., width:]], axis=-1
        )

    def for_shards(values):
        values = values.reshape((-1, m, values.shape[-1] // m))
        return jnp.transpose(values, (1, 0, 2))

    small_grads = [
        grad_gain_input,
        grad_gain_second,
        to_wide(grad_gain_mamba, c * width, wide),
        conv_wide(grad_bias),
        conv_wide(grad_taps),
        lax.dynamic_update_slice_in_dim(
            jnp.zeros((MH, dim), F32), grad_w_step, c * heads, 0
        ),
    ]
    heads_grads = jnp.stack(
        [
            to_wide(grad_step_bias, c * heads, MH),
            to_wide(grad_decay_log, c * heads, MH),
            to_wide(grad_skip, c * heads, MH),
            jnp.full((MH,), squared),
        ]
    )
    laid = [jax.vmap(lay)(for_shards(g)) for g in small_grads]
    laid.append(jnp.broadcast_to(lay(heads_grads)[None], (m, 4, 128)))
    used = sum(p.shape[1] for p in laid)
    laid.append(jnp.zeros((m, -used % 16, 128), F32))
    totals = net.ctx_sum(net.collect(jnp.concatenate(laid, axis=1), kind=F32))
    own_small = [unlay(totals, start, *shape) for start, shape in zip(starts, shapes)]
    head_totals = totals[starts[-1] : starts[-1] + 4, :MH]
    loss = head_totals[3, 0] / (2.0 * count)

    got = net.ctx_all(grad_first).astype(F32)
    cuts = [0, width, 2 * width, 2 * width + 2 * NS]
    cuts += [cuts[-1] + q_width, cuts[-1] + q_width + HD, cuts[-1] + q_width + 2 * HD]

    def side(i):
        return [got[j][:, cuts[i] : cuts[i + 1]] for j in range(n)]

    shared = n // KVH
    out_w_in = jnp.concatenate(
        side(0) + side(1) + [sum(side(2)), own_small[5].T],
        axis=1,
    )
    out_w_qkv = jnp.concatenate(
        side(3)
        + [sum(side(i)[k * shared : (k + 1) * shared]) for i in (4, 5) for k in range(KVH)],
        axis=1,
    )
    got = net.ctx_all(grad_outs).astype(F32)
    out_outs = jnp.transpose(got, (1, 0, 2)).reshape(out_rows, dim)
    got = net.ctx_all(grad_gu).astype(F32)
    got = got.reshape(halves, 2, gu_rows, 2, m, ff_part)
    got = jnp.transpose(got, (3, 0, 2, 4, 1, 5)).reshape(2, shard, ff)
    out_down = net.ctx_all(grad_down).astype(F32).reshape(halves, 2, d_rows, dim)
    out_down = jnp.transpose(out_down, (1, 0, 2, 3)).reshape(ff_shard, dim)
    return (
        loss,
        layer_out[None],
        grad_tokens[None],
        own_small[0][0],
        out_w_in,
        own_small[4],
        own_small[3][0],
        head_totals[0],
        head_totals[1],
        head_totals[2],
        own_small[2][0],
        out_outs[:mamba_rows],
        out_w_qkv,
        out_outs[mamba_rows:],
        own_small[1][0],
        got[0],
        got[1],
        out_down,
    )


def solution(mesh):
    in_specs = (
        P("fsdp", "ctx", None),
        P("fsdp", "ctx", None),
        P("fsdp", None),
        P("fsdp", "ctx"),
        P("fsdp"),
        P("fsdp", None),
        P(None, "fsdp"),
        P("fsdp"),
        P(),
        P(),
        P(),
        P("fsdp"),
        P("fsdp", None),
        P("fsdp", None),
        P("fsdp", None),
        P("fsdp"),
        P("fsdp", None),
        P("fsdp", None),
        P("fsdp", None),
    )
    out_specs = (
        P(),
        P("fsdp", "ctx", None),
        P("fsdp", "ctx", None),
        P("fsdp"),
        P("fsdp", None),
        P(None, "fsdp"),
        P("fsdp"),
        P(),
        P(),
        P(),
        P("fsdp"),
        P("fsdp", None),
        P("fsdp", None),
        P("fsdp", None),
        P("fsdp"),
        P("fsdp", None),
        P("fsdp", None),
        P("fsdp", None),
    )
    return jax.shard_map(
        per_device, mesh=mesh, in_specs=in_specs, out_specs=out_specs, check_vma=False
    )
```

```python
import functools

import jax
import jax.numpy as jnp
import numpy as np
from jax import lax
from jax.experimental import pallas as pl
from jax.experimental.pallas import tpu as pltpu
from jax.sharding import PartitionSpec as P

MH = 24
HP = 64
NS = 128
KW = 4
QH = 8
KVH = 2
HD = 64
SPAN = 128
QBLK = 256

EPSILON = 1e-05
ROPE_BASE = 100000000000.0
MASKED = -1e30

F32 = jnp.float32
BF16 = jnp.bfloat16
HIGH = lax.Precision.HIGHEST


def nn(left, right, precision=None):
    return lax.dot_general(
        left, right, (((1,), (0,)), ((), ())), precision=precision, preferred_element_type=F32
    )


def nt(left, right):
    return lax.dot_general(left, right, (((1,), (1,)), ((), ())), preferred_element_type=F32)


def tn(left, right):
    return lax.dot_general(left, right, (((0,), (0,)), ((), ())), preferred_element_type=F32)


def swap_halves(values):
    lane = lax.broadcasted_iota(jnp.int32, values.shape, 1) % HD
    size = values.shape[1]
    return jnp.where(
        lane < HD // 2,
        pltpu.roll(values, size - HD // 2, 1),
        pltpu.roll(values, HD // 2, 1),
    )


def conv_kernel(
    tok, gain, weight, taps, bias, same, params, normed_ref, cin_ref, pre_ref, act_ref, step_ref,
    row_ref, halo,
):
    conv = taps.shape[1]
    block = tok.shape[0]

    @pl.when(pl.program_id(0) == 0)
    def _():
        halo[...] = jnp.zeros_like(halo)

    values = tok[...].astype(F32)
    scale = lax.rsqrt(jnp.mean(values * values, axis=-1, keepdims=True) + EPSILON)
    normed = (values * scale * gain[...]).astype(BF16)
    normed_ref[...] = normed
    cin = nn(normed, weight[:, :conv])
    cin_ref[...] = cin.astype(BF16)
    halo[8 : 8 + block, :] = cin
    pre = bias[...] + taps[KW - 1 : KW, :] * cin
    for by in range(1, KW):
        tap = taps[KW - 1 - by : KW - by, :]
        pre = pre + tap * halo[8 - by : 8 - by + block, :] * same[:, by : by + 1]
    halo[0:8, :] = halo[block : block + 8, :]
    pre_ref[...] = pre.astype(BF16)
    act_ref[...] = (pre * jax.nn.sigmoid(pre)).astype(BF16)
    raw = nn(normed, weight[:, conv:]) + params[0:1, :]
    dt = jnp.maximum(raw, 0.0) + jnp.log1p(jnp.exp(-jnp.abs(raw)))
    loga = -dt * params[1:2, :]
    step_ref[:, :128] = dt
    step_ref[:, 128:] = loga
    row_ref[0:8, :] = jnp.transpose(dt)[0:8, :]
    row_ref[8:16, :] = jnp.transpose(loga)[0:8, :]


def by_rows(size):
    return pl.BlockSpec((QBLK, size), lambda i: (i, 0))


def whole(a):
    return pl.BlockSpec(a.shape, lambda i: (0, 0))


def project_conv(tokens, gain, weight, taps, bias, same, params):
    length, dim = tokens.shape
    conv = taps.shape[1]
    sizes = [(dim, BF16), (conv, BF16), (conv, BF16), (conv, BF16), (256, F32)]
    return pl.pallas_call(
        conv_kernel,
        grid=(length // QBLK,),
        in_specs=[
            by_rows(dim),
            whole(gain),
            whole(weight),
            whole(taps),
            whole(bias),
            by_rows(same.shape[1]),
            whole(params),
        ],
        out_specs=[by_rows(size) for size, _ in sizes]
        + [pl.BlockSpec((16, QBLK), lambda i: (0, i))],
        out_shape=[jax.ShapeDtypeStruct((length, size), kind) for size, kind in sizes]
        + [jax.ShapeDtypeStruct((16, length), F32)],
        scratch_shapes=[pltpu.VMEM((QBLK + 8, conv), F32)],
        compiler_params=pltpu.CompilerParams(vmem_limit_bytes=40 * 1024 * 1024),
        cost_estimate=pl.CostEstimate(
            flops=2 * length * dim * weight.shape[1], bytes_accessed=10**7, transcendentals=10**6
        ),
        name="project_conv",
    )(tokens, gain, weight, taps, bias, same, params)


def gate_kernel(normed_ref, weight, y_ref, cosine, sine, z_ref, qkv_ref, sq_ref):
    width = y_ref.shape[1]
    normed = normed_ref[...]
    gate = nn(normed, weight[:, :width])
    z_ref[...] = gate
    qkv = nn(normed, weight[:, width:])
    qkv_ref[...] = (qkv * cosine[...] + swap_halves(qkv) * sine[...]).astype(BF16)
    gated = y_ref[...] * (gate * jax.nn.sigmoid(gate))
    sq_ref[...] = lax.dot_general(
        jnp.ones((8, width), F32),
        gated * gated,
        (((1,), (1,)), ((), ())),
        precision=HIGH,
        preferred_element_type=F32,
    )


def project_gate(normed, weight, y, cosine, sine):
    length, dim = normed.shape
    width = y.shape[1]
    slab = cosine.shape[1]
    return pl.pallas_call(
        gate_kernel,
        grid=(length // QBLK,),
        in_specs=[by_rows(dim), whole(weight), by_rows(width), by_rows(slab), by_rows(slab)],
        out_specs=[
            by_rows(width),
            by_rows(slab),
            pl.BlockSpec((8, QBLK), lambda i: (0, i)),
        ],
        out_shape=[
            jax.ShapeDtypeStruct((length, width), F32),
            jax.ShapeDtypeStruct((length, slab), BF16),
            jax.ShapeDtypeStruct((8, length), F32),
        ],
        compiler_params=pltpu.CompilerParams(vmem_limit_bytes=40 * 1024 * 1024),
        cost_estimate=pl.CostEstimate(
            flops=2 * length * dim * weight.shape[1], bytes_accessed=10**7, transcendentals=10**6
        ),
        name="project_gate",
    )(normed, weight, y, cosine, sine)


def decays(seg_c, seg_r, loga_c, loga_r, before, end):
    row = lax.broadcasted_iota(jnp.int32, (SPAN, SPAN), 0)
    col = lax.broadcasted_iota(jnp.int32, (SPAN, SPAN), 1)
    lower = row >= col
    same = (seg_c == seg_r) & lower
    run_c = nn(lower.astype(F32), loga_c, HIGH)
    run_r = nn(loga_r, (row <= col).astype(F32), HIGH)
    keep = (seg_c == before).astype(F32)
    tail = (seg_c == end).astype(F32)
    return row, col, same, run_c, run_r, keep, tail


def ssm_fwd_kernel(
    heads, ends, skip, act, steps, rows, seg_c, seg_r, y_ref, st_ref, state
):
    step = pl.program_id(0)

    @pl.when(step == 0)
    def _():
        state[...] = jnp.zeros_like(state)

    before, end = ends[step], ends[step + 1]
    link = (before == end).astype(F32)
    _, _, same, run_c, run_r, keep, tail = decays(
        seg_c[...], seg_r[...], steps[:, 128:], rows[8:16, :], before, end
    )
    width = heads * HP
    b_in = act[:, width : width + NS]
    c_in = act[:, width + NS : width + 2 * NS]
    gram = nt(c_in, b_in)
    for h in range(heads):
        lanes = slice(h * HP, (h + 1) * HP)
        x_in = act[:, lanes]
        own_c = run_c[:, h : h + 1]
        last = own_c[SPAN - 1 :, :]
        decay = jnp.where(same, jnp.exp(own_c - run_r[h : h + 1, :]), 0.0)
        mixing = (gram * decay * rows[h : h + 1, :]).astype(BF16)
        prior = state[h]
        st_ref[0, h] = prior
        x_wide = x_in.astype(F32)
        y_out = nn(mixing, x_in) + nt(c_in, prior.astype(BF16)) * (jnp.exp(own_c) * keep)
        y_ref[:, lanes] = y_out + skip[h] * x_wide
        weight = jnp.exp(last - own_c) * tail * steps[:, h : h + 1]
        state[h] = (jnp.exp(last) * link) * prior + tn((x_wide * weight).astype(BF16), b_in)


def ssm_bwd_kernel(
    heads,
    ends,
    skip,
    act,
    steps,
    rows,
    seg_c,
    seg_r,
    st_ref,
    z_ref,
    gym_ref,
    y_ref,
    stat_ref,
    gain_ref,
    pre_ref,
    cin_ref,
    up_ref,
    taps,
    params,
    first_ref,
    gconv_ref,
    gwide_ref,
    gstep_ref,
    gstate,
    gbuf,
    gcol,
    grow,
):
    step = pl.num_programs(0) - 1 - pl.program_id(0)
    width = heads * HP
    conv = width + 2 * NS

    @pl.when(pl.program_id(0) == 0)
    def _():
        gstate[...] = jnp.zeros_like(gstate)
        gbuf[...] = jnp.zeros_like(gbuf)
        gcol[...] = jnp.zeros_like(gcol)
        grow[...] = jnp.zeros_like(grow)
        gconv_ref[...] = jnp.zeros_like(gconv_ref)
        gwide_ref[...] = jnp.zeros_like(gwide_ref)
        gstep_ref[...] = jnp.zeros_like(gstep_ref)

    before, end = ends[step], ends[step + 1]
    link = (before == end).astype(F32)
    row, col, same, run_c, run_r, keep, tail = decays(
        seg_c[...], seg_r[...], steps[:, 128:], rows[8:16, :], before, end
    )
    gate = z_ref[...]
    sig = jax.nn.sigmoid(gate)
    silu = gate * sig
    y_all = y_ref[...]
    gated = y_all * silu
    scale = stat_ref[:, 0:1]
    g_ym = gym_ref[...]
    g_gated = scale * (g_ym * gain_ref[...]) - gated * stat_ref[:, 1:2]
    g_all = g_gated * silu
    gwide_ref[0:1, :] += jnp.sum(g_all * act[:, :width].astype(F32), axis=0, keepdims=True)

    b_in = act[:, width : width + NS]
    c_in = act[:, width + NS : width + 2 * NS]
    gram = nt(c_in, b_in)
    g_gram = jnp.zeros((SPAN, SPAN), F32)
    g_b = jnp.zeros((SPAN, NS), F32)
    g_c = jnp.zeros((SPAN, NS), F32)
    at_last = lax.broadcasted_iota(jnp.int32, (SPAN, 1), 0) == SPAN - 1
    for h in range(heads):
        lanes = slice(h * HP, (h + 1) * HP)
        x_in = act[:, lanes]
        x_wide = x_in.astype(F32)
        gy = g_all[:, lanes]
        gy_low = gy.astype(BF16)
        own_c = run_c[:, h : h + 1]
        last = own_c[SPAN - 1 :, :]
        dt_row = rows[h : h + 1, :]
        decay = jnp.where(same, jnp.exp(own_c - run_r[h : h + 1, :]), 0.0)
        prior = st_ref[0, h]
        prior_low = prior.astype(BF16)
        after = gstate[h]
        after_low = after.astype(BF16)
        carry_w = jnp.exp(own_c) * keep
        tail_w = jnp.exp(last - own_c) * tail
        end_w = tail_w * steps[:, h : h + 1]
        mixing = (gram * decay * dt_row).astype(BF16)
        g_mix = nt(gy_low, x_in) * decay
        g_gram_h = g_mix * dt_row
        g_gram = g_gram + g_gram_h
        inner = g_gram_h * gram
        from_state = nt(b_in, after_low)
        gbuf[0:SPAN, lanes] = tn(mixing, gy_low) + from_state * end_w + skip[h] * gy
        g_carry = jnp.sum(gy * nt(c_in, prior_low), axis=1, keepdims=True)
        g_tail = jnp.sum(x_wide * from_state, axis=1, keepdims=True)
        g_link = jnp.exp(last) * link
        total_last = jnp.sum(g_tail * end_w, axis=0, keepdims=True) + g_link * jnp.sum(
            jnp.sum(after * prior, axis=1, keepdims=True), axis=0, keepdims=True
        )
        g_run_c = jnp.sum(inner, axis=1, keepdims=True) + g_carry * carry_w - g_tail * end_w
        gcol[:, h : h + 1] = g_run_c + jnp.where(at_last, total_last, 0.0)
        gcol[:, 128 + h : 128 + h + 1] = g_tail * tail_w
        grow[h : h + 1, :] = jnp.sum(inner, axis=0, keepdims=True)
        grow[128 + h : 128 + h + 1, :] = jnp.sum(g_mix * gram, axis=0, keepdims=True)
        weighted = (gy * carry_w).astype(BF16)
        g_c = g_c + nn(weighted, prior_low)
        g_b = g_b + nn((x_wide * end_w).astype(BF16), after_low)
        gstate[h] = g_link * after + tn(weighted, c_in)
    g_gram_low = g_gram.astype(BF16)
    gbuf[0:SPAN, width : width + NS] = g_b + tn(g_gram_low, c_in)
    gbuf[0:SPAN, width + NS :] = g_c + nn(g_gram_low, b_in)

    pre = pre_ref[...].astype(F32)
    sig = jax.nn.sigmoid(pre)
    g_pre = gbuf[0:SPAN, :] * (sig + pre * sig * (1.0 - sig))
    gbuf[0:SPAN, :] = g_pre
    cin = cin_ref[...].astype(F32)
    g_conv = taps[KW - 1 : KW, :] * g_pre
    gconv_ref[KW - 1 : KW, :] += jnp.sum(g_pre * cin, axis=0, keepdims=True)
    gconv_ref[KW : KW + 1, :] += jnp.sum(g_pre, axis=0, keepdims=True)
    for by in range(1, KW):
        ahead = gbuf[by : by + SPAN, :] * up_ref[:, by : by + 1]
        tap = KW - 1 - by
        g_conv = g_conv + taps[tap : tap + 1, :] * ahead
        gconv_ref[tap : tap + 1, :] += jnp.sum(ahead * cin, axis=0, keepdims=True)
    gbuf[SPAN : SPAN + 8, :] = gbuf[0:8, :]
    first_ref[:, :conv] = g_conv.astype(BF16)

    later = (col >= row).astype(F32)
    eye = (col == row).astype(F32)

    def across(left, right):
        return lax.dot_general(
            left, right, (((1,), (1,)), ((), ())), precision=HIGH, preferred_element_type=F32
        )

    g_loga = nn(later, gcol[:, :128], HIGH) - across(later, grow[:128, :])
    g_dt = gcol[:, 128:] + across(eye, grow[128:, :]) - g_loga * params[1:2, :]
    g_step = g_dt * (1.0 - jnp.exp(-steps[:, :128]))
    first_ref[:, conv:] = g_step.astype(BF16)
    gstep_ref[0:1, :] += jnp.sum(g_step, axis=0, keepdims=True)
    gstep_ref[1:2, :] += jnp.sum(g_loga * steps[:, 128:], axis=0, keepdims=True)


def ssm_specs(heads, at):
    width = heads * HP
    return [
        pl.BlockSpec(memory_space=pltpu.SMEM),
        pl.BlockSpec(memory_space=pltpu.SMEM),
        pl.BlockSpec((SPAN, width + 2 * NS), lambda i: (at(i), 0)),
        pl.BlockSpec((SPAN, 256), lambda i: (at(i), 0)),
        pl.BlockSpec((16, SPAN), lambda i: (0, at(i))),
        pl.BlockSpec((SPAN, 1), lambda i: (at(i), 0)),
        pl.BlockSpec((1, SPAN), lambda i: (0, at(i))),
    ]


def ssm_forward(heads, inputs):
    length = inputs[2].shape[0]
    steps = length // SPAN
    width = heads * HP
    return pl.pallas_call(
        functools.partial(ssm_fwd_kernel, heads),
        grid=(steps,),
        in_specs=ssm_specs(heads, lambda i: i),
        out_specs=[
            pl.BlockSpec((SPAN, width), lambda i: (i, 0)),
            pl.BlockSpec((1, heads, HP, NS), lambda i: (i, 0, 0, 0)),
        ],
        out_shape=[
            jax.ShapeDtypeStruct((length, width), F32),
            jax.ShapeDtypeStruct((steps, heads, HP, NS), F32),
        ],
        scratch_shapes=[pltpu.VMEM((heads, HP, NS), F32)],
        compiler_params=pltpu.CompilerParams(vmem_limit_bytes=32 * 1024 * 1024),
        cost_estimate=pl.CostEstimate(
            flops=10**9, bytes_accessed=4 * 10**7, transcendentals=10**6
        ),
        name="ssm_forward",
    )(*inputs)


def ssm_backward(heads, inputs, states, gate_z, g_ym, ssm_y, stats, gain, pre, cin, up, taps, params):
    length = inputs[2].shape[0]
    steps = length // SPAN
    width = heads * HP
    conv = width + 2 * NS
    total = conv + 128

    def at(i):
        return steps - 1 - i

    def part(size):
        return pl.BlockSpec((SPAN, size), lambda i: (at(i), 0))

    def fixed(shape):
        return pl.BlockSpec(shape, lambda i: (0, 0))

    return pl.pallas_call(
        functools.partial(ssm_bwd_kernel, heads),
        grid=(steps,),
        in_specs=ssm_specs(heads, at)
        + [
            pl.BlockSpec((1, heads, HP, NS), lambda i: (at(i), 0, 0, 0)),
            part(width),
            part(width),
            part(width),
            part(stats.shape[1]),
            fixed(gain.shape),
            part(conv),
            part(conv),
            part(up.shape[1]),
            fixed(taps.shape),
            fixed(params.shape),
        ],
        out_specs=[part(total), fixed((8, conv)), fixed((8, width)), fixed((8, 128))],
        out_shape=[
            jax.ShapeDtypeStruct((length, total), BF16),
            jax.ShapeDtypeStruct((8, conv), F32),
            jax.ShapeDtypeStruct((8, width), F32),
            jax.ShapeDtypeStruct((8, 128), F32),
        ],
        scratch_shapes=[
            pltpu.VMEM((heads, HP, NS), F32),
            pltpu.VMEM((SPAN + 8, conv), F32),
            pltpu.VMEM((SPAN, 256), F32),
            pltpu.VMEM((256, SPAN), F32),
        ],
        compiler_params=pltpu.CompilerParams(vmem_limit_bytes=56 * 1024 * 1024),
        cost_estimate=pl.CostEstimate(
            flops=3 * 10**9, bytes_accessed=10**8, transcendentals=10**6
        ),
        name="ssm_backward",
    )(*inputs, states, gate_z, g_ym, ssm_y, stats, gain, pre, cin, up, taps, params)


def allowed_keys(index, reach, seg_c, seg_r):
    row = lax.broadcasted_iota(jnp.int32, (QBLK, reach), 0) + index * QBLK
    col = lax.broadcasted_iota(jnp.int32, (QBLK, reach), 1)
    return (seg_c[...] == seg_r[:, :reach]) & (col <= row)


def attn_fwd_kernel(heads, blocks, qkv_ref, seg_c, seg_r, out_ref, lse_ref):
    wide = heads * HD
    for index in range(blocks):

        @pl.when(pl.program_id(0) == index)
        def _(index=index):
            reach = (index + 1) * QBLK
            allowed = allowed_keys(index, reach, seg_c, seg_r)
            own = slice(index * QBLK, reach)
            keys = qkv_ref[:reach, wide : wide + HD]
            values = qkv_ref[:reach, wide + HD : wide + 2 * HD]
            for h in range(heads):
                lanes = slice(h * HD, (h + 1) * HD)
                scores = nt(qkv_ref[own, lanes], keys) * (HD**-0.5)
                scores = jnp.where(allowed, scores, MASKED)
                top = jnp.max(scores, axis=1, keepdims=True)
                expo = jnp.exp(scores - top)
                total = jnp.sum(expo, axis=1, keepdims=True)
                probs = (expo * (1.0 / total)).astype(BF16)
                out_ref[:, lanes] = nn(probs, values).astype(BF16)
                lse_ref[:, h : h + 1] = top + jnp.log(total)


def attn_bwd_kernel(
    heads, blocks, qkv_ref, seg_c, seg_r, lse_ref, go_ref, cosine, sine, out_ref, grads
):
    wide = heads * HD

    @pl.when(pl.program_id(0) == 0)
    def _():
        grads[...] = jnp.zeros_like(grads)

    for index in range(blocks):

        @pl.when(pl.program_id(0) == index)
        def _(index=index):
            reach = (index + 1) * QBLK
            allowed = allowed_keys(index, reach, seg_c, seg_r)
            own = slice(index * QBLK, reach)
            keys = qkv_ref[:reach, wide : wide + HD]
            values = qkv_ref[:reach, wide + HD : wide + 2 * HD]
            for h in range(heads):
                lanes = slice(h * HD, (h + 1) * HD)
                query = qkv_ref[own, lanes]
                g_out = go_ref[:, lanes]
                scores = nt(query, keys) * (HD**-0.5)
                probs = jnp.where(allowed, jnp.exp(scores - lse_ref[:, h : h + 1]), 0.0)
                g_probs = nt(g_out, values)
                delta = jnp.sum(probs * g_probs, axis=1, keepdims=True)
                g_scores = (probs * (g_probs - delta)).astype(BF16)
                grads[own, lanes] = nn(g_scores, keys) * (HD**-0.5)
                grads[:reach, wide : wide + HD] += tn(g_scores, query) * (HD**-0.5)
                grads[:reach, wide + HD : wide + 2 * HD] += tn(probs.astype(BF16), g_out)
            if index == blocks - 1:
                for b in range(blocks):
                    part = slice(b * QBLK, (b + 1) * QBLK)
                    slab = grads[part, :]
                    out_ref[part, :] = (
                        slab * cosine[part, :] - swap_halves(slab) * sine[part, :]
                    ).astype(BF16)


def attn_specs(length, slab):
    return [
        pl.BlockSpec((length, slab), lambda i: (0, 0)),
        pl.BlockSpec((QBLK, 1), lambda i: (i, 0)),
        pl.BlockSpec((1, length), lambda i: (0, 0)),
    ]


def attn_forward(heads, inputs):
    length, slab = inputs[0].shape
    blocks = length // QBLK
    return pl.pallas_call(
        functools.partial(attn_fwd_kernel, heads, blocks),
        grid=(blocks,),
        in_specs=attn_specs(length, slab),
        out_specs=[
            pl.BlockSpec((QBLK, heads * HD), lambda i: (i, 0)),
            pl.BlockSpec((QBLK, heads), lambda i: (i, 0)),
        ],
        out_shape=[
            jax.ShapeDtypeStruct((length, heads * HD), BF16),
            jax.ShapeDtypeStruct((length, heads), F32),
        ],
        compiler_params=pltpu.CompilerParams(vmem_limit_bytes=32 * 1024 * 1024),
        cost_estimate=pl.CostEstimate(
            flops=10**9, bytes_accessed=2 * 10**7, transcendentals=10**6
        ),
        name="attn_forward",
    )(*inputs)


def attn_backward(heads, inputs, lse, g_out, cosine, sine):
    length, slab = inputs[0].shape
    blocks = length // QBLK
    full = pl.BlockSpec((length, slab), lambda i: (0, 0))
    return pl.pallas_call(
        functools.partial(attn_bwd_kernel, heads, blocks),
        grid=(blocks,),
        in_specs=attn_specs(length, slab)
        + [
            pl.BlockSpec((QBLK, heads), lambda i: (i, 0)),
            pl.BlockSpec((QBLK, heads * HD), lambda i: (i, 0)),
            full,
            full,
        ],
        out_specs=full,
        out_shape=jax.ShapeDtypeStruct((length, slab), BF16),
        scratch_shapes=[pltpu.VMEM((length, slab), F32)],
        compiler_params=pltpu.CompilerParams(vmem_limit_bytes=40 * 1024 * 1024),
        cost_estimate=pl.CostEstimate(
            flops=3 * 10**9, bytes_accessed=3 * 10**7, transcendentals=10**6
        ),
        name="attn_backward",
    )(*inputs, lse, g_out, cosine, sine)


def tie(value, *after):
    return lax.optimization_barrier((value,) + after)[0]


def stage(compute, inputs, sends):
    inputs, operands = lax.optimization_barrier((inputs, [operand for _, operand in sends]))
    got = [send(operand) for (send, _), operand in zip(sends, operands)]
    return lax.optimization_barrier((compute(*inputs), got))


class Net:
    def __init__(self):
        self.n = lax.axis_size("ctx")
        self.m = lax.axis_size("fsdp")
        self.c = lax.axis_index("ctx")
        self.f = lax.axis_index("fsdp")
        self.direct = self.n == 4 and self.m == 8
        self.x, self.core = self.c // 2, self.c % 2
        self.z, self.y = self.f // 2, self.f % 2
        self.by_core = [[i * 2 + k for i in range(self.n // 2)] for k in range(2)]

    def flip(self, value, axis, bit):
        size = lax.axis_size(axis)
        return lax.ppermute(value, axis, [(i, i ^ bit) for i in range(size)])

    def shift_z(self, value, by):
        return lax.ppermute(value, "fsdp", [(i, (i + 2 * by) % self.m) for i in range(self.m)])

    def cross(self, value):
        pairs = [
            (c * 8 + z * 2 + y, z * 8 + c * 2 + y)
            for c in range(4)
            for z in range(4)
            for y in range(2)
        ]
        return lax.ppermute(value, ("ctx", "fsdp"), pairs)

    def along_z(self, block):
        return [block] + [self.shift_z(block, k) for k in range(1, 4)]

    def along_y(self, pieces):
        return [self.flip(piece, "fsdp", 1) for piece in pieces]

    def in_order(self, own, mate, columns=None):
        places = [2 * ((self.z - k) % 4) + (self.y ^ o) for o in range(2) for k in range(4)]
        return put(own + mate, places, columns)

    def flip_y(self, value):
        return self.flip(value, "fsdp", 1)

    def flip_x(self, value):
        return self.flip(value, "ctx", 2)

    def flip_core(self, value):
        return self.flip(value, "ctx", 1)

    def halves_y(self, sums):
        low = sums.astype(BF16)
        low = low.reshape((4, 2) + low.shape[1:])
        away = lax.dynamic_index_in_dim(low, 1 - self.y, 1, False)
        return lax.dynamic_index_in_dim(low, self.y, 1, False), away

    def shifts_z(self, both):
        sent = [lax.dynamic_index_in_dim(both, (self.z + k) % 4, 0, False) for k in range(4)]
        return [sent[0]] + [self.shift_z(sent[k], k) for k in range(1, 4)]

    def collect(self, sums):
        return lax.psum_scatter(sums.astype(BF16), "fsdp", scatter_dimension=0, tiled=False)

    def ctx_all(self, value):
        if not self.direct:
            return lax.all_gather(value, "ctx", axis=0, tiled=False)
        pair = jnp.stack([value, self.flip(value, "ctx", 2)])
        mates = self.flip(pair, "ctx", 1)
        return put([pair, mates], [self.c, self.c ^ 2, self.c ^ 1, self.c ^ 3])

    def ctx_sum(self, value):
        if not self.direct:
            return lax.psum(value, "ctx")
        value = value + self.flip(value, "ctx", 1)
        return value + self.flip(value, "ctx", 2)

    def ctx_collect(self, parts):
        if not self.direct:
            low = lax.psum_scatter(parts.astype(BF16), "ctx", scatter_dimension=0, tiled=False)
            return low.astype(F32)
        pairs = parts.reshape((2, 2) + parts.shape[1:])
        away = lax.dynamic_index_in_dim(pairs, 1 - self.core, 1, False).astype(BF16)
        here = lax.dynamic_index_in_dim(pairs, self.core, 1, False)
        got = self.flip(away, "ctx", 1)

        def half(which):
            return lax.dynamic_index_in_dim(here, which, 0, False).astype(
                F32
            ) + lax.dynamic_index_in_dim(got, which, 0, False).astype(F32)

        across = self.flip(half(1 - self.x).astype(BF16), "ctx", 2)
        return half(self.x) + across.astype(F32)

    def over_cores(self, value):
        if not self.direct:
            value = lax.psum(value, "ctx", axis_index_groups=self.by_core)
            return lax.all_gather(value, "ctx", axis=0)[:2].astype(F32)
        value = (value.astype(F32) + self.flip(value, "ctx", 2).astype(F32)).astype(BF16)
        mate = self.flip(value, "ctx", 1)
        pair = jnp.stack([value, mate]).astype(F32)
        return jnp.where(self.core == 0, pair, pair[::-1])

    def rows_out(self, shard):
        per = self.m // self.n
        got = lax.all_gather(shard, "fsdp", axis=0, tiled=False)
        return lax.dynamic_slice_in_dim(got, self.c * per, per, 0)

    def rows_back(self, sums):
        wide = jnp.zeros((self.m,) + sums.shape[1:], BF16)
        wide = lax.dynamic_update_slice_in_dim(
            wide, sums.astype(BF16), self.c * (self.m // self.n), 0
        )
        out = lax.psum_scatter(wide, "fsdp", scatter_dimension=0, tiled=False)
        return lax.psum(out, "ctx")


def put_kernel(counts, cuts, places, *refs):
    parts, outs = refs[: len(counts)], refs[len(counts) :]
    start = 0
    for part, count in zip(parts, counts):

        @pl.when((pl.program_id(0) >= start) & (pl.program_id(0) < start + count))
        def _(part=part):
            for out, low, high in zip(outs, cuts[:-1], cuts[1:]):
                out[...] = part[..., low:high]

        start += count


def put(parts, places, columns=None):
    counts = [part.shape[0] for part in parts]
    total = sum(counts)
    shape = parts[0].shape[1:]
    zeros = (0,) * len(shape)
    sizes = columns or [shape[-1]]
    cuts = [0]
    for size in sizes:
        cuts.append(cuts[-1] + size)
    places = jnp.stack([jnp.asarray(p, jnp.int32) for p in places])
    size = parts[0][0].size * parts[0].dtype.itemsize
    specs = []
    for p in range(len(parts)):
        start = sum(counts[:p])

        def at(i, at, start=start, last=counts[p] - 1):
            return (jnp.clip(i - start, 0, last),) + zeros

        specs.append(pl.BlockSpec((1,) + shape, at))
    out = pl.pallas_call(
        functools.partial(put_kernel, counts, cuts),
        grid_spec=pltpu.PrefetchScalarGridSpec(
            num_scalar_prefetch=1,
            grid=(total,),
            in_specs=specs,
            out_specs=[
                pl.BlockSpec((1,) + shape[:-1] + (w,), lambda i, at: (at[i],) + zeros)
                for w in sizes
            ],
        ),
        out_shape=[
            jax.ShapeDtypeStruct((total,) + shape[:-1] + (w,), parts[0].dtype) for w in sizes
        ],
        compiler_params=pltpu.CompilerParams(vmem_limit_bytes=40 * 1024 * 1024),
        cost_estimate=pl.CostEstimate(
            flops=0, bytes_accessed=2 * total * size, transcendentals=0
        ),
        name="put",
    )(places, *parts)
    return out if columns else out[0]


def rms_scale(values):
    return lax.rsqrt(jnp.mean(values * values, axis=-1, keepdims=True) + EPSILON)


def rms_back(values, gain, scale, grad):
    scaled = grad * gain
    inner = jnp.mean(values * scaled, axis=-1, keepdims=True)
    return scale * scaled - values * (scale * scale * scale * inner)


def columns_of(w, start, size):
    return lax.dynamic_slice_in_dim(w, start, size, 1)


def rotary_tables(length, q_heads, slab):
    half = HD // 2
    freq = (ROPE_BASE ** (-(np.arange(half) * 2.0 / HD))).astype(np.float32)
    angle = np.arange(length, dtype=np.float32)[:, None] * freq[None, :]
    one = np.concatenate([np.cos(angle), np.cos(angle)], axis=1)
    two = np.concatenate([-np.sin(angle), np.sin(angle)], axis=1)
    room = slab - (q_heads + 1) * HD
    cosine = np.concatenate([one] * (q_heads + 1) + [np.ones((length, room))], axis=1)
    sine = np.concatenate([two] * (q_heads + 1) + [np.zeros((length, room))], axis=1)
    return jnp.asarray(cosine, F32), jnp.asarray(sine, F32)


def per_device(
    tokens,
    teacher,
    segment_ids,
    valid_mask,
    gain_in,
    w_in,
    conv_w,
    conv_b,
    dt_bias,
    a_log,
    d_skip,
    gain_m,
    w_out,
    w_qkv,
    w_o,
    gain_ffn,
    w_gate,
    w_up,
    w_down,
):
    net = Net()
    n, m, c, f = net.n, net.m, net.c, net.f
    rows, dim = tokens.shape[1:]
    length = segment_ids.shape[1]
    shard = w_in.shape[0]
    wide = MH * HP
    conv_full = wide + 2 * NS
    heads = MH // n
    q_heads = QH // n
    width = heads * HP
    conv_width = width + 2 * NS
    q_width = q_heads * HD
    slab = q_width + 2 * HD
    slab += -slab % 128
    group = QH // KVH
    kv_at = (c * q_heads) // group
    ff = w_gate.shape[1]
    ff_shard = w_down.shape[0]
    per = m // n
    seg = segment_ids[0]
    seg_c, seg_r = seg[:, None], seg[None, :]
    ends = jnp.concatenate([jnp.full((1,), -1, jnp.int32), seg[SPAN - 1 :: SPAN]])
    valid = valid_mask[0].astype(F32)

    def lay(values):
        values = values.reshape((-1, values.shape[-1]))
        room = -values.shape[1] % 128
        return jnp.pad(values, ((0, 0), (0, room))).reshape(-1, 128)

    def unlay(small, start, lead, size):
        room = size + -size % 128
        count = lead * room // 128
        return small[..., start : start + count, :].reshape(small.shape[:-2] + (lead, room))[
            ..., :size
        ]

    shapes = [(1, shard), (1, shard), (1, w_out.shape[0]), (1, conv_b.shape[0])]
    shapes += [(KW, conv_b.shape[0])]
    starts = [0]
    for lead, size in shapes:
        starts.append(starts[-1] + lead * (size + -size % 128) // 128)
    laid = [lay(p) for p in (gain_in[None], gain_ffn[None], gain_m[None], conv_b[None], conv_w)]
    laid.append(jnp.full((1, 128), jnp.sum(valid), F32).astype(BF16))
    laid.append(jnp.zeros((-(starts[-1] + 1) % 16, 128), BF16))
    at_small = 64
    packed = jnp.concatenate(laid, axis=0)
    first = jnp.concatenate(
        [
            columns_of(w_in, wide + c * width, width),
            w_in[:, 2 * wide : 2 * wide + 2 * NS],
            columns_of(w_in, wide + conv_full + c * heads, heads),
            jnp.zeros((shard, at_small - heads), BF16),
            packed.T if net.direct else jnp.zeros((shard, packed.shape[0]), BF16),
            jnp.zeros((shard, 128 - at_small - packed.shape[0]), BF16),
        ],
        axis=1,
    )
    second = jnp.concatenate(
        [
            columns_of(w_in, c * width, width),
            columns_of(w_qkv, c * q_width, q_width),
            columns_of(w_qkv, QH * HD + kv_at * HD, HD),
            columns_of(w_qkv, (QH + KVH) * HD + kv_at * HD, HD),
            jnp.zeros((shard, slab - q_width - 2 * HD), BF16),
        ],
        axis=1,
    )
    both_out = jnp.concatenate([w_out, w_o], axis=0)
    out_rows, mamba_rows = both_out.shape[0], w_out.shape[0]
    ff_half = ff_shard // 2
    size = m * ff_half

    def ff_cut(w):
        w = w.reshape(shard, m, 2, ff_half)
        return lax.dynamic_index_in_dim(w, net.core, 2, False).reshape(shard, size)

    w_ff = jnp.concatenate(
        [
            ff_cut(w_gate).reshape(-1, dim),
            ff_cut(w_up).reshape(-1, dim),
            lax.dynamic_slice_in_dim(w_down, net.core * ff_half, ff_half, 0),
        ],
        axis=0,
    )
    w_ff = lax.all_gather(w_ff, "fsdp", axis=0, tiled=False)
    if net.direct:
        both_cols = jnp.concatenate([first, second], axis=1)
        pair = jnp.stack([tokens[0], net.flip_x(tokens[0])])
        near = net.along_z(both_cols)
        far = net.along_y([tie(near[0], pair)] + near[1:])
        w_first, w_second = net.in_order(
            [p[None] for p in near],
            [p[None] for p in far],
            [first.shape[1], second.shape[1]],
        )
        at = conv_width + at_small
        small = jnp.swapaxes(w_first[:, :, at : at + packed.shape[0]], 1, 2)
        all_tokens = put([pair, net.flip_core(pair)], [c, c ^ 2, c ^ 1, c ^ 3])
        crossed = net.cross(tie(both_out, *near[1:]))
    else:
        small = lax.all_gather(packed, "fsdp", axis=0, tiled=False)
        w_first = lax.all_gather(first, "fsdp", axis=0, tiled=False)
        w_second = lax.all_gather(second, "fsdp", axis=0, tiled=False)
        w_outs = net.rows_out(both_out)
        all_tokens = net.ctx_all(tokens[0])
    all_tokens = all_tokens.reshape(length, dim)
    w_first = w_first.reshape(dim, first.shape[1])
    cuts = [
        jnp.transpose(unlay(small, start, *shape), (1, 0, 2)).reshape(shape[0], -1)
        for start, shape in zip(starts, shapes)
    ]
    gain_input = cuts[0].astype(F32)
    gain_second = cuts[1].astype(F32)
    gain_mamba = lax.dynamic_slice_in_dim(cuts[2], c * width, width, 1).astype(F32)
    count_ctx = jnp.sum(small[:, starts[-1], 0].astype(F32))

    def conv_cut(values):
        own = lax.dynamic_slice_in_dim(values, c * width, width, 1)
        return jnp.concatenate([own, values[:, wide:]], axis=1).astype(F32)

    bias, taps = conv_cut(cuts[3]), conv_cut(cuts[4])
    rate = jnp.exp(a_log)
    params = jnp.stack(
        [lax.dynamic_slice_in_dim(v, c * heads, heads) for v in (dt_bias, rate)]
    )
    params = jnp.pad(params, ((0, 6), (0, 128 - heads)))
    skip = lax.dynamic_slice_in_dim(d_skip, c * heads, heads)

    def shifted(by):
        return jnp.concatenate([jnp.full((by,), -1, jnp.int32), seg[: length - by]]) == seg

    same = jnp.stack([shifted(by) for by in range(KW)], axis=1).astype(F32)
    up = jnp.stack(
        [
            jnp.concatenate([seg[by:], jnp.full((by,), -1, jnp.int32)]) == seg
            for by in range(KW)
        ],
        axis=1,
    ).astype(F32)
    cosine, sine = rotary_tables(length, q_heads, slab)
    conv_args = (all_tokens, gain_input, w_first, taps, bias, same, params)

    def square_rows(square):
        return jnp.concatenate([square[0].reshape(-1, 128), jnp.full((8, 128), count_ctx)])

    def ssm(act, steps, step_rows):
        return ssm_forward(heads, (ends, skip, act, steps, step_rows, seg_c, seg_r))

    def attend(qkv):
        return attn_forward(q_heads, (qkv, seg_c, seg_r))

    w_second = w_second.reshape(dim, second.shape[1])
    if net.direct:
        normed, cin, pre, act, steps, step_rows = project_conv(*conv_args)
        ssm_y, states = ssm(act, steps, step_rows)
        gate_z, qkv, square = project_gate(normed, w_second, ssm_y, cosine, sine)
        mated = net.flip_y(tie(crossed, ssm_y))
        (attended, lse), (square,) = stage(
            attend, (qkv,), [(net.ctx_sum, square_rows(square))]
        )
        w_outs = jnp.where(
            net.y == 0, jnp.stack([crossed, mated]), jnp.stack([mated, crossed])
        )
    else:
        normed, cin, pre, act, steps, step_rows = project_conv(*conv_args)
        ssm_y, states = ssm(act, steps, step_rows)
        gate_z, qkv, square = project_gate(normed, w_second, ssm_y, cosine, sine)
        square = net.ctx_sum(square_rows(square))
        attended, lse = attend(qkv)
    w_mamba = w_outs[:, :mamba_rows].reshape(per * mamba_rows, dim)
    w_attn = w_outs[:, mamba_rows:].reshape(per * (out_rows - mamba_rows), dim)
    ssm_in = (ends, skip, act, steps, step_rows, seg_c, seg_r)
    count = square[-1, 0]
    scale_m = lax.rsqrt(square[:-8].reshape(length, 1) / wide + EPSILON)
    gated = ssm_y * (gate_z * jax.nn.sigmoid(gate_z))
    ym = (gated * scale_m * gain_mamba).astype(BF16)
    outs = nn(ym, w_mamba) + nn(attended, w_attn)
    mixed = tokens[0].astype(F32) + net.ctx_collect(outs.reshape(n, rows, dim))

    ff_rows = shard * size // dim
    w_g = w_ff[:, :ff_rows].reshape(dim, size)
    w_u = w_ff[:, ff_rows : 2 * ff_rows].reshape(dim, size)
    w_d = w_ff[:, 2 * ff_rows :].reshape(size, dim)
    scale2 = rms_scale(mixed)
    normed2 = (mixed * scale2 * gain_second).astype(BF16)
    mate = [(i, i ^ 1) for i in range(n)]
    both = jnp.concatenate([normed2, lax.ppermute(normed2, "ctx", mate)], axis=0)
    gate_v, up_v = nn(both, w_g), nn(both, w_u)
    sig = jax.nn.sigmoid(gate_v)
    product = (gate_v * sig * up_v).astype(BF16)
    down_out = nn(product, w_d)
    from_mate = lax.ppermute(down_out[rows:].astype(BF16), "ctx", mate)
    layer_out = mixed + down_out[:rows] + from_mate.astype(F32)
    diff = layer_out - teacher[0].astype(F32)
    squared = jnp.sum(valid[:, None] * diff * diff)
    token_total = length * m * tokens.shape[0]
    grad_out = token_total * valid[:, None] * diff / count

    gb = grad_out.astype(BF16)
    gb_both = jnp.concatenate([gb, lax.ppermute(gb, "ctx", mate)], axis=0)
    g_prod = nt(gb_both, w_d)
    g_gate = (g_prod * up_v * (sig * (1.0 + gate_v * (1.0 - sig)))).astype(BF16)
    g_up = (g_prod * gate_v * sig).astype(BF16)
    g_n2 = nt(g_gate, w_g) + nt(g_up, w_u)
    from_mate = lax.ppermute(g_n2[rows:].astype(BF16), "ctx", mate)
    grad_n2 = g_n2[:rows] + from_mate.astype(F32)
    part = rms_back(mixed, gain_second, scale2, grad_n2)
    grad_mixed = grad_out + part

    def ff_weights(both, g_gate, g_up, product, gb_both):
        return jnp.concatenate(
            [
                tn(both, g_gate).reshape(m, ff_rows, dim),
                tn(both, g_up).reshape(m, ff_rows, dim),
                tn(product, gb_both).reshape(m, ff_half, dim),
            ],
            axis=1,
        ).astype(BF16)

    ff_args = (both, g_gate, g_up, product, gb_both)
    gm = grad_mixed.astype(BF16)
    if net.direct:
        g_ff, (across,) = stage(ff_weights, ff_args, [(net.flip_x, gm)])
        pair = jnp.stack([gm, across])
        gm = put([pair, net.flip_core(pair)], [c, c ^ 2, c ^ 1, c ^ 3])
    else:
        gm = net.ctx_all(gm)
        g_ff = ff_weights(*ff_args)
    gm = gm.reshape(length, dim)
    g_ff = lax.psum_scatter(g_ff, "fsdp", scatter_dimension=0, tiled=False)

    g_ym = nt(gm, w_mamba)
    inner = jnp.sum(gated * (g_ym * gain_mamba), axis=1).reshape(-1, 128)

    def outs_back(gm):
        g_ob = nt(gm, w_attn).astype(BF16)
        g_outs = jnp.concatenate(
            [
                tn(ym, gm).reshape(per, mamba_rows, dim),
                tn(attended, gm).reshape(per, out_rows - mamba_rows, dim),
            ],
            axis=1,
        )
        return g_ob, g_outs.astype(BF16)

    def attend_back(qkv, g_ob):
        return attn_backward(q_heads, (qkv, seg_c, seg_r), lse, g_ob, cosine, sine)

    def plus(here, got):
        return (here.astype(F32) + got.astype(F32)).astype(BF16)

    if net.direct:
        (g_ob, g_outs), (got,) = stage(outs_back, (gm,), [(net.flip_core, inner)])
        inner = inner + got
        here = lax.dynamic_index_in_dim(g_outs, net.y, 0, False)
        away = lax.dynamic_index_in_dim(g_outs, 1 - net.y, 0, False)
        g_qkv, (got_x, got) = stage(
            attend_back, (qkv, g_ob), [(net.flip_x, inner), (net.flip_y, away)]
        )
        inner = inner + got_x
        out_both = plus(here, got).reshape(4, out_rows // 4, dim)
    else:
        g_ob, g_outs = outs_back(gm)
        inner = net.ctx_sum(inner)
        g_qkv = attend_back(qkv, g_ob)
    inner = inner.reshape(length, 1) / wide
    stats = jnp.concatenate([scale_m, scale_m * scale_m * scale_m * inner], axis=1)
    g_gated = stats[:, :1] * (g_ym * gain_mamba) - gated * stats[:, 1:]
    sig_z = jax.nn.sigmoid(gate_z)
    g_z = (g_gated * ssm_y * (sig_z + gate_z * sig_z * (1.0 - sig_z))).astype(BF16)
    early = jnp.concatenate([g_z, g_qkv], axis=1)
    grad_early = tn(normed, early).reshape(m, shard, width + slab)

    def ssm_back(states):
        return ssm_backward(
            heads,
            ssm_in,
            states,
            gate_z,
            g_ym,
            ssm_y,
            stats,
            gain_mamba,
            pre,
            cin,
            up,
            taps,
            params,
        )

    if net.direct:
        here, away = net.halves_y(grad_early)
        (g_late, g_conv, g_wide, g_steps), (got, out_parts) = stage(
            ssm_back, (states,), [(net.flip_y, away), (net.shifts_z, out_both)]
        )
        grad_early = plus(here, got)
        out_quarter = sum(p.astype(F32) for p in out_parts).astype(BF16)
    else:
        g_late, g_conv, g_wide, g_steps = ssm_back(states)

    def to_wide(values, at, size):
        out = jnp.zeros(values.shape[:-1] + (size,), F32)
        return lax.dynamic_update_slice_in_dim(out, values, at, values.ndim - 1)

    def for_shards(values):
        values = jnp.concatenate(
            [to_wide(values[:, :width], c * width, wide), values[:, width:]], axis=1
        )
        values = values.reshape((-1, m, values.shape[-1] // m))
        return jnp.transpose(values, (1, 0, 2))

    conv_rows = (conv_b.shape[0] + 127) // 128
    heads_grads = jnp.stack(
        [
            to_wide(g_steps[0, :heads], c * heads, MH),
            to_wide(g_steps[1, :heads], c * heads, MH),
            to_wide(jnp.sum(g_wide[0].reshape(heads, HP), axis=1), c * heads, MH),
            jnp.full((MH,), squared),
        ]
    )
    laid = [jax.vmap(lay)(for_shards(g_conv[: KW + 1]))]
    laid.append(jnp.broadcast_to(lay(heads_grads)[None], (m, 4, 128)))
    laid = jnp.concatenate(laid, axis=1)
    room = -laid.shape[1] % 16
    laid = jnp.pad(laid, ((0, 0), (0, room), (0, conv_width)))
    late_size = conv_width + 128
    grad_late = jnp.concatenate(
        [tn(normed, g_late).reshape(m, shard, late_size).astype(BF16), laid.astype(BF16)], axis=1
    )
    resid = tokens[0].astype(F32)

    def normed_back(early, g_late):
        return (nt(early, w_second) + nt(g_late, w_first)).reshape(n, rows, dim)

    def tokens_back(grad_normed):
        return grad_mixed + rms_back(resid, gain_input, rms_scale(resid), grad_normed)

    if net.direct:
        here, away = net.halves_y(grad_late)
        g_normed, (got, early_parts, out_quarter) = stage(
            normed_back,
            (early, g_late),
            [(net.flip_y, away), (net.shifts_z, grad_early), (net.cross, out_quarter)],
        )
        grad_early = sum(p.astype(F32) for p in early_parts).astype(BF16)
        _, (late_parts, grad_normed) = stage(
            tuple,
            (),
            [(net.shifts_z, plus(here, got)), (net.ctx_collect, g_normed)],
        )
        grad_late = sum(p.astype(F32) for p in late_parts).astype(BF16)
        joined = jnp.concatenate([grad_early, out_quarter.reshape(shard, -1)], axis=1)
        joined = jnp.pad(joined, ((0, grad_late.shape[0] - shard), (0, 0)))
        joined = jnp.concatenate([grad_late, joined], axis=1)
        grad_tokens, (got, got_ff) = stage(
            tokens_back, (grad_normed,), [(net.ctx_all, joined), (net.over_cores, g_ff)]
        )
        got_late = got[:, :, :late_size]
        got = got[:, :shard, late_size:].astype(F32)
        got_early = got[:, :, : width + slab]
        out_outs = got[:, :, width + slab :].reshape(out_rows, dim)
    else:
        grad_tokens = tokens_back(net.ctx_collect(normed_back(early, g_late)))
        got_early = net.ctx_all(net.collect(grad_early)).astype(F32)
        got_late = net.ctx_all(net.collect(grad_late))
        out_outs = net.rows_back(g_outs).astype(F32)
        got_ff = net.over_cores(g_ff)
    got_late = got_late.astype(F32)
    totals = jnp.sum(got_late[:, shard:, :128], axis=0)
    got_late = got_late[:, :shard]
    grad_conv = unlay(totals, 0, KW + 1, conv_b.shape[0])
    head_totals = totals[(KW + 1) * conv_rows : (KW + 1) * conv_rows + 4, :MH]
    loss = head_totals[3, 0] / (2.0 * count)

    def side(got, start, size):
        return [got[j][:, start : start + size] for j in range(n)]

    shared = n // KVH
    out_w_in = jnp.concatenate(
        side(got_early, 0, width)
        + side(got_late, 0, width)
        + [sum(side(got_late, width, 2 * NS))]
        + side(got_late, conv_width, heads),
        axis=1,
    )
    out_w_qkv = jnp.concatenate(
        side(got_early, width, q_width)
        + [
            sum(side(got_early, width + q_width + i * HD, HD)[k * shared : (k + 1) * shared])
            for i in range(2)
            for k in range(KVH)
        ],
        axis=1,
    )

    def ff_wide(values):
        values = values.reshape(2, shard, m, ff_half)
        return jnp.transpose(values, (1, 2, 0, 3)).reshape(shard, ff)

    out_gate = ff_wide(got_ff[:, :ff_rows])
    out_up = ff_wide(got_ff[:, ff_rows : 2 * ff_rows])
    out_mamba = out_outs[:mamba_rows]

    def along(*pairs):
        return sum(jnp.sum(w.astype(F32) * g, axis=1) for w, g in pairs)

    return (
        loss,
        layer_out[None],
        grad_tokens[None],
        along((w_in, out_w_in), (w_qkv, out_w_qkv)) / gain_in.astype(F32),
        out_w_in,
        grad_conv[:KW],
        grad_conv[KW],
        head_totals[0],
        head_totals[1],
        head_totals[2],
        along((w_out, out_mamba)) / gain_m.astype(F32),
        out_mamba,
        out_w_qkv,
        out_outs[mamba_rows:],
        along((w_gate, out_gate), (w_up, out_up)) / gain_ffn.astype(F32),
        out_gate,
        out_up,
        got_ff[:, 2 * ff_rows :].reshape(ff_shard, dim),
    )


def solution(mesh):
    in_specs = (
        P("fsdp", "ctx", None),
        P("fsdp", "ctx", None),
        P("fsdp", None),
        P("fsdp", "ctx"),
        P("fsdp"),
        P("fsdp", None),
        P(None, "fsdp"),
        P("fsdp"),
        P(),
        P(),
        P(),
        P("fsdp"),
        P("fsdp", None),
        P("fsdp", None),
        P("fsdp", None),
        P("fsdp"),
        P("fsdp", None),
        P("fsdp", None),
        P("fsdp", None),
    )
    out_specs = (
        P(),
        P("fsdp", "ctx", None),
        P("fsdp", "ctx", None),
        P("fsdp"),
        P("fsdp", None),
        P(None, "fsdp"),
        P("fsdp"),
        P(),
        P(),
        P(),
        P("fsdp"),
        P("fsdp", None),
        P("fsdp", None),
        P("fsdp", None),
        P("fsdp"),
        P("fsdp", None),
        P("fsdp", None),
        P("fsdp", None),
    )
    return jax.shard_map(
        per_device, mesh=mesh, in_specs=in_specs, out_specs=out_specs, check_vma=False
    )
```

```python
import functools

import jax
import jax.numpy as jnp
import numpy as np
from jax import lax
from jax.experimental import pallas as pl
from jax.experimental.pallas import tpu as pltpu
from jax.sharding import PartitionSpec as P

MH = 24
HP = 64
NS = 128
KW = 4
QH = 8
KVH = 2
HD = 64
SPAN = 128
QBLK = 256

EPSILON = 1e-05
ROPE_BASE = 100000000000.0
MASKED = -1e30

F32 = jnp.float32
BF16 = jnp.bfloat16
HIGH = lax.Precision.HIGHEST


def nn(left, right, precision=None):
    return lax.dot_general(
        left, right, (((1,), (0,)), ((), ())), precision=precision, preferred_element_type=F32
    )


def nt(left, right):
    return lax.dot_general(left, right, (((1,), (1,)), ((), ())), preferred_element_type=F32)


def tn(left, right):
    return lax.dot_general(left, right, (((0,), (0,)), ((), ())), preferred_element_type=F32)


def swap_halves(values):
    lane = lax.broadcasted_iota(jnp.int32, values.shape, 1) % HD
    size = values.shape[1]
    return jnp.where(
        lane < HD // 2,
        pltpu.roll(values, size - HD // 2, 1),
        pltpu.roll(values, HD // 2, 1),
    )


def conv_kernel(
    tok, gain, weight, taps, bias, same, params, normed_ref, cin_ref, pre_ref, act_ref, step_ref,
    row_ref, halo,
):
    conv = taps.shape[1]
    block = tok.shape[0]

    @pl.when(pl.program_id(0) == 0)
    def _():
        halo[...] = jnp.zeros_like(halo)

    values = tok[...].astype(F32)
    scale = lax.rsqrt(jnp.mean(values * values, axis=-1, keepdims=True) + EPSILON)
    normed = (values * scale * gain[...]).astype(BF16)
    normed_ref[...] = normed
    cin = nn(normed, weight[:, :conv])
    cin_ref[...] = cin.astype(BF16)
    halo[8 : 8 + block, :] = cin
    pre = bias[...] + taps[KW - 1 : KW, :] * cin
    for by in range(1, KW):
        tap = taps[KW - 1 - by : KW - by, :]
        pre = pre + tap * halo[8 - by : 8 - by + block, :] * same[:, by : by + 1]
    halo[0:8, :] = halo[block : block + 8, :]
    pre_ref[...] = pre.astype(BF16)
    act_ref[...] = (pre * jax.nn.sigmoid(pre)).astype(BF16)
    raw = nn(normed, weight[:, conv:]) + params[0:1, :]
    dt = jnp.maximum(raw, 0.0) + jnp.log1p(jnp.exp(-jnp.abs(raw)))
    loga = -dt * params[1:2, :]
    step_ref[:, :128] = dt
    step_ref[:, 128:] = loga
    row_ref[0:8, :] = jnp.transpose(dt)[0:8, :]
    row_ref[8:16, :] = jnp.transpose(loga)[0:8, :]


def by_rows(size):
    return pl.BlockSpec((QBLK, size), lambda i: (i, 0))


def whole(a):
    return pl.BlockSpec(a.shape, lambda i: (0, 0))


def project_conv(tokens, gain, weight, taps, bias, same, params):
    length, dim = tokens.shape
    conv = taps.shape[1]
    sizes = [(dim, BF16), (conv, BF16), (conv, BF16), (conv, BF16), (256, F32)]
    return pl.pallas_call(
        conv_kernel,
        grid=(length // QBLK,),
        in_specs=[
            by_rows(dim),
            whole(gain),
            whole(weight),
            whole(taps),
            whole(bias),
            by_rows(same.shape[1]),
            whole(params),
        ],
        out_specs=[by_rows(size) for size, _ in sizes]
        + [pl.BlockSpec((16, QBLK), lambda i: (0, i))],
        out_shape=[jax.ShapeDtypeStruct((length, size), kind) for size, kind in sizes]
        + [jax.ShapeDtypeStruct((16, length), F32)],
        scratch_shapes=[pltpu.VMEM((QBLK + 8, conv), F32)],
        compiler_params=pltpu.CompilerParams(vmem_limit_bytes=40 * 1024 * 1024),
        cost_estimate=pl.CostEstimate(
            flops=2 * length * dim * weight.shape[1], bytes_accessed=10**7, transcendentals=10**6
        ),
        name="project_conv",
    )(tokens, gain, weight, taps, bias, same, params)


def gate_kernel(normed_ref, weight, y_ref, cosine, sine, z_ref, qkv_ref, sq_ref):
    width = y_ref.shape[1]
    normed = normed_ref[...]
    gate = nn(normed, weight[:, :width])
    z_ref[...] = gate
    qkv = nn(normed, weight[:, width:])
    qkv_ref[...] = (qkv * cosine[...] + swap_halves(qkv) * sine[...]).astype(BF16)
    gated = y_ref[...] * (gate * jax.nn.sigmoid(gate))
    sq_ref[...] = lax.dot_general(
        jnp.ones((8, width), F32),
        gated * gated,
        (((1,), (1,)), ((), ())),
        precision=HIGH,
        preferred_element_type=F32,
    )


def project_gate(normed, weight, y, cosine, sine):
    length, dim = normed.shape
    width = y.shape[1]
    slab = cosine.shape[1]
    return pl.pallas_call(
        gate_kernel,
        grid=(length // QBLK,),
        in_specs=[by_rows(dim), whole(weight), by_rows(width), by_rows(slab), by_rows(slab)],
        out_specs=[
            by_rows(width),
            by_rows(slab),
            pl.BlockSpec((8, QBLK), lambda i: (0, i)),
        ],
        out_shape=[
            jax.ShapeDtypeStruct((length, width), F32),
            jax.ShapeDtypeStruct((length, slab), BF16),
            jax.ShapeDtypeStruct((8, length), F32),
        ],
        compiler_params=pltpu.CompilerParams(vmem_limit_bytes=40 * 1024 * 1024),
        cost_estimate=pl.CostEstimate(
            flops=2 * length * dim * weight.shape[1], bytes_accessed=10**7, transcendentals=10**6
        ),
        name="project_gate",
    )(normed, weight, y, cosine, sine)


def decays(seg_c, seg_r, loga_c, loga_r, before, end):
    row = lax.broadcasted_iota(jnp.int32, (SPAN, SPAN), 0)
    col = lax.broadcasted_iota(jnp.int32, (SPAN, SPAN), 1)
    lower = row >= col
    same = (seg_c == seg_r) & lower
    run_c = nn(lower.astype(F32), loga_c, HIGH)
    run_r = nn(loga_r, (row <= col).astype(F32), HIGH)
    keep = (seg_c == before).astype(F32)
    tail = (seg_c == end).astype(F32)
    return row, col, same, run_c, run_r, keep, tail


def head_groups(heads):
    return [tuple(range(g, min(g + 2, heads))) for g in range(0, heads, 2)]


def by_lane(columns, group, size):
    first = columns[:, group[0] : group[0] + 1]
    if len(group) == 1:
        return first
    lane = lax.broadcasted_iota(jnp.int32, (columns.shape[0], size), 1)
    return jnp.where(lane < HP, first, columns[:, group[1] : group[1] + 1])


def stacked(values, group):
    if len(group) == 1:
        return values
    lane = lax.broadcasted_iota(jnp.int32, values.shape, 1)
    zero = jnp.zeros_like(values)
    return jnp.concatenate(
        [jnp.where(lane < HP, values, zero), jnp.where(lane < HP, zero, values)], axis=0
    )


def ssm_fwd_kernel(
    heads, ends, skip, act, steps, rows, seg_c, seg_r, y_ref, st_ref, state, weighted
):
    step = pl.program_id(0)

    @pl.when(step == 0)
    def _():
        state[...] = jnp.zeros_like(state)

    before, end = ends[step], ends[step + 1]
    link = (before == end).astype(F32)
    _, _, same, run_c, run_r, keep, tail = decays(
        seg_c[...], seg_r[...], steps[:, 128:], rows[8:16, :], before, end
    )
    width = heads * HP
    b_in = act[:, width : width + NS]
    c_in = act[:, width + NS : width + 2 * NS]
    gram = nt(c_in, b_in)
    last = run_c[SPAN - 1 :, :]
    carry_w = jnp.exp(run_c) * keep
    end_w = jnp.exp(last - run_c) * tail * steps[:, :128]
    prior = state[...]
    st_ref[0] = prior
    from_state = nt(c_in, prior.astype(BF16))
    for group in head_groups(heads):
        size = len(group) * HP
        lanes = slice(group[0] * HP, group[0] * HP + size)
        x_in = act[:, lanes]
        x_wide = x_in.astype(F32)
        mixing = []
        for h in group:
            decay = jnp.where(same, jnp.exp(run_c[:, h : h + 1] - run_r[h : h + 1, :]), 0.0)
            mixing.append((gram * decay * rows[h : h + 1, :]).astype(BF16))
        y_in = nn(jnp.concatenate(mixing, axis=1), stacked(x_in, group))
        skips = [skip[h] for h in group]
        lane = lax.broadcasted_iota(jnp.int32, (1, size), 1)
        skip_w = jnp.where(lane < HP, skips[0], skips[-1])
        y_ref[:, lanes] = (
            y_in + from_state[:, lanes] * by_lane(carry_w, group, size) + skip_w * x_wide
        )
        weighted[:, lanes] = (x_wide * by_lane(end_w, group, size)).astype(BF16)
    local = tn(weighted[...], b_in)
    for h in range(heads):
        part = slice(h * HP, (h + 1) * HP)
        state[part, :] = (jnp.exp(last[:, h : h + 1]) * link) * prior[part, :] + local[part, :]


def ssm_bwd_kernel(
    heads,
    ends,
    skip,
    act,
    steps,
    rows,
    seg_c,
    seg_r,
    st_ref,
    z_ref,
    gym_ref,
    y_ref,
    stat_ref,
    gain_ref,
    pre_ref,
    cin_ref,
    up_ref,
    taps,
    params,
    first_ref,
    gconv_ref,
    gwide_ref,
    gstep_ref,
    gstate,
    gbuf,
    grow,
    carried,
    ended,
):
    step = pl.num_programs(0) - 1 - pl.program_id(0)
    width = heads * HP
    conv = width + 2 * NS

    @pl.when(pl.program_id(0) == 0)
    def _():
        gstate[...] = jnp.zeros_like(gstate)
        gbuf[...] = jnp.zeros_like(gbuf)
        grow[...] = jnp.zeros_like(grow)
        gconv_ref[...] = jnp.zeros_like(gconv_ref)
        gwide_ref[...] = jnp.zeros_like(gwide_ref)
        gstep_ref[...] = jnp.zeros_like(gstep_ref)

    before, end = ends[step], ends[step + 1]
    link = (before == end).astype(F32)
    row, col, same, run_c, run_r, keep, tail = decays(
        seg_c[...], seg_r[...], steps[:, 128:], rows[8:16, :], before, end
    )
    gate = z_ref[...]
    silu = gate * jax.nn.sigmoid(gate)
    gated = y_ref[...] * silu
    g_gated = stat_ref[:, 0:1] * (gym_ref[...] * gain_ref[...]) - gated * stat_ref[:, 1:2]
    g_all = g_gated * silu
    x_all = act[:, :width].astype(F32)
    gwide_ref[0:1, :] += jnp.sum(g_all * x_all, axis=0, keepdims=True)

    b_in = act[:, width : width + NS]
    c_in = act[:, width + NS : width + 2 * NS]
    gram = nt(c_in, b_in)
    last = run_c[SPAN - 1 :, :]
    carry_w = jnp.exp(run_c) * keep
    tail_w = jnp.exp(last - run_c) * tail
    end_w = tail_w * steps[:, :128]
    prior = st_ref[0]
    prior_low = prior.astype(BF16)
    after = gstate[...]
    after_low = after.astype(BF16)
    from_prior = nt(c_in, prior_low)
    from_after = nt(b_in, after_low)
    g_gram = jnp.zeros((SPAN, SPAN), F32)
    row_sums = jnp.zeros((SPAN, SPAN), F32)
    for group in head_groups(heads):
        size = len(group) * HP
        lanes = slice(group[0] * HP, group[0] * HP + size)
        gy = g_all[:, lanes]
        gy_parts = stacked(gy.astype(BF16), group)
        g_mixes = nt(gy_parts, act[:, lanes])
        mixing = []
        for i, h in enumerate(group):
            dt_row = rows[h : h + 1, :]
            decay = jnp.where(same, jnp.exp(run_c[:, h : h + 1] - run_r[h : h + 1, :]), 0.0)
            mixing.append((gram * decay * dt_row).astype(BF16))
            g_mix = g_mixes[i * SPAN : (i + 1) * SPAN, :] * decay
            g_gram_h = g_mix * dt_row
            g_gram = g_gram + g_gram_h
            sums = jnp.sum(g_gram_h * gram, axis=1, keepdims=True)
            row_sums = jnp.where(col == h, sums, row_sums)
            by_key = jnp.sum(g_mix * gram, axis=0, keepdims=True)
            grow[h : h + 1, :] = by_key * dt_row
            grow[128 + h : 128 + h + 1, :] = by_key
        skips = [skip[h] for h in group]
        lane = lax.broadcasted_iota(jnp.int32, (1, size), 1)
        skip_w = jnp.where(lane < HP, skips[0], skips[-1])
        end_l = by_lane(end_w, group, size)
        gbuf[0:SPAN, lanes] = (
            tn(jnp.concatenate(mixing, axis=0), gy_parts)
            + from_after[:, lanes] * end_l
            + skip_w * gy
        )
        carried[:, lanes] = (gy * by_lane(carry_w, group, size)).astype(BF16)
        ended[:, lanes] = (x_all[:, lanes] * end_l).astype(BF16)
    of_head = (
        lax.broadcasted_iota(jnp.int32, (width, 128), 0) // HP
        == lax.broadcasted_iota(jnp.int32, (width, 128), 1)
    ).astype(BF16)

    def head_sums(values):
        high = values.astype(BF16)
        return nn(high, of_head) + nn((values - high.astype(F32)).astype(BF16), of_head)

    g_carry = head_sums(g_all * from_prior)
    g_tail = head_sums(x_all * from_after)
    state_sums = jnp.sum(after * prior, axis=1, keepdims=True)
    of_head_t = (
        lax.broadcasted_iota(jnp.int32, (width, 128), 0) // HP
        == lax.broadcasted_iota(jnp.int32, (width, 128), 1)
    )
    state_sums = jnp.sum(jnp.where(of_head_t, state_sums, 0.0), axis=0, keepdims=True)
    g_end = g_tail * end_w
    g_link = jnp.exp(last) * link
    total_last = jnp.sum(g_end, axis=0, keepdims=True) + g_link * state_sums
    g_run = row_sums + g_carry * carry_w - g_end + jnp.where(row == SPAN - 1, total_last, 0.0)
    weighted = carried[...]
    g_gram_low = g_gram.astype(BF16)
    gbuf[0:SPAN, width : width + NS] = nn(ended[...], after_low) + tn(g_gram_low, c_in)
    gbuf[0:SPAN, width + NS :] = nn(weighted, prior_low) + nn(g_gram_low, b_in)
    to_state = tn(weighted, c_in)
    for h in range(heads):
        part = slice(h * HP, (h + 1) * HP)
        gstate[part, :] = g_link[:, h : h + 1] * after[part, :] + to_state[part, :]

    pre = pre_ref[...].astype(F32)
    sig = jax.nn.sigmoid(pre)
    g_pre = gbuf[0:SPAN, :] * (sig + pre * sig * (1.0 - sig))
    gbuf[0:SPAN, :] = g_pre
    cin = cin_ref[...].astype(F32)
    g_conv = taps[KW - 1 : KW, :] * g_pre
    gconv_ref[KW - 1 : KW, :] += jnp.sum(g_pre * cin, axis=0, keepdims=True)
    gconv_ref[KW : KW + 1, :] += jnp.sum(g_pre, axis=0, keepdims=True)
    for by in range(1, KW):
        ahead = gbuf[by : by + SPAN, :] * up_ref[:, by : by + 1]
        tap = KW - 1 - by
        g_conv = g_conv + taps[tap : tap + 1, :] * ahead
        gconv_ref[tap : tap + 1, :] += jnp.sum(ahead * cin, axis=0, keepdims=True)
    gbuf[SPAN : SPAN + 8, :] = gbuf[0:8, :]
    first_ref[:, :conv] = g_conv.astype(BF16)

    later = (col >= row).astype(F32)
    eye = (col == row).astype(F32)

    def across(left, right):
        return lax.dot_general(
            left, right, (((1,), (1,)), ((), ())), precision=HIGH, preferred_element_type=F32
        )

    g_loga = nn(later, g_run, HIGH) - across(later, grow[:128, :])
    g_dt = g_tail * tail_w + across(eye, grow[128:, :]) - g_loga * params[1:2, :]
    g_step = g_dt * (1.0 - jnp.exp(-steps[:, :128]))
    first_ref[:, conv:] = g_step.astype(BF16)
    gstep_ref[0:1, :] += jnp.sum(g_step, axis=0, keepdims=True)
    gstep_ref[1:2, :] += jnp.sum(g_loga * steps[:, 128:], axis=0, keepdims=True)


def ssm_specs(heads, at):
    width = heads * HP
    return [
        pl.BlockSpec(memory_space=pltpu.SMEM),
        pl.BlockSpec(memory_space=pltpu.SMEM),
        pl.BlockSpec((SPAN, width + 2 * NS), lambda i: (at(i), 0)),
        pl.BlockSpec((SPAN, 256), lambda i: (at(i), 0)),
        pl.BlockSpec((16, SPAN), lambda i: (0, at(i))),
        pl.BlockSpec((SPAN, 1), lambda i: (at(i), 0)),
        pl.BlockSpec((1, SPAN), lambda i: (0, at(i))),
    ]


def ssm_forward(heads, inputs):
    length = inputs[2].shape[0]
    steps = length // SPAN
    width = heads * HP
    return pl.pallas_call(
        functools.partial(ssm_fwd_kernel, heads),
        grid=(steps,),
        in_specs=ssm_specs(heads, lambda i: i),
        out_specs=[
            pl.BlockSpec((SPAN, width), lambda i: (i, 0)),
            pl.BlockSpec((1, width, NS), lambda i: (i, 0, 0)),
        ],
        out_shape=[
            jax.ShapeDtypeStruct((length, width), F32),
            jax.ShapeDtypeStruct((steps, width, NS), F32),
        ],
        scratch_shapes=[pltpu.VMEM((width, NS), F32), pltpu.VMEM((SPAN, width), BF16)],
        compiler_params=pltpu.CompilerParams(vmem_limit_bytes=32 * 1024 * 1024),
        cost_estimate=pl.CostEstimate(
            flops=10**9, bytes_accessed=4 * 10**7, transcendentals=10**6
        ),
        name="ssm_forward",
    )(*inputs)


def ssm_backward(heads, inputs, states, gate_z, g_ym, ssm_y, stats, gain, pre, cin, up, taps, params):
    length = inputs[2].shape[0]
    steps = length // SPAN
    width = heads * HP
    conv = width + 2 * NS
    total = conv + 128

    def at(i):
        return steps - 1 - i

    def part(size):
        return pl.BlockSpec((SPAN, size), lambda i: (at(i), 0))

    def fixed(shape):
        return pl.BlockSpec(shape, lambda i: (0, 0))

    return pl.pallas_call(
        functools.partial(ssm_bwd_kernel, heads),
        grid=(steps,),
        in_specs=ssm_specs(heads, at)
        + [
            pl.BlockSpec((1, width, NS), lambda i: (at(i), 0, 0)),
            part(width),
            part(width),
            part(width),
            part(stats.shape[1]),
            fixed(gain.shape),
            part(conv),
            part(conv),
            part(up.shape[1]),
            fixed(taps.shape),
            fixed(params.shape),
        ],
        out_specs=[part(total), fixed((8, conv)), fixed((8, width)), fixed((8, 128))],
        out_shape=[
            jax.ShapeDtypeStruct((length, total), BF16),
            jax.ShapeDtypeStruct((8, conv), F32),
            jax.ShapeDtypeStruct((8, width), F32),
            jax.ShapeDtypeStruct((8, 128), F32),
        ],
        scratch_shapes=[
            pltpu.VMEM((width, NS), F32),
            pltpu.VMEM((SPAN + 8, conv), F32),
            pltpu.VMEM((256, SPAN), F32),
            pltpu.VMEM((SPAN, width), BF16),
            pltpu.VMEM((SPAN, width), BF16),
        ],
        compiler_params=pltpu.CompilerParams(vmem_limit_bytes=56 * 1024 * 1024),
        cost_estimate=pl.CostEstimate(
            flops=10**7, bytes_accessed=10**6, transcendentals=10**4
        ),
        name="ssm_backward",
    )(*inputs, states, gate_z, g_ym, ssm_y, stats, gain, pre, cin, up, taps, params)


def allowed_keys(index, reach, seg_c, seg_r):
    row = lax.broadcasted_iota(jnp.int32, (QBLK, reach), 0) + index * QBLK
    col = lax.broadcasted_iota(jnp.int32, (QBLK, reach), 1)
    return (seg_c[...] == seg_r[:, :reach]) & (col <= row)


def attn_fwd_kernel(heads, blocks, qkv_ref, seg_c, seg_r, out_ref, lse_ref):
    wide = heads * HD
    for index in range(blocks):

        @pl.when(pl.program_id(0) == index)
        def _(index=index):
            reach = (index + 1) * QBLK
            allowed = allowed_keys(index, reach, seg_c, seg_r)
            own = slice(index * QBLK, reach)
            keys = qkv_ref[:reach, wide : wide + HD]
            values = qkv_ref[:reach, wide + HD : wide + 2 * HD]
            for h in range(heads):
                lanes = slice(h * HD, (h + 1) * HD)
                scores = nt(qkv_ref[own, lanes], keys) * (HD**-0.5)
                scores = jnp.where(allowed, scores, MASKED)
                top = jnp.max(scores, axis=1, keepdims=True)
                expo = jnp.exp(scores - top)
                total = jnp.sum(expo, axis=1, keepdims=True)
                probs = (expo * (1.0 / total)).astype(BF16)
                out_ref[:, lanes] = nn(probs, values).astype(BF16)
                lse_ref[:, h : h + 1] = top + jnp.log(total)


def attn_bwd_kernel(
    heads, blocks, qkv_ref, seg_c, seg_r, lse_ref, go_ref, cosine, sine, out_ref, grads
):
    wide = heads * HD

    @pl.when(pl.program_id(0) == 0)
    def _():
        grads[...] = jnp.zeros_like(grads)

    for index in range(blocks):

        @pl.when(pl.program_id(0) == index)
        def _(index=index):
            reach = (index + 1) * QBLK
            allowed = allowed_keys(index, reach, seg_c, seg_r)
            own = slice(index * QBLK, reach)
            keys = qkv_ref[:reach, wide : wide + HD]
            values = qkv_ref[:reach, wide + HD : wide + 2 * HD]
            for h in range(heads):
                lanes = slice(h * HD, (h + 1) * HD)
                query = qkv_ref[own, lanes]
                g_out = go_ref[:, lanes]
                scores = nt(query, keys) * (HD**-0.5)
                probs = jnp.where(allowed, jnp.exp(scores - lse_ref[:, h : h + 1]), 0.0)
                g_probs = nt(g_out, values)
                delta = jnp.sum(probs * g_probs, axis=1, keepdims=True)
                g_scores = (probs * (g_probs - delta)).astype(BF16)
                grads[own, lanes] = nn(g_scores, keys) * (HD**-0.5)
                grads[:reach, wide : wide + HD] += tn(g_scores, query) * (HD**-0.5)
                grads[:reach, wide + HD : wide + 2 * HD] += tn(probs.astype(BF16), g_out)
            if index == blocks - 1:
                for b in range(blocks):
                    part = slice(b * QBLK, (b + 1) * QBLK)
                    slab = grads[part, :]
                    out_ref[part, :] = (
                        slab * cosine[part, :] - swap_halves(slab) * sine[part, :]
                    ).astype(BF16)


def attn_specs(length, slab):
    return [
        pl.BlockSpec((length, slab), lambda i: (0, 0)),
        pl.BlockSpec((QBLK, 1), lambda i: (i, 0)),
        pl.BlockSpec((1, length), lambda i: (0, 0)),
    ]


def attn_forward(heads, inputs):
    length, slab = inputs[0].shape
    blocks = length // QBLK
    return pl.pallas_call(
        functools.partial(attn_fwd_kernel, heads, blocks),
        grid=(blocks,),
        in_specs=attn_specs(length, slab),
        out_specs=[
            pl.BlockSpec((QBLK, heads * HD), lambda i: (i, 0)),
            pl.BlockSpec((QBLK, heads), lambda i: (i, 0)),
        ],
        out_shape=[
            jax.ShapeDtypeStruct((length, heads * HD), BF16),
            jax.ShapeDtypeStruct((length, heads), F32),
        ],
        compiler_params=pltpu.CompilerParams(vmem_limit_bytes=32 * 1024 * 1024),
        cost_estimate=pl.CostEstimate(
            flops=10**9, bytes_accessed=2 * 10**7, transcendentals=10**6
        ),
        name="attn_forward",
    )(*inputs)


def attn_backward(heads, inputs, lse, g_out, cosine, sine):
    length, slab = inputs[0].shape
    blocks = length // QBLK
    full = pl.BlockSpec((length, slab), lambda i: (0, 0))
    return pl.pallas_call(
        functools.partial(attn_bwd_kernel, heads, blocks),
        grid=(blocks,),
        in_specs=attn_specs(length, slab)
        + [
            pl.BlockSpec((QBLK, heads), lambda i: (i, 0)),
            pl.BlockSpec((QBLK, heads * HD), lambda i: (i, 0)),
            full,
            full,
        ],
        out_specs=full,
        out_shape=jax.ShapeDtypeStruct((length, slab), BF16),
        scratch_shapes=[pltpu.VMEM((length, slab), F32)],
        compiler_params=pltpu.CompilerParams(vmem_limit_bytes=56 * 1024 * 1024),
        cost_estimate=pl.CostEstimate(
            flops=10**7, bytes_accessed=10**6, transcendentals=10**4
        ),
        name="attn_backward",
    )(*inputs, lse, g_out, cosine, sine)


def ff_kernel(both, product, g_gate, g_up, gb, out):
    rows = both.shape[1]
    out[0, :rows] = tn(both[...], g_gate[...]).astype(BF16)
    out[0, rows : 2 * rows] = tn(both[...], g_up[...]).astype(BF16)
    out[0, 2 * rows :] = tn(product[...], gb[...]).astype(BF16)


def ff_gradients(m, both, product, g_gate, g_up, gb):
    tokens, dim = both.shape
    rows, down = dim // m, product.shape[1] // m
    full = pl.BlockSpec((tokens, dim), lambda i: (0, 0))
    return pl.pallas_call(
        ff_kernel,
        grid=(m,),
        in_specs=[
            pl.BlockSpec((tokens, rows), lambda i: (0, i)),
            pl.BlockSpec((tokens, down), lambda i: (0, i)),
            full,
            full,
            full,
        ],
        out_specs=pl.BlockSpec((1, 2 * rows + down, dim), lambda i: (i, 0, 0)),
        out_shape=jax.ShapeDtypeStruct((m, 2 * rows + down, dim), BF16),
        compiler_params=pltpu.CompilerParams(vmem_limit_bytes=40 * 1024 * 1024),
        cost_estimate=pl.CostEstimate(
            flops=6 * tokens * dim * dim, bytes_accessed=10**7, transcendentals=0
        ),
        name="ff_gradients",
    )(both, product, g_gate, g_up, gb)


def row_totals(values):
    ones = jnp.ones((8, values.shape[1]), F32)
    return lax.dot_general(
        ones, values, (((1,), (1,)), ((), ())), precision=HIGH, preferred_element_type=F32
    )


def finish_ff_kernel(core, own, mate, w_gate, w_up, gain, gate_ref, up_ref, down_ref, gain_ref):
    rows = w_gate.shape[0]
    tiles = own.shape[1] // 128
    total = jnp.zeros((rows, 128), F32)
    for half in range(2):
        mine = core[0] == half

        def pick(low, high, lanes, mine=mine):
            return jnp.where(mine, own[low:high, lanes], mate[low:high, lanes]).astype(F32)

        for f in range(tiles):
            lanes = slice(f * 128, (f + 1) * 128)
            to = slice((2 * f + half) * 128, (2 * f + half + 1) * 128)
            gate_ref[:, to] = pick(0, rows, lanes)
            up_ref[:, to] = pick(rows, 2 * rows, lanes)
        down = down_ref.shape[0] // 2
        down_ref[half * down : (half + 1) * down, :] = pick(2 * rows, 2 * rows + down, slice(None))
    for t in range(2 * tiles):
        lanes = slice(t * 128, (t + 1) * 128)
        total = total + gate_ref[:, lanes] * w_gate[:, lanes].astype(F32)
        total = total + up_ref[:, lanes] * w_up[:, lanes].astype(F32)
    gain_ref[...] = row_totals(total) / gain[...]


def finish_ff(core, own, mate, w_gate, w_up, gain):
    shard, ff = w_gate.shape
    down = own.shape[0] - 2 * shard
    vmem = pl.BlockSpec(memory_space=pltpu.VMEM)
    out = pl.pallas_call(
        finish_ff_kernel,
        in_specs=[pl.BlockSpec(memory_space=pltpu.SMEM)] + [vmem] * 5,
        out_specs=[vmem] * 4,
        out_shape=[
            jax.ShapeDtypeStruct((shard, ff), F32),
            jax.ShapeDtypeStruct((shard, ff), F32),
            jax.ShapeDtypeStruct((2 * down, own.shape[1]), F32),
            jax.ShapeDtypeStruct((8, shard), F32),
        ],
        compiler_params=pltpu.CompilerParams(vmem_limit_bytes=40 * 1024 * 1024),
        name="finish_ff",
    )(core.astype(jnp.int32)[None], own, mate, w_gate, w_up, gain.astype(F32)[None])
    return out[0], out[1], out[2], out[3][0]


def finish_kernel(
    got,
    w_in,
    w_qkv,
    w_out,
    gain_in,
    gain_m,
    in_ref,
    qkv_ref,
    out_ref,
    o_ref,
    gain_in_ref,
    gain_m_ref,
    small_ref,
    steps,
):
    count = got.shape[0]
    shard = w_qkv.shape[0]
    heads = MH // count
    width = heads * HP
    conv = width + 2 * NS
    late = conv + 128
    q_width = QH * HD // count
    wide = count * width
    steps[...] = jnp.zeros_like(steps)
    shared = jnp.zeros((shard, 2 * NS), F32)
    gain = jnp.zeros((1, shard), F32)
    small = jnp.zeros((shard, 128), F32)
    pairs = []

    def lay(at, values, gain):
        flat = jnp.transpose(values)
        rows = slice(at, at + flat.shape[0])
        in_ref[rows, :] = flat
        return gain + jnp.sum(flat * w_in[rows, :].astype(F32), axis=0, keepdims=True)

    for j in range(count):

        def part(low, high, j=j):
            return got[j, :shard, low:high].astype(F32)

        gain = lay(j * width, part(late, late + width), gain)
        gain = lay(wide + j * width, part(0, width), gain)
        shared = shared + part(width, conv)
        steps[:, j * heads : (j + 1) * heads] = part(conv, conv + heads)
        at = late + width
        qkv_ref[:, j * q_width : (j + 1) * q_width] = part(at, at + q_width)
        pairs.append(part(at + q_width, at + q_width + 128))
        at = at + q_width + 128
        rows = got[j, : shard // 2, at:], got[j, shard // 2 :, at:]
        rows = jnp.concatenate(rows, axis=1).astype(F32)
        low = j * (shard // 2)
        if low < out_ref.shape[0]:
            out_ref[low : low + shard // 2, :] = rows
        else:
            low -= out_ref.shape[0]
            o_ref[low : low + shard // 2, :] = rows
        small = small + part(conv, late)
    gain = lay(2 * wide, shared, gain)
    at = 2 * wide + 2 * NS
    flat = jnp.transpose(steps[...])[: in_ref.shape[0] - at, :]
    in_ref[at:, :] = flat
    gain = gain + jnp.sum(flat * w_in[at:, :].astype(F32), axis=0, keepdims=True)
    one, two = pairs[0] + pairs[1], pairs[2] + pairs[3]
    low = lax.broadcasted_iota(jnp.int32, one.shape, 1) < HD
    at = QH * HD
    qkv_ref[:, at : at + 128] = jnp.where(low, one, pltpu.roll(two, HD, 1))
    qkv_ref[:, at + 128 :] = jnp.where(low, pltpu.roll(one, HD, 1), two)
    gain = row_totals(qkv_ref[...] * w_qkv[...].astype(F32)) + gain
    gain_in_ref[...] = gain / gain_in[...]
    gain_m_ref[...] = row_totals(out_ref[...] * w_out[...].astype(F32)) / gain_m[...]
    small_ref[...] = jnp.transpose(small)


def finish(got, w_in, w_qkv, w_out, w_o, gain_in, gain_m):
    shard = w_qkv.shape[0]
    vmem = pl.BlockSpec(memory_space=pltpu.VMEM)
    shapes = [w_in.shape[::-1], w_qkv.shape, w_out.shape, w_o.shape]
    shapes += [(8, shard), (8, w_out.shape[0]), (128, shard)]
    out = pl.pallas_call(
        finish_kernel,
        in_specs=[vmem] * 6,
        out_specs=[vmem] * 7,
        out_shape=[jax.ShapeDtypeStruct(shape, F32) for shape in shapes],
        scratch_shapes=[pltpu.VMEM((shard, 128), F32)],
        compiler_params=pltpu.CompilerParams(vmem_limit_bytes=40 * 1024 * 1024),
        name="finish",
    )(got, w_in.T, w_qkv, w_out, gain_in.astype(F32)[None], gain_m.astype(F32)[None])
    return out[0].T, out[1], out[2], out[3], out[4][0], out[5][0], out[6]


def tie(value, *after):
    return lax.optimization_barrier((value,) + after)[0]


def stage(compute, inputs, sends):
    inputs, operands = lax.optimization_barrier((inputs, [operand for _, operand in sends]))
    got = [send(operand) for (send, _), operand in zip(sends, operands)]
    return lax.optimization_barrier((compute(*inputs), got))


class Net:
    def __init__(self):
        self.n = lax.axis_size("ctx")
        self.m = lax.axis_size("fsdp")
        self.c = lax.axis_index("ctx")
        self.f = lax.axis_index("fsdp")
        self.direct = self.n == 4 and self.m == 8
        self.x, self.core = self.c // 2, self.c % 2
        self.z, self.y = self.f // 2, self.f % 2
        self.by_core = [[i * 2 + k for i in range(self.n // 2)] for k in range(2)]

    def flip(self, value, axis, bit):
        size = lax.axis_size(axis)
        return lax.ppermute(value, axis, [(i, i ^ bit) for i in range(size)])

    def shift_z(self, value, by):
        return lax.ppermute(value, "fsdp", [(i, (i + 2 * by) % self.m) for i in range(self.m)])

    def cross(self, value):
        pairs = [
            (c * 8 + z * 2 + y, z * 8 + c * 2 + y)
            for c in range(4)
            for z in range(4)
            for y in range(2)
        ]
        return lax.ppermute(value, ("ctx", "fsdp"), pairs)

    def along_z(self, block):
        return [block] + [self.shift_z(block, k) for k in range(1, 4)]

    def along_y(self, pieces):
        return [self.flip(piece, "fsdp", 1) for piece in pieces]

    def in_order(self, own, mate, columns=None):
        places = [2 * ((self.z - k) % 4) + (self.y ^ o) for o in range(2) for k in range(4)]
        return put(own + mate, places, columns)

    def flip_y(self, value):
        return self.flip(value, "fsdp", 1)

    def flip_x(self, value):
        return self.flip(value, "ctx", 2)

    def flip_core(self, value):
        return self.flip(value, "ctx", 1)

    def halves_y(self, sums):
        low = sums.astype(BF16)
        low = low.reshape((4, 2) + low.shape[1:])
        away = lax.dynamic_index_in_dim(low, 1 - self.y, 1, False)
        return lax.dynamic_index_in_dim(low, self.y, 1, False), away

    def shifts_z(self, both):
        sent = [lax.dynamic_index_in_dim(both, (self.z + k) % 4, 0, False) for k in range(4)]
        return [sent[0]] + [self.shift_z(sent[k], k) for k in range(1, 4)]

    def collect(self, sums):
        return lax.psum_scatter(sums.astype(BF16), "fsdp", scatter_dimension=0, tiled=False)

    def ctx_all(self, value):
        if not self.direct:
            return lax.all_gather(value, "ctx", axis=0, tiled=False)
        pair = jnp.stack([value, self.flip(value, "ctx", 2)])
        mates = self.flip(pair, "ctx", 1)
        return put([pair, mates], [self.c, self.c ^ 2, self.c ^ 1, self.c ^ 3])

    def ctx_sum(self, value):
        if not self.direct:
            return lax.psum(value, "ctx")
        value = value + self.flip(value, "ctx", 1)
        return value + self.flip(value, "ctx", 2)

    def ctx_collect(self, parts):
        if not self.direct:
            low = lax.psum_scatter(parts.astype(BF16), "ctx", scatter_dimension=0, tiled=False)
            return low.astype(F32)
        pairs = parts.reshape((2, 2) + parts.shape[1:])
        away = lax.dynamic_index_in_dim(pairs, 1 - self.core, 1, False).astype(BF16)
        here = lax.dynamic_index_in_dim(pairs, self.core, 1, False)
        got = self.flip(away, "ctx", 1)

        def half(which):
            return lax.dynamic_index_in_dim(here, which, 0, False).astype(
                F32
            ) + lax.dynamic_index_in_dim(got, which, 0, False).astype(F32)

        across = self.flip(half(1 - self.x).astype(BF16), "ctx", 2)
        return half(self.x) + across.astype(F32)

    def over_cores(self, value):
        value = lax.psum(value, "ctx", axis_index_groups=self.by_core)
        return lax.all_gather(value, "ctx", axis=0)[:2].astype(F32)

    def rows_out(self, shard):
        per = self.m // self.n
        got = lax.all_gather(shard, "fsdp", axis=0, tiled=False)
        return lax.dynamic_slice_in_dim(got, self.c * per, per, 0)

    def rows_back(self, sums):
        wide = jnp.zeros((self.m,) + sums.shape[1:], BF16)
        wide = lax.dynamic_update_slice_in_dim(
            wide, sums.astype(BF16), self.c * (self.m // self.n), 0
        )
        out = lax.psum_scatter(wide, "fsdp", scatter_dimension=0, tiled=False)
        return lax.psum(out, "ctx")


def put_kernel(counts, cuts, places, *refs):
    parts, outs = refs[: len(counts)], refs[len(counts) :]
    start = 0
    for part, count in zip(parts, counts):

        @pl.when((pl.program_id(0) >= start) & (pl.program_id(0) < start + count))
        def _(part=part):
            for out, low, high in zip(outs, cuts[:-1], cuts[1:]):
                out[...] = part[..., low:high]

        start += count


def put(parts, places, columns=None):
    counts = [part.shape[0] for part in parts]
    total = sum(counts)
    shape = parts[0].shape[1:]
    zeros = (0,) * len(shape)
    sizes = columns or [shape[-1]]
    cuts = [0]
    for size in sizes:
        cuts.append(cuts[-1] + size)
    places = jnp.stack([jnp.asarray(p, jnp.int32) for p in places])
    size = parts[0][0].size * parts[0].dtype.itemsize
    specs = []
    for p in range(len(parts)):
        start = sum(counts[:p])

        def at(i, at, start=start, last=counts[p] - 1):
            return (jnp.clip(i - start, 0, last),) + zeros

        specs.append(pl.BlockSpec((1,) + shape, at))
    out = pl.pallas_call(
        functools.partial(put_kernel, counts, cuts),
        grid_spec=pltpu.PrefetchScalarGridSpec(
            num_scalar_prefetch=1,
            grid=(total,),
            in_specs=specs,
            out_specs=[
                pl.BlockSpec((1,) + shape[:-1] + (w,), lambda i, at: (at[i],) + zeros)
                for w in sizes
            ],
        ),
        out_shape=[
            jax.ShapeDtypeStruct((total,) + shape[:-1] + (w,), parts[0].dtype) for w in sizes
        ],
        compiler_params=pltpu.CompilerParams(vmem_limit_bytes=40 * 1024 * 1024),
        cost_estimate=pl.CostEstimate(
            flops=0, bytes_accessed=2 * total * size, transcendentals=0
        ),
        name="put",
    )(places, *parts)
    return out if columns else out[0]


def rms_scale(values):
    return lax.rsqrt(jnp.mean(values * values, axis=-1, keepdims=True) + EPSILON)


def rms_back(values, gain, scale, grad):
    scaled = grad * gain
    inner = jnp.mean(values * scaled, axis=-1, keepdims=True)
    return scale * scaled - values * (scale * scale * scale * inner)


def columns_of(w, start, size):
    return lax.dynamic_slice_in_dim(w, start, size, 1)


def rotary_tables(length, q_heads, slab):
    half = HD // 2
    freq = (ROPE_BASE ** (-(np.arange(half) * 2.0 / HD))).astype(np.float32)
    angle = np.arange(length, dtype=np.float32)[:, None] * freq[None, :]
    one = np.concatenate([np.cos(angle), np.cos(angle)], axis=1)
    two = np.concatenate([-np.sin(angle), np.sin(angle)], axis=1)
    room = slab - (q_heads + 1) * HD
    cosine = np.concatenate([one] * (q_heads + 1) + [np.ones((length, room))], axis=1)
    sine = np.concatenate([two] * (q_heads + 1) + [np.zeros((length, room))], axis=1)
    return jnp.asarray(cosine, F32), jnp.asarray(sine, F32)


def per_device(
    tokens,
    teacher,
    segment_ids,
    valid_mask,
    gain_in,
    w_in,
    conv_w,
    conv_b,
    dt_bias,
    a_log,
    d_skip,
    gain_m,
    w_out,
    w_qkv,
    w_o,
    gain_ffn,
    w_gate,
    w_up,
    w_down,
):
    net = Net()
    n, m, c, f = net.n, net.m, net.c, net.f
    rows, dim = tokens.shape[1:]
    length = segment_ids.shape[1]
    shard = w_in.shape[0]
    wide = MH * HP
    conv_full = wide + 2 * NS
    heads = MH // n
    q_heads = QH // n
    width = heads * HP
    conv_width = width + 2 * NS
    q_width = q_heads * HD
    slab = q_width + 2 * HD
    slab += -slab % 128
    group = QH // KVH
    kv_at = (c * q_heads) // group
    ff = w_gate.shape[1]
    ff_shard = w_down.shape[0]
    per = m // n
    seg = segment_ids[0]
    seg_c, seg_r = seg[:, None], seg[None, :]
    ends = jnp.concatenate([jnp.full((1,), -1, jnp.int32), seg[SPAN - 1 :: SPAN]])
    valid = valid_mask[0].astype(F32)

    def lay(values):
        values = values.reshape((-1, values.shape[-1]))
        room = -values.shape[1] % 128
        return jnp.pad(values, ((0, 0), (0, room))).reshape(-1, 128)

    def unlay(small, start, lead, size):
        room = size + -size % 128
        count = lead * room // 128
        return small[..., start : start + count, :].reshape(small.shape[:-2] + (lead, room))[
            ..., :size
        ]

    shapes = [(1, shard), (1, shard), (1, w_out.shape[0]), (1, conv_b.shape[0])]
    shapes += [(KW, conv_b.shape[0])]
    starts = [0]
    for lead, size in shapes:
        starts.append(starts[-1] + lead * (size + -size % 128) // 128)
    laid = [lay(p) for p in (gain_in[None], gain_ffn[None], gain_m[None], conv_b[None], conv_w)]
    laid.append(jnp.full((1, 128), jnp.sum(valid), F32).astype(BF16))
    laid.append(jnp.zeros((-(starts[-1] + 1) % 16, 128), BF16))
    at_small = 64
    packed = jnp.concatenate(laid, axis=0)
    first = jnp.concatenate(
        [
            columns_of(w_in, wide + c * width, width),
            w_in[:, 2 * wide : 2 * wide + 2 * NS],
            columns_of(w_in, wide + conv_full + c * heads, heads),
            jnp.zeros((shard, at_small - heads), BF16),
            packed.T if net.direct else jnp.zeros((shard, packed.shape[0]), BF16),
            jnp.zeros((shard, 128 - at_small - packed.shape[0]), BF16),
        ],
        axis=1,
    )
    second = jnp.concatenate(
        [
            columns_of(w_in, c * width, width),
            columns_of(w_qkv, c * q_width, q_width),
            columns_of(w_qkv, QH * HD + kv_at * HD, HD),
            columns_of(w_qkv, (QH + KVH) * HD + kv_at * HD, HD),
            jnp.zeros((shard, slab - q_width - 2 * HD), BF16),
        ],
        axis=1,
    )
    both_out = jnp.concatenate([w_out, w_o], axis=0)
    out_rows, mamba_rows = both_out.shape[0], w_out.shape[0]
    ff_half = ff_shard // 2
    size = m * ff_half

    def ff_cut(w):
        w = w.reshape(shard, m, 2, ff_half)
        return lax.dynamic_index_in_dim(w, net.core, 2, False).reshape(shard, size)

    places_x = n // 2

    def quarter_x(w):
        size = w.shape[0] // places_x
        return lax.dynamic_slice_in_dim(w, net.x * size, size, 0)

    w_ff = jnp.concatenate(
        [
            quarter_x(ff_cut(w_gate).reshape(-1, dim)),
            quarter_x(ff_cut(w_up).reshape(-1, dim)),
            quarter_x(lax.dynamic_slice_in_dim(w_down, net.core * ff_half, ff_half, 0)),
        ],
        axis=0,
    )
    groups = [[d * m + i for d in net.by_core[k] for i in range(m)] for k in range(2)]
    w_ff = lax.all_gather(
        w_ff, ("ctx", "fsdp"), axis=0, tiled=False, axis_index_groups=groups
    ).reshape((places_x, m) + w_ff.shape)
    if net.direct:
        both_cols = jnp.concatenate([first, second], axis=1)
        pair = jnp.stack([tokens[0], net.flip_x(tokens[0])])
        near = net.along_z(both_cols)
        far = net.along_y([tie(near[0], pair)] + near[1:])
        w_first, w_second = net.in_order(
            [p[None] for p in near],
            [p[None] for p in far],
            [first.shape[1], second.shape[1]],
        )
        at = conv_width + at_small
        small = jnp.swapaxes(w_first[:, :, at : at + packed.shape[0]], 1, 2)
        all_tokens = put([pair, net.flip_core(pair)], [c, c ^ 2, c ^ 1, c ^ 3])
        crossed = net.cross(tie(both_out, *near[1:]))
    else:
        small = lax.all_gather(packed, "fsdp", axis=0, tiled=False)
        w_first = lax.all_gather(first, "fsdp", axis=0, tiled=False)
        w_second = lax.all_gather(second, "fsdp", axis=0, tiled=False)
        w_outs = net.rows_out(both_out)
        all_tokens = net.ctx_all(tokens[0])
    all_tokens = all_tokens.reshape(length, dim)
    w_first = w_first.reshape(dim, first.shape[1])
    cuts = [
        jnp.transpose(unlay(small, start, *shape), (1, 0, 2)).reshape(shape[0], -1)
        for start, shape in zip(starts, shapes)
    ]
    gain_input = cuts[0].astype(F32)
    gain_second = cuts[1].astype(F32)
    gain_mamba = lax.dynamic_slice_in_dim(cuts[2], c * width, width, 1).astype(F32)
    count_ctx = jnp.sum(small[:, starts[-1], 0].astype(F32))

    def conv_cut(values):
        own = lax.dynamic_slice_in_dim(values, c * width, width, 1)
        return jnp.concatenate([own, values[:, wide:]], axis=1).astype(F32)

    bias, taps = conv_cut(cuts[3]), conv_cut(cuts[4])
    rate = jnp.exp(a_log)
    params = jnp.stack(
        [lax.dynamic_slice_in_dim(v, c * heads, heads) for v in (dt_bias, rate)]
    )
    params = jnp.pad(params, ((0, 6), (0, 128 - heads)))
    skip = lax.dynamic_slice_in_dim(d_skip, c * heads, heads)

    def shifted(by):
        return jnp.concatenate([jnp.full((by,), -1, jnp.int32), seg[: length - by]]) == seg

    same = jnp.stack([shifted(by) for by in range(KW)], axis=1).astype(F32)
    up = jnp.stack(
        [
            jnp.concatenate([seg[by:], jnp.full((by,), -1, jnp.int32)]) == seg
            for by in range(KW)
        ],
        axis=1,
    ).astype(F32)
    cosine, sine = rotary_tables(length, q_heads, slab)
    conv_args = (all_tokens, gain_input, w_first, taps, bias, same, params)

    def square_rows(square):
        return jnp.concatenate([square[0].reshape(-1, 128), jnp.full((8, 128), count_ctx)])

    def ssm(act, steps, step_rows):
        return ssm_forward(heads, (ends, skip, act, steps, step_rows, seg_c, seg_r))

    def attend(qkv):
        return attn_forward(q_heads, (qkv, seg_c, seg_r))

    w_second = w_second.reshape(dim, second.shape[1])
    if net.direct:
        normed, cin, pre, act, steps, step_rows = project_conv(*conv_args)
        ssm_y, states = ssm(act, steps, step_rows)
        gate_z, qkv, square = project_gate(normed, w_second, ssm_y, cosine, sine)
        mated = net.flip_y(tie(crossed, ssm_y))
        (attended, lse), (square,) = stage(
            attend, (qkv,), [(net.ctx_sum, square_rows(square))]
        )
        w_outs = jnp.where(
            net.y == 0, jnp.stack([crossed, mated]), jnp.stack([mated, crossed])
        )
    else:
        normed, cin, pre, act, steps, step_rows = project_conv(*conv_args)
        ssm_y, states = ssm(act, steps, step_rows)
        gate_z, qkv, square = project_gate(normed, w_second, ssm_y, cosine, sine)
        square = net.ctx_sum(square_rows(square))
        attended, lse = attend(qkv)
    w_mamba = w_outs[:, :mamba_rows].reshape(per * mamba_rows, dim)
    w_attn = w_outs[:, mamba_rows:].reshape(per * (out_rows - mamba_rows), dim)
    ssm_in = (ends, skip, act, steps, step_rows, seg_c, seg_r)
    count = square[-1, 0]
    scale_m = lax.rsqrt(square[:-8].reshape(length, 1) / wide + EPSILON)
    gated = ssm_y * (gate_z * jax.nn.sigmoid(gate_z))
    ym = (gated * scale_m * gain_mamba).astype(BF16)
    outs = nn(ym, w_mamba) + nn(attended, w_attn)
    mixed = tokens[0].astype(F32) + net.ctx_collect(outs.reshape(n, rows, dim))

    ff_rows = shard * size // dim
    part_rows = ff_rows // places_x

    def ff_part(low, high, columns):
        return jnp.swapaxes(w_ff[:, :, low:high], 0, 1).reshape(-1, columns)

    w_g = ff_part(0, part_rows, size)
    w_u = ff_part(part_rows, 2 * part_rows, size)
    w_d = ff_part(2 * part_rows, w_ff.shape[2], dim)
    scale2 = rms_scale(mixed)
    normed2 = (mixed * scale2 * gain_second).astype(BF16)
    mate = [(i, i ^ 1) for i in range(n)]
    both = jnp.concatenate([normed2, lax.ppermute(normed2, "ctx", mate)], axis=0)
    gate_v, up_v = nn(both, w_g), nn(both, w_u)
    sig = jax.nn.sigmoid(gate_v)
    product = (gate_v * sig * up_v).astype(BF16)
    down_out = nn(product, w_d)
    from_mate = lax.ppermute(down_out[rows:].astype(BF16), "ctx", mate)
    layer_out = mixed + down_out[:rows] + from_mate.astype(F32)
    diff = layer_out - teacher[0].astype(F32)
    squared = jnp.sum(valid[:, None] * diff * diff)
    token_total = length * m * tokens.shape[0]
    grad_out = token_total * valid[:, None] * diff / count

    gb = grad_out.astype(BF16)
    gb_both = jnp.concatenate([gb, lax.ppermute(gb, "ctx", mate)], axis=0)
    g_prod = nt(gb_both, w_d)
    g_gate = (g_prod * up_v * (sig * (1.0 + gate_v * (1.0 - sig)))).astype(BF16)
    g_up = (g_prod * gate_v * sig).astype(BF16)
    if net.direct:
        g_ff = ff_gradients(m, both, product, g_gate, g_up, gb_both)
    else:
        g_ff = jnp.concatenate(
            [
                tn(both, g_gate).reshape(m, ff_rows, dim),
                tn(both, g_up).reshape(m, ff_rows, dim),
                tn(product, gb_both).reshape(m, ff_half, dim),
            ],
            axis=1,
        ).astype(BF16)
    g_n2 = nt(tie(g_gate, g_ff), w_g) + nt(g_up, w_u)
    from_mate = lax.ppermute(g_n2[rows:].astype(BF16), "ctx", mate)
    grad_n2 = g_n2[:rows] + from_mate.astype(F32)
    part = rms_back(mixed, gain_second, scale2, grad_n2)
    grad_mixed = grad_out + part

    gm = net.ctx_all(grad_mixed.astype(BF16))
    gm = gm.reshape(length, dim)
    g_ff = lax.psum_scatter(g_ff, "fsdp", scatter_dimension=0, tiled=False)

    g_ym = nt(gm, w_mamba)
    inner = jnp.sum(gated * (g_ym * gain_mamba), axis=1).reshape(-1, 128)

    def outs_back(gm):
        g_ob = nt(gm, w_attn).astype(BF16)
        g_outs = jnp.concatenate(
            [
                tn(ym, gm).reshape(per, mamba_rows, dim),
                tn(attended, gm).reshape(per, out_rows - mamba_rows, dim),
            ],
            axis=1,
        )
        return g_ob, g_outs.astype(BF16)

    def attend_back(qkv, g_ob):
        return attn_backward(q_heads, (qkv, seg_c, seg_r), lse, g_ob, cosine, sine)

    def plus(here, got):
        return (here.astype(F32) + got.astype(F32)).astype(BF16)

    if net.direct:
        (g_ob, g_outs), (got,) = stage(outs_back, (gm,), [(net.flip_core, inner)])
        inner = inner + got
        here = lax.dynamic_index_in_dim(g_outs, net.y, 0, False)
        away = lax.dynamic_index_in_dim(g_outs, 1 - net.y, 0, False)
        got = net.flip_y(away)
        g_qkv, (got_x,) = stage(attend_back, (qkv, g_ob), [(net.flip_x, inner)])
        inner = inner + got_x
        out_both = plus(here, got).reshape(4, out_rows // 4, dim)
    else:
        g_ob, g_outs = outs_back(gm)
        inner = net.ctx_sum(inner)
        g_qkv = attend_back(qkv, g_ob)
    inner = inner.reshape(length, 1) / wide
    stats = jnp.concatenate([scale_m, scale_m * scale_m * scale_m * inner], axis=1)
    g_gated = stats[:, :1] * (g_ym * gain_mamba) - gated * stats[:, 1:]
    sig_z = jax.nn.sigmoid(gate_z)
    g_z = (g_gated * ssm_y * (sig_z + gate_z * sig_z * (1.0 - sig_z))).astype(BF16)
    early = jnp.concatenate([g_z, g_qkv], axis=1)
    grad_early = tn(normed, early).reshape(m, shard, width + slab)

    def ssm_back(states):
        return ssm_backward(
            heads,
            ssm_in,
            states,
            gate_z,
            g_ym,
            ssm_y,
            stats,
            gain_mamba,
            pre,
            cin,
            up,
            taps,
            params,
        )

    if net.direct:
        here, away = net.halves_y(grad_early)
        (g_late, g_conv, g_wide, g_steps), (got, out_parts) = stage(
            ssm_back, (states,), [(net.flip_y, away), (net.shifts_z, out_both)]
        )
        grad_early = plus(here, got)
        out_quarter = sum(p.astype(F32) for p in out_parts).astype(BF16)
    else:
        g_late, g_conv, g_wide, g_steps = ssm_back(states)

    def to_wide(values, at, size):
        out = jnp.zeros(values.shape[:-1] + (size,), F32)
        return lax.dynamic_update_slice_in_dim(out, values, at, values.ndim - 1)

    def for_shards(values):
        values = jnp.concatenate(
            [to_wide(values[:, :width], c * width, wide), values[:, width:]], axis=1
        )
        values = values.reshape((-1, m, values.shape[-1] // m))
        return jnp.transpose(values, (1, 0, 2))

    conv_rows = (conv_b.shape[0] + 127) // 128
    heads_grads = jnp.stack(
        [
            to_wide(g_steps[0, :heads], c * heads, MH),
            to_wide(g_steps[1, :heads], c * heads, MH),
            to_wide(jnp.sum(g_wide[0].reshape(heads, HP), axis=1), c * heads, MH),
            jnp.full((MH,), squared),
        ]
    )
    laid = [jax.vmap(lay)(for_shards(g_conv[: KW + 1]))]
    laid.append(jnp.broadcast_to(lay(heads_grads)[None], (m, 4, 128)))
    laid = jnp.concatenate(laid, axis=1)
    late_size = conv_width + 128
    grad_late = tn(normed, g_late).reshape(m, shard, late_size)
    if net.direct:
        laid = jnp.swapaxes(laid, 1, 2)
        ends_at = conv_width + at_small
        grad_late = jnp.concatenate(
            [grad_late[..., :ends_at], laid, grad_late[..., ends_at + laid.shape[2] :]], axis=2
        )
    grad_late = grad_late.astype(BF16)
    resid = tokens[0].astype(F32)

    def normed_back(early, g_late):
        return (nt(early, w_second) + nt(g_late, w_first)).reshape(n, rows, dim)

    def tokens_back(grad_normed):
        return grad_mixed + rms_back(resid, gain_input, rms_scale(resid), grad_normed)

    if net.direct:
        g_normed = normed_back(early, g_late)
        here, away = net.halves_y(grad_late)
        _, (grad_normed, got, early_parts) = stage(
            tuple,
            (),
            [
                (net.ctx_collect, g_normed),
                (net.flip_y, away),
                (net.shifts_z, grad_early),
            ],
        )
        grad_early = sum(p.astype(F32) for p in early_parts).astype(BF16)
        grad_tokens, (late_parts, out_quarter, got_ff) = stage(
            tokens_back,
            (grad_normed,),
            [
                (net.shifts_z, plus(here, got)),
                (net.cross, out_quarter),
                (net.flip_x, g_ff),
            ],
        )
        g_ff = plus(g_ff, got_ff)
        grad_late = sum(p.astype(F32) for p in late_parts).astype(BF16)
        joined = jnp.concatenate([out_quarter[:, : dim // 2], out_quarter[:, dim // 2 :]], axis=0)
        joined = jnp.concatenate([grad_early, joined], axis=1)
        joined = jnp.concatenate([grad_late, joined], axis=1)
        got, got_ff = net.ctx_all(joined), net.flip_core(g_ff)
        out_w_in, out_w_qkv, out_mamba, out_attn, out_gain_in, out_gain_m, totals = finish(
            got, w_in, w_qkv, w_out, w_o, gain_in, gain_m
        )
        totals = totals[at_small : at_small + laid.shape[2]]
        out_gate, out_up, out_down, out_gain_ffn = finish_ff(
            net.core, g_ff, got_ff, w_gate, w_up, gain_ffn
        )
    else:
        grad_tokens = tokens_back(net.ctx_collect(normed_back(early, g_late)))
        got_early = net.ctx_all(net.collect(grad_early)).astype(F32)
        got_late = net.ctx_all(net.collect(grad_late))
        out_outs = net.rows_back(g_outs).astype(F32)
        got_ff = net.over_cores(g_ff)
        got_late = got_late.astype(F32)
        totals = lax.psum_scatter(laid, "fsdp", scatter_dimension=0, tiled=False)
        totals = lax.psum(totals, "ctx")
        def side(got, start, size):
            return [got[j][:, start : start + size] for j in range(n)]

        shared = n // KVH
        out_w_in = jnp.concatenate(
            side(got_early, 0, width)
            + side(got_late, 0, width)
            + [sum(side(got_late, width, 2 * NS))]
            + side(got_late, conv_width, heads),
            axis=1,
        )
        out_w_qkv = jnp.concatenate(
            side(got_early, width, q_width)
            + [
                sum(side(got_early, width + q_width + i * HD, HD)[k * shared : (k + 1) * shared])
                for i in range(2)
                for k in range(KVH)
            ],
            axis=1,
        )

        def ff_wide(values):
            values = values.reshape(2, shard, m, ff_half)
            return jnp.transpose(values, (1, 2, 0, 3)).reshape(shard, ff)

        out_gate = ff_wide(got_ff[:, :ff_rows])
        out_up = ff_wide(got_ff[:, ff_rows : 2 * ff_rows])
        out_mamba = out_outs[:mamba_rows]

        def along(*pairs):
            return sum(jnp.sum(w.astype(F32) * g, axis=1) for w, g in pairs)

        out_attn = out_outs[mamba_rows:]
        out_down = got_ff[:, 2 * ff_rows :].reshape(ff_shard, dim)
        out_gain_in = along((w_in, out_w_in), (w_qkv, out_w_qkv)) / gain_in.astype(F32)
        out_gain_m = along((w_out, out_mamba)) / gain_m.astype(F32)
        out_gain_ffn = along((w_gate, out_gate), (w_up, out_up)) / gain_ffn.astype(F32)
    grad_conv = unlay(totals, 0, KW + 1, conv_b.shape[0])
    head_totals = totals[(KW + 1) * conv_rows : (KW + 1) * conv_rows + 4, :MH]
    loss = head_totals[3, 0] / (2.0 * count)
    return (
        loss,
        layer_out[None],
        grad_tokens[None],
        out_gain_in,
        out_w_in,
        grad_conv[:KW],
        grad_conv[KW],
        head_totals[0],
        head_totals[1],
        head_totals[2],
        out_gain_m,
        out_mamba,
        out_w_qkv,
        out_attn,
        out_gain_ffn,
        out_gate,
        out_up,
        out_down,
    )


def solution(mesh):
    in_specs = (
        P("fsdp", "ctx", None),
        P("fsdp", "ctx", None),
        P("fsdp", None),
        P("fsdp", "ctx"),
        P("fsdp"),
        P("fsdp", None),
        P(None, "fsdp"),
        P("fsdp"),
        P(),
        P(),
        P(),
        P("fsdp"),
        P("fsdp", None),
        P("fsdp", None),
        P("fsdp", None),
        P("fsdp"),
        P("fsdp", None),
        P("fsdp", None),
        P("fsdp", None),
    )
    out_specs = (
        P(),
        P("fsdp", "ctx", None),
        P("fsdp", "ctx", None),
        P("fsdp"),
        P("fsdp", None),
        P(None, "fsdp"),
        P("fsdp"),
        P(),
        P(),
        P(),
        P("fsdp"),
        P("fsdp", None),
        P("fsdp", None),
        P("fsdp", None),
        P("fsdp"),
        P("fsdp", None),
        P("fsdp", None),
        P("fsdp", None),
    )
    return jax.shard_map(
        per_device, mesh=mesh, in_specs=in_specs, out_specs=out_specs, check_vma=False
    )
```

```python
import functools

import jax
import jax.numpy as jnp
import numpy as np
from jax import lax
from jax.experimental import pallas as pl
from jax.experimental.pallas import tpu as pltpu
from jax.sharding import PartitionSpec as P

MH = 24
HP = 64
NS = 128
KW = 4
QH = 8
KVH = 2
HD = 64
SPAN = 128
QBLK = 256

EPSILON = 1e-05
ROPE_BASE = 100000000000.0
MASKED = -1e30

F32 = jnp.float32
BF16 = jnp.bfloat16
HIGH = lax.Precision.HIGHEST


def nn(left, right, precision=None):
    return lax.dot_general(
        left, right, (((1,), (0,)), ((), ())), precision=precision, preferred_element_type=F32
    )


def nt(left, right):
    return lax.dot_general(left, right, (((1,), (1,)), ((), ())), preferred_element_type=F32)


def tn(left, right):
    return lax.dot_general(left, right, (((0,), (0,)), ((), ())), preferred_element_type=F32)


def swap_halves(values):
    lane = lax.broadcasted_iota(jnp.int32, values.shape, 1) % HD
    size = values.shape[1]
    return jnp.where(
        lane < HD // 2,
        pltpu.roll(values, size - HD // 2, 1),
        pltpu.roll(values, HD // 2, 1),
    )


def conv_kernel(
    tok, gain, weight, taps, bias, same, params, normed_ref, cin_ref, pre_ref, act_ref, step_ref,
    row_ref, halo,
):
    conv = taps.shape[1]
    block = tok.shape[0]

    @pl.when(pl.program_id(0) == 0)
    def _():
        halo[...] = jnp.zeros_like(halo)

    values = tok[...].astype(F32)
    scale = lax.rsqrt(jnp.mean(values * values, axis=-1, keepdims=True) + EPSILON)
    normed = (values * scale * gain[...]).astype(BF16)
    normed_ref[...] = normed
    cin = nn(normed, weight[:, :conv])
    cin_ref[...] = cin.astype(BF16)
    halo[8 : 8 + block, :] = cin
    pre = bias[...] + taps[KW - 1 : KW, :] * cin
    for by in range(1, KW):
        tap = taps[KW - 1 - by : KW - by, :]
        pre = pre + tap * halo[8 - by : 8 - by + block, :] * same[:, by : by + 1]
    halo[0:8, :] = halo[block : block + 8, :]
    pre_ref[...] = pre.astype(BF16)
    act_ref[...] = (pre * jax.nn.sigmoid(pre)).astype(BF16)
    raw = nn(normed, weight[:, conv:]) + params[0:1, :]
    dt = jnp.maximum(raw, 0.0) + jnp.log1p(jnp.exp(-jnp.abs(raw)))
    loga = -dt * params[1:2, :]
    step_ref[:, :128] = dt
    step_ref[:, 128:] = loga
    row_ref[0:8, :] = jnp.transpose(dt)[0:8, :]
    row_ref[8:16, :] = jnp.transpose(loga)[0:8, :]


def by_rows(size):
    return pl.BlockSpec((QBLK, size), lambda i: (i, 0))


def whole(a):
    return pl.BlockSpec(a.shape, lambda i: (0, 0))


def project_conv(tokens, gain, weight, taps, bias, same, params):
    length, dim = tokens.shape
    conv = taps.shape[1]
    sizes = [(dim, BF16), (conv, BF16), (conv, BF16), (conv, BF16), (256, F32)]
    return pl.pallas_call(
        conv_kernel,
        grid=(length // QBLK,),
        in_specs=[
            by_rows(dim),
            whole(gain),
            whole(weight),
            whole(taps),
            whole(bias),
            by_rows(same.shape[1]),
            whole(params),
        ],
        out_specs=[by_rows(size) for size, _ in sizes]
        + [pl.BlockSpec((16, QBLK), lambda i: (0, i))],
        out_shape=[jax.ShapeDtypeStruct((length, size), kind) for size, kind in sizes]
        + [jax.ShapeDtypeStruct((16, length), F32)],
        scratch_shapes=[pltpu.VMEM((QBLK + 8, conv), F32)],
        compiler_params=pltpu.CompilerParams(vmem_limit_bytes=40 * 1024 * 1024),
        cost_estimate=pl.CostEstimate(
            flops=2 * length * dim * weight.shape[1], bytes_accessed=10**7, transcendentals=10**6
        ),
        name="project_conv",
    )(tokens, gain, weight, taps, bias, same, params)


def gate_kernel(normed_ref, weight, y_ref, cosine, sine, z_ref, qkv_ref, sq_ref):
    width = y_ref.shape[1]
    normed = normed_ref[...]
    gate = nn(normed, weight[:, :width])
    z_ref[...] = gate
    qkv = nn(normed, weight[:, width:])
    qkv_ref[...] = (qkv * cosine[...] + swap_halves(qkv) * sine[...]).astype(BF16)
    gated = y_ref[...] * (gate * jax.nn.sigmoid(gate))
    sq_ref[...] = lax.dot_general(
        jnp.ones((8, width), F32),
        gated * gated,
        (((1,), (1,)), ((), ())),
        precision=HIGH,
        preferred_element_type=F32,
    )


def project_gate(normed, weight, y, cosine, sine):
    length, dim = normed.shape
    width = y.shape[1]
    slab = cosine.shape[1]
    return pl.pallas_call(
        gate_kernel,
        grid=(length // QBLK,),
        in_specs=[by_rows(dim), whole(weight), by_rows(width), by_rows(slab), by_rows(slab)],
        out_specs=[
            by_rows(width),
            by_rows(slab),
            pl.BlockSpec((8, QBLK), lambda i: (0, i)),
        ],
        out_shape=[
            jax.ShapeDtypeStruct((length, width), F32),
            jax.ShapeDtypeStruct((length, slab), BF16),
            jax.ShapeDtypeStruct((8, length), F32),
        ],
        compiler_params=pltpu.CompilerParams(vmem_limit_bytes=40 * 1024 * 1024),
        cost_estimate=pl.CostEstimate(
            flops=2 * length * dim * weight.shape[1], bytes_accessed=10**7, transcendentals=10**6
        ),
        name="project_gate",
    )(normed, weight, y, cosine, sine)


def decays(seg_c, seg_r, loga_c, loga_r, before, end):
    row = lax.broadcasted_iota(jnp.int32, (SPAN, SPAN), 0)
    col = lax.broadcasted_iota(jnp.int32, (SPAN, SPAN), 1)
    lower = row >= col
    same = (seg_c == seg_r) & lower
    run_c = nn(lower.astype(F32), loga_c, HIGH)
    run_r = nn(loga_r, (row <= col).astype(F32), HIGH)
    keep = (seg_c == before).astype(F32)
    tail = (seg_c == end).astype(F32)
    return row, col, same, run_c, run_r, keep, tail


def head_groups(heads):
    return [tuple(range(g, min(g + 2, heads))) for g in range(0, heads, 2)]


def by_lane(columns, group, size):
    first = columns[:, group[0] : group[0] + 1]
    if len(group) == 1:
        return first
    lane = lax.broadcasted_iota(jnp.int32, (columns.shape[0], size), 1)
    return jnp.where(lane < HP, first, columns[:, group[1] : group[1] + 1])


def stacked(values, group):
    if len(group) == 1:
        return values
    lane = lax.broadcasted_iota(jnp.int32, values.shape, 1)
    zero = jnp.zeros_like(values)
    return jnp.concatenate(
        [jnp.where(lane < HP, values, zero), jnp.where(lane < HP, zero, values)], axis=0
    )


def ssm_fwd_kernel(
    heads, ends, skip, act, steps, rows, seg_c, seg_r, y_ref, st_ref, state, weighted
):
    step = pl.program_id(0)

    @pl.when(step == 0)
    def _():
        state[...] = jnp.zeros_like(state)

    before, end = ends[step], ends[step + 1]
    link = (before == end).astype(F32)
    _, _, same, run_c, run_r, keep, tail = decays(
        seg_c[...], seg_r[...], steps[:, 128:], rows[8:16, :], before, end
    )
    width = heads * HP
    b_in = act[:, width : width + NS]
    c_in = act[:, width + NS : width + 2 * NS]
    gram = nt(c_in, b_in)
    last = run_c[SPAN - 1 :, :]
    carry_w = jnp.exp(run_c) * keep
    end_w = jnp.exp(last - run_c) * tail * steps[:, :128]
    prior = state[...]
    st_ref[0] = prior
    from_state = nt(c_in, prior.astype(BF16))
    for group in head_groups(heads):
        size = len(group) * HP
        lanes = slice(group[0] * HP, group[0] * HP + size)
        x_in = act[:, lanes]
        x_wide = x_in.astype(F32)
        mixing = []
        for h in group:
            decay = jnp.where(same, jnp.exp(run_c[:, h : h + 1] - run_r[h : h + 1, :]), 0.0)
            mixing.append((gram * decay * rows[h : h + 1, :]).astype(BF16))
        y_in = nn(jnp.concatenate(mixing, axis=1), stacked(x_in, group))
        skips = [skip[h] for h in group]
        lane = lax.broadcasted_iota(jnp.int32, (1, size), 1)
        skip_w = jnp.where(lane < HP, skips[0], skips[-1])
        y_ref[:, lanes] = (
            y_in + from_state[:, lanes] * by_lane(carry_w, group, size) + skip_w * x_wide
        )
        weighted[:, lanes] = (x_wide * by_lane(end_w, group, size)).astype(BF16)
    local = tn(weighted[...], b_in)
    for h in range(heads):
        part = slice(h * HP, (h + 1) * HP)
        state[part, :] = (jnp.exp(last[:, h : h + 1]) * link) * prior[part, :] + local[part, :]


def ssm_bwd_kernel(
    heads,
    ends,
    skip,
    act,
    steps,
    rows,
    seg_c,
    seg_r,
    st_ref,
    z_ref,
    gym_ref,
    y_ref,
    stat_ref,
    gain_ref,
    pre_ref,
    cin_ref,
    up_ref,
    taps,
    params,
    first_ref,
    gconv_ref,
    gwide_ref,
    gstep_ref,
    gstate,
    gbuf,
    grow,
    carried,
    ended,
):
    step = pl.num_programs(0) - 1 - pl.program_id(0)
    width = heads * HP
    conv = width + 2 * NS

    @pl.when(pl.program_id(0) == 0)
    def _():
        gstate[...] = jnp.zeros_like(gstate)
        gbuf[...] = jnp.zeros_like(gbuf)
        grow[...] = jnp.zeros_like(grow)
        gconv_ref[...] = jnp.zeros_like(gconv_ref)
        gwide_ref[...] = jnp.zeros_like(gwide_ref)
        gstep_ref[...] = jnp.zeros_like(gstep_ref)

    before, end = ends[step], ends[step + 1]
    link = (before == end).astype(F32)
    row, col, same, run_c, run_r, keep, tail = decays(
        seg_c[...], seg_r[...], steps[:, 128:], rows[8:16, :], before, end
    )
    gate = z_ref[...]
    silu = gate * jax.nn.sigmoid(gate)
    gated = y_ref[...] * silu
    g_gated = stat_ref[:, 0:1] * (gym_ref[...] * gain_ref[...]) - gated * stat_ref[:, 1:2]
    g_all = g_gated * silu
    x_all = act[:, :width].astype(F32)
    gwide_ref[0:1, :] += jnp.sum(g_all * x_all, axis=0, keepdims=True)

    b_in = act[:, width : width + NS]
    c_in = act[:, width + NS : width + 2 * NS]
    gram = nt(c_in, b_in)
    last = run_c[SPAN - 1 :, :]
    carry_w = jnp.exp(run_c) * keep
    tail_w = jnp.exp(last - run_c) * tail
    end_w = tail_w * steps[:, :128]
    prior = st_ref[0]
    prior_low = prior.astype(BF16)
    after = gstate[...]
    after_low = after.astype(BF16)
    from_prior = nt(c_in, prior_low)
    from_after = nt(b_in, after_low)
    g_gram = jnp.zeros((SPAN, SPAN), F32)
    row_sums = jnp.zeros((SPAN, SPAN), F32)
    for group in head_groups(heads):
        size = len(group) * HP
        lanes = slice(group[0] * HP, group[0] * HP + size)
        gy = g_all[:, lanes]
        gy_parts = stacked(gy.astype(BF16), group)
        g_mixes = nt(gy_parts, act[:, lanes])
        mixing = []
        for i, h in enumerate(group):
            dt_row = rows[h : h + 1, :]
            decay = jnp.where(same, jnp.exp(run_c[:, h : h + 1] - run_r[h : h + 1, :]), 0.0)
            mixing.append((gram * decay * dt_row).astype(BF16))
            g_mix = g_mixes[i * SPAN : (i + 1) * SPAN, :] * decay
            g_gram_h = g_mix * dt_row
            g_gram = g_gram + g_gram_h
            sums = jnp.sum(g_gram_h * gram, axis=1, keepdims=True)
            row_sums = jnp.where(col == h, sums, row_sums)
            by_key = jnp.sum(g_mix * gram, axis=0, keepdims=True)
            grow[h : h + 1, :] = by_key * dt_row
            grow[128 + h : 128 + h + 1, :] = by_key
        skips = [skip[h] for h in group]
        lane = lax.broadcasted_iota(jnp.int32, (1, size), 1)
        skip_w = jnp.where(lane < HP, skips[0], skips[-1])
        end_l = by_lane(end_w, group, size)
        gbuf[0:SPAN, lanes] = (
            tn(jnp.concatenate(mixing, axis=0), gy_parts)
            + from_after[:, lanes] * end_l
            + skip_w * gy
        )
        carried[:, lanes] = (gy * by_lane(carry_w, group, size)).astype(BF16)
        ended[:, lanes] = (x_all[:, lanes] * end_l).astype(BF16)
    of_head = (
        lax.broadcasted_iota(jnp.int32, (width, 128), 0) // HP
        == lax.broadcasted_iota(jnp.int32, (width, 128), 1)
    ).astype(BF16)

    def head_sums(values):
        high = values.astype(BF16)
        return nn(high, of_head) + nn((values - high.astype(F32)).astype(BF16), of_head)

    g_carry = head_sums(g_all * from_prior)
    g_tail = head_sums(x_all * from_after)
    state_sums = jnp.sum(after * prior, axis=1, keepdims=True)
    of_head_t = (
        lax.broadcasted_iota(jnp.int32, (width, 128), 0) // HP
        == lax.broadcasted_iota(jnp.int32, (width, 128), 1)
    )
    state_sums = jnp.sum(jnp.where(of_head_t, state_sums, 0.0), axis=0, keepdims=True)
    g_end = g_tail * end_w
    g_link = jnp.exp(last) * link
    total_last = jnp.sum(g_end, axis=0, keepdims=True) + g_link * state_sums
    g_run = row_sums + g_carry * carry_w - g_end + jnp.where(row == SPAN - 1, total_last, 0.0)
    weighted = carried[...]
    g_gram_low = g_gram.astype(BF16)
    gbuf[0:SPAN, width : width + NS] = nn(ended[...], after_low) + tn(g_gram_low, c_in)
    gbuf[0:SPAN, width + NS :] = nn(weighted, prior_low) + nn(g_gram_low, b_in)
    to_state = tn(weighted, c_in)
    for h in range(heads):
        part = slice(h * HP, (h + 1) * HP)
        gstate[part, :] = g_link[:, h : h + 1] * after[part, :] + to_state[part, :]

    pre = pre_ref[...].astype(F32)
    sig = jax.nn.sigmoid(pre)
    g_pre = gbuf[0:SPAN, :] * (sig + pre * sig * (1.0 - sig))
    gbuf[0:SPAN, :] = g_pre
    cin = cin_ref[...].astype(F32)
    g_conv = taps[KW - 1 : KW, :] * g_pre
    gconv_ref[KW - 1 : KW, :] += jnp.sum(g_pre * cin, axis=0, keepdims=True)
    gconv_ref[KW : KW + 1, :] += jnp.sum(g_pre, axis=0, keepdims=True)
    for by in range(1, KW):
        ahead = gbuf[by : by + SPAN, :] * up_ref[:, by : by + 1]
        tap = KW - 1 - by
        g_conv = g_conv + taps[tap : tap + 1, :] * ahead
        gconv_ref[tap : tap + 1, :] += jnp.sum(ahead * cin, axis=0, keepdims=True)
    gbuf[SPAN : SPAN + 8, :] = gbuf[0:8, :]
    first_ref[:, :conv] = g_conv.astype(BF16)

    later = (col >= row).astype(F32)
    eye = (col == row).astype(F32)

    def across(left, right):
        return lax.dot_general(
            left, right, (((1,), (1,)), ((), ())), precision=HIGH, preferred_element_type=F32
        )

    g_loga = nn(later, g_run, HIGH) - across(later, grow[:128, :])
    g_dt = g_tail * tail_w + across(eye, grow[128:, :]) - g_loga * params[1:2, :]
    g_step = g_dt * (1.0 - jnp.exp(-steps[:, :128]))
    first_ref[:, conv:] = g_step.astype(BF16)
    gstep_ref[0:1, :] += jnp.sum(g_step, axis=0, keepdims=True)
    gstep_ref[1:2, :] += jnp.sum(g_loga * steps[:, 128:], axis=0, keepdims=True)


def ssm_specs(heads, at):
    width = heads * HP
    return [
        pl.BlockSpec(memory_space=pltpu.SMEM),
        pl.BlockSpec(memory_space=pltpu.SMEM),
        pl.BlockSpec((SPAN, width + 2 * NS), lambda i: (at(i), 0)),
        pl.BlockSpec((SPAN, 256), lambda i: (at(i), 0)),
        pl.BlockSpec((16, SPAN), lambda i: (0, at(i))),
        pl.BlockSpec((SPAN, 1), lambda i: (at(i), 0)),
        pl.BlockSpec((1, SPAN), lambda i: (0, at(i))),
    ]


def ssm_forward(heads, inputs):
    length = inputs[2].shape[0]
    steps = length // SPAN
    width = heads * HP
    return pl.pallas_call(
        functools.partial(ssm_fwd_kernel, heads),
        grid=(steps,),
        in_specs=ssm_specs(heads, lambda i: i),
        out_specs=[
            pl.BlockSpec((SPAN, width), lambda i: (i, 0)),
            pl.BlockSpec((1, width, NS), lambda i: (i, 0, 0)),
        ],
        out_shape=[
            jax.ShapeDtypeStruct((length, width), F32),
            jax.ShapeDtypeStruct((steps, width, NS), F32),
        ],
        scratch_shapes=[pltpu.VMEM((width, NS), F32), pltpu.VMEM((SPAN, width), BF16)],
        compiler_params=pltpu.CompilerParams(vmem_limit_bytes=32 * 1024 * 1024),
        cost_estimate=pl.CostEstimate(
            flops=10**9, bytes_accessed=4 * 10**7, transcendentals=10**6
        ),
        name="ssm_forward",
    )(*inputs)


def ssm_backward(heads, inputs, states, gate_z, g_ym, ssm_y, stats, gain, pre, cin, up, taps, params):
    length = inputs[2].shape[0]
    steps = length // SPAN
    width = heads * HP
    conv = width + 2 * NS
    total = conv + 128

    def at(i):
        return steps - 1 - i

    def part(size):
        return pl.BlockSpec((SPAN, size), lambda i: (at(i), 0))

    def fixed(shape):
        return pl.BlockSpec(shape, lambda i: (0, 0))

    return pl.pallas_call(
        functools.partial(ssm_bwd_kernel, heads),
        grid=(steps,),
        in_specs=ssm_specs(heads, at)
        + [
            pl.BlockSpec((1, width, NS), lambda i: (at(i), 0, 0)),
            part(width),
            part(width),
            part(width),
            part(stats.shape[1]),
            fixed(gain.shape),
            part(conv),
            part(conv),
            part(up.shape[1]),
            fixed(taps.shape),
            fixed(params.shape),
        ],
        out_specs=[part(total), fixed((8, conv)), fixed((8, width)), fixed((8, 128))],
        out_shape=[
            jax.ShapeDtypeStruct((length, total), BF16),
            jax.ShapeDtypeStruct((8, conv), F32),
            jax.ShapeDtypeStruct((8, width), F32),
            jax.ShapeDtypeStruct((8, 128), F32),
        ],
        scratch_shapes=[
            pltpu.VMEM((width, NS), F32),
            pltpu.VMEM((SPAN + 8, conv), F32),
            pltpu.VMEM((256, SPAN), F32),
            pltpu.VMEM((SPAN, width), BF16),
            pltpu.VMEM((SPAN, width), BF16),
        ],
        compiler_params=pltpu.CompilerParams(vmem_limit_bytes=56 * 1024 * 1024),
        cost_estimate=pl.CostEstimate(
            flops=10**7, bytes_accessed=10**6, transcendentals=10**4
        ),
        name="ssm_backward",
    )(*inputs, states, gate_z, g_ym, ssm_y, stats, gain, pre, cin, up, taps, params)


def allowed_keys(index, reach, seg_c, seg_r):
    row = lax.broadcasted_iota(jnp.int32, (QBLK, reach), 0) + index * QBLK
    col = lax.broadcasted_iota(jnp.int32, (QBLK, reach), 1)
    return (seg_c[...] == seg_r[:, :reach]) & (col <= row)


def attn_fwd_kernel(heads, blocks, qkv_ref, seg_c, seg_r, out_ref, lse_ref):
    wide = heads * HD
    for index in range(blocks):

        @pl.when(pl.program_id(0) == index)
        def _(index=index):
            reach = (index + 1) * QBLK
            allowed = allowed_keys(index, reach, seg_c, seg_r)
            own = slice(index * QBLK, reach)
            keys = qkv_ref[:reach, wide : wide + HD]
            values = qkv_ref[:reach, wide + HD : wide + 2 * HD]
            for h in range(heads):
                lanes = slice(h * HD, (h + 1) * HD)
                scores = nt(qkv_ref[own, lanes], keys) * (HD**-0.5)
                scores = jnp.where(allowed, scores, MASKED)
                top = jnp.max(scores, axis=1, keepdims=True)
                expo = jnp.exp(scores - top)
                total = jnp.sum(expo, axis=1, keepdims=True)
                probs = (expo * (1.0 / total)).astype(BF16)
                out_ref[:, lanes] = nn(probs, values).astype(BF16)
                lse_ref[:, h : h + 1] = top + jnp.log(total)


def attn_bwd_kernel(
    heads, blocks, qkv_ref, seg_c, seg_r, lse_ref, go_ref, cosine, sine, out_ref, grads
):
    wide = heads * HD

    @pl.when(pl.program_id(0) == 0)
    def _():
        grads[...] = jnp.zeros_like(grads)

    for index in range(blocks):

        @pl.when(pl.program_id(0) == index)
        def _(index=index):
            reach = (index + 1) * QBLK
            allowed = allowed_keys(index, reach, seg_c, seg_r)
            own = slice(index * QBLK, reach)
            keys = qkv_ref[:reach, wide : wide + HD]
            values = qkv_ref[:reach, wide + HD : wide + 2 * HD]
            for h in range(heads):
                lanes = slice(h * HD, (h + 1) * HD)
                query = qkv_ref[own, lanes]
                g_out = go_ref[:, lanes]
                scores = nt(query, keys) * (HD**-0.5)
                probs = jnp.where(allowed, jnp.exp(scores - lse_ref[:, h : h + 1]), 0.0)
                g_probs = nt(g_out, values)
                delta = jnp.sum(probs * g_probs, axis=1, keepdims=True)
                g_scores = (probs * (g_probs - delta)).astype(BF16)
                grads[own, lanes] = nn(g_scores, keys) * (HD**-0.5)
                grads[:reach, wide : wide + HD] += tn(g_scores, query) * (HD**-0.5)
                grads[:reach, wide + HD : wide + 2 * HD] += tn(probs.astype(BF16), g_out)
            if index == blocks - 1:
                for b in range(blocks):
                    part = slice(b * QBLK, (b + 1) * QBLK)
                    slab = grads[part, :]
                    out_ref[part, :] = (
                        slab * cosine[part, :] - swap_halves(slab) * sine[part, :]
                    ).astype(BF16)


def attn_specs(length, slab):
    return [
        pl.BlockSpec((length, slab), lambda i: (0, 0)),
        pl.BlockSpec((QBLK, 1), lambda i: (i, 0)),
        pl.BlockSpec((1, length), lambda i: (0, 0)),
    ]


def attn_forward(heads, inputs):
    length, slab = inputs[0].shape
    blocks = length // QBLK
    return pl.pallas_call(
        functools.partial(attn_fwd_kernel, heads, blocks),
        grid=(blocks,),
        in_specs=attn_specs(length, slab),
        out_specs=[
            pl.BlockSpec((QBLK, heads * HD), lambda i: (i, 0)),
            pl.BlockSpec((QBLK, heads), lambda i: (i, 0)),
        ],
        out_shape=[
            jax.ShapeDtypeStruct((length, heads * HD), BF16),
            jax.ShapeDtypeStruct((length, heads), F32),
        ],
        compiler_params=pltpu.CompilerParams(vmem_limit_bytes=32 * 1024 * 1024),
        cost_estimate=pl.CostEstimate(
            flops=10**9, bytes_accessed=2 * 10**7, transcendentals=10**6
        ),
        name="attn_forward",
    )(*inputs)


def attn_backward(heads, inputs, lse, g_out, cosine, sine):
    length, slab = inputs[0].shape
    blocks = length // QBLK
    full = pl.BlockSpec((length, slab), lambda i: (0, 0))
    return pl.pallas_call(
        functools.partial(attn_bwd_kernel, heads, blocks),
        grid=(blocks,),
        in_specs=attn_specs(length, slab)
        + [
            pl.BlockSpec((QBLK, heads), lambda i: (i, 0)),
            pl.BlockSpec((QBLK, heads * HD), lambda i: (i, 0)),
            full,
            full,
        ],
        out_specs=full,
        out_shape=jax.ShapeDtypeStruct((length, slab), BF16),
        scratch_shapes=[pltpu.VMEM((length, slab), F32)],
        compiler_params=pltpu.CompilerParams(vmem_limit_bytes=56 * 1024 * 1024),
        cost_estimate=pl.CostEstimate(
            flops=10**7, bytes_accessed=10**6, transcendentals=10**4
        ),
        name="attn_backward",
    )(*inputs, lse, g_out, cosine, sine)


def ff_kernel(both, product, g_gate, g_up, gb, out):
    rows = both.shape[1]
    out[0, :rows] = tn(both[...], g_gate[...]).astype(BF16)
    out[0, rows : 2 * rows] = tn(both[...], g_up[...]).astype(BF16)
    out[0, 2 * rows :] = tn(product[...], gb[...]).astype(BF16)


def ff_gradients(m, both, product, g_gate, g_up, gb):
    tokens, dim = both.shape
    rows, down = dim // m, product.shape[1] // m
    full = pl.BlockSpec((tokens, dim), lambda i: (0, 0))
    return pl.pallas_call(
        ff_kernel,
        grid=(m,),
        in_specs=[
            pl.BlockSpec((tokens, rows), lambda i: (0, i)),
            pl.BlockSpec((tokens, down), lambda i: (0, i)),
            full,
            full,
            full,
        ],
        out_specs=pl.BlockSpec((1, 2 * rows + down, dim), lambda i: (i, 0, 0)),
        out_shape=jax.ShapeDtypeStruct((m, 2 * rows + down, dim), BF16),
        compiler_params=pltpu.CompilerParams(vmem_limit_bytes=40 * 1024 * 1024),
        cost_estimate=pl.CostEstimate(
            flops=6 * tokens * dim * dim, bytes_accessed=10**7, transcendentals=0
        ),
        name="ff_gradients",
    )(both, product, g_gate, g_up, gb)


def row_totals(values):
    ones = jnp.ones((8, values.shape[1]), F32)
    return lax.dot_general(
        ones, values, (((1,), (1,)), ((), ())), precision=HIGH, preferred_element_type=F32
    )


def finish_ff_kernel(core, own, mate, w_gate, w_up, gain, gate_ref, up_ref, down_ref, gain_ref):
    rows = w_gate.shape[0]
    tiles = own.shape[1] // 128
    total = jnp.zeros((rows, 128), F32)
    for half in range(2):
        mine = core[0] == half

        def pick(low, high, lanes, mine=mine):
            return jnp.where(mine, own[low:high, lanes], mate[low:high, lanes]).astype(F32)

        for f in range(tiles):
            lanes = slice(f * 128, (f + 1) * 128)
            to = slice((2 * f + half) * 128, (2 * f + half + 1) * 128)
            gate_ref[:, to] = pick(0, rows, lanes)
            up_ref[:, to] = pick(rows, 2 * rows, lanes)
        down = down_ref.shape[0] // 2
        down_ref[half * down : (half + 1) * down, :] = pick(2 * rows, 2 * rows + down, slice(None))
    for t in range(2 * tiles):
        lanes = slice(t * 128, (t + 1) * 128)
        total = total + gate_ref[:, lanes] * w_gate[:, lanes].astype(F32)
        total = total + up_ref[:, lanes] * w_up[:, lanes].astype(F32)
    gain_ref[...] = row_totals(total) / gain[...]


def finish_ff(core, own, mate, w_gate, w_up, gain):
    shard, ff = w_gate.shape
    down = own.shape[0] - 2 * shard
    vmem = pl.BlockSpec(memory_space=pltpu.VMEM)
    out = pl.pallas_call(
        finish_ff_kernel,
        in_specs=[pl.BlockSpec(memory_space=pltpu.SMEM)] + [vmem] * 5,
        out_specs=[vmem] * 4,
        out_shape=[
            jax.ShapeDtypeStruct((shard, ff), F32),
            jax.ShapeDtypeStruct((shard, ff), F32),
            jax.ShapeDtypeStruct((2 * down, own.shape[1]), F32),
            jax.ShapeDtypeStruct((8, shard), F32),
        ],
        compiler_params=pltpu.CompilerParams(vmem_limit_bytes=40 * 1024 * 1024),
        name="finish_ff",
    )(core.astype(jnp.int32)[None], own, mate, w_gate, w_up, gain.astype(F32)[None])
    return out[0], out[1], out[2], out[3][0]


def finish_kernel(
    place,
    own,
    mates,
    w_in,
    w_qkv,
    w_out,
    gain_in,
    gain_m,
    in_ref,
    qkv_ref,
    out_ref,
    o_ref,
    gain_in_ref,
    gain_m_ref,
    small_ref,
    steps,
):
    count = 2 * own.shape[0]
    shard = w_qkv.shape[0]
    heads = MH // count
    width = heads * HP
    conv = width + 2 * NS
    late = conv + 128
    q_width = QH * HD // count
    wide = count * width
    steps[...] = jnp.zeros_like(steps)
    shared = jnp.zeros((shard, 2 * NS), F32)
    gain = jnp.zeros((1, shard), F32)
    small = jnp.zeros((shard, 128), F32)
    pairs = []

    def lay(at, values, gain):
        flat = jnp.transpose(values)
        rows = slice(at, at + flat.shape[0])
        in_ref[rows, :] = flat
        return gain + jnp.sum(flat * w_in[rows, :].astype(F32), axis=0, keepdims=True)

    for j in range(count):

        at_x = (place[0] + j // 2) % 2
        mine = place[1] == j % 2

        def pick(rows, lanes, at_x=at_x, mine=mine):
            return jnp.where(mine, own[at_x, rows, lanes], mates[at_x, rows, lanes]).astype(F32)

        def part(low, high, pick=pick):
            return pick(slice(None), slice(low, high))

        gain = lay(j * width, part(late, late + width), gain)
        gain = lay(wide + j * width, part(0, width), gain)
        shared = shared + part(width, conv)
        steps[:, j * heads : (j + 1) * heads] = part(conv, conv + heads)
        at = late + width
        qkv_ref[:, j * q_width : (j + 1) * q_width] = part(at, at + q_width)
        pairs.append(part(at + q_width, at + q_width + 128))
        at = at + q_width + 128
        lanes = slice(at, own.shape[2])
        rows = pick(slice(0, shard // 2), lanes), pick(slice(shard // 2, shard), lanes)
        rows = jnp.concatenate(rows, axis=1)
        low = j * (shard // 2)
        if low < out_ref.shape[0]:
            out_ref[low : low + shard // 2, :] = rows
        else:
            low -= out_ref.shape[0]
            o_ref[low : low + shard // 2, :] = rows
        small = small + part(conv, late)
    gain = lay(2 * wide, shared, gain)
    at = 2 * wide + 2 * NS
    flat = jnp.transpose(steps[...])[: in_ref.shape[0] - at, :]
    in_ref[at:, :] = flat
    gain = gain + jnp.sum(flat * w_in[at:, :].astype(F32), axis=0, keepdims=True)
    one, two = pairs[0] + pairs[1], pairs[2] + pairs[3]
    low = lax.broadcasted_iota(jnp.int32, one.shape, 1) < HD
    at = QH * HD
    qkv_ref[:, at : at + 128] = jnp.where(low, one, pltpu.roll(two, HD, 1))
    qkv_ref[:, at + 128 :] = jnp.where(low, pltpu.roll(one, HD, 1), two)
    gain = row_totals(qkv_ref[...] * w_qkv[...].astype(F32)) + gain
    gain_in_ref[...] = gain / gain_in[...]
    gain_m_ref[...] = row_totals(out_ref[...] * w_out[...].astype(F32)) / gain_m[...]
    small_ref[...] = jnp.transpose(small)


def finish(place, own, mates, w_in, w_qkv, w_out, w_o, gain_in, gain_m):
    shard = w_qkv.shape[0]
    vmem = pl.BlockSpec(memory_space=pltpu.VMEM)
    shapes = [w_in.shape[::-1], w_qkv.shape, w_out.shape, w_o.shape]
    shapes += [(8, shard), (8, w_out.shape[0]), (128, shard)]
    out = pl.pallas_call(
        finish_kernel,
        in_specs=[pl.BlockSpec(memory_space=pltpu.SMEM)] + [vmem] * 7,
        out_specs=[vmem] * 7,
        out_shape=[jax.ShapeDtypeStruct(shape, F32) for shape in shapes],
        scratch_shapes=[pltpu.VMEM((shard, 128), F32)],
        compiler_params=pltpu.CompilerParams(vmem_limit_bytes=40 * 1024 * 1024),
        name="finish",
    )(place, own, mates, w_in.T, w_qkv, w_out, gain_in.astype(F32)[None], gain_m.astype(F32)[None])
    return out[0].T, out[1], out[2], out[3], out[4][0], out[5][0], out[6]


def tie(value, *after):
    return lax.optimization_barrier((value,) + after)[0]


def stage(compute, inputs, sends, late=()):
    inputs, operands = lax.optimization_barrier((inputs, [operand for _, operand in sends]))
    got = [send(operand) for (send, _), operand in zip(sends, operands)]
    out, got, late = lax.optimization_barrier((compute(*inputs), got, late))
    return (out, got, late) if late else (out, got)


class Net:
    def __init__(self):
        self.n = lax.axis_size("ctx")
        self.m = lax.axis_size("fsdp")
        self.c = lax.axis_index("ctx")
        self.f = lax.axis_index("fsdp")
        self.direct = self.n == 4 and self.m == 8
        self.x, self.core = self.c // 2, self.c % 2
        self.z, self.y = self.f // 2, self.f % 2
        self.by_core = [[i * 2 + k for i in range(self.n // 2)] for k in range(2)]

    def flip(self, value, axis, bit):
        size = lax.axis_size(axis)
        return lax.ppermute(value, axis, [(i, i ^ bit) for i in range(size)])

    def shift_z(self, value, by):
        return lax.ppermute(value, "fsdp", [(i, (i + 2 * by) % self.m) for i in range(self.m)])

    def cross(self, value):
        pairs = [
            (c * 8 + z * 2 + y, z * 8 + c * 2 + y)
            for c in range(4)
            for z in range(4)
            for y in range(2)
        ]
        return lax.ppermute(value, ("ctx", "fsdp"), pairs)

    def along_z(self, block):
        return [block] + [self.shift_z(block, k) for k in range(1, 4)]

    def along_y(self, pieces):
        return [self.flip(piece, "fsdp", 1) for piece in pieces]

    def in_order(self, own, mate, columns=None):
        places = [2 * ((self.z - k) % 4) + (self.y ^ o) for o in range(2) for k in range(4)]
        return put(own + mate, places, columns)

    def flip_y(self, value):
        return self.flip(value, "fsdp", 1)

    def flip_x(self, value):
        return self.flip(value, "ctx", 2)

    def flip_core(self, value):
        return self.flip(value, "ctx", 1)

    def halves_y(self, sums):
        low = sums.astype(BF16)
        low = low.reshape((4, 2) + low.shape[1:])
        away = lax.dynamic_index_in_dim(low, 1 - self.y, 1, False)
        return lax.dynamic_index_in_dim(low, self.y, 1, False), away

    def shifts_z(self, both):
        return self.send_z(self.blocks_z(both))

    def blocks_z(self, both):
        return [lax.dynamic_index_in_dim(both, (self.z + k) % 4, 0, False) for k in range(4)]

    def send_z(self, blocks):
        return [blocks[0]] + [self.shift_z(blocks[k], k) for k in range(1, 4)]

    def collect(self, sums):
        return lax.psum_scatter(sums.astype(BF16), "fsdp", scatter_dimension=0, tiled=False)

    def ctx_all(self, value):
        if not self.direct:
            return lax.all_gather(value, "ctx", axis=0, tiled=False)
        pair = jnp.stack([value, self.flip(value, "ctx", 2)])
        mates = self.flip(pair, "ctx", 1)
        return put([pair, mates], [self.c, self.c ^ 2, self.c ^ 1, self.c ^ 3])

    def ctx_sum(self, value):
        if not self.direct:
            return lax.psum(value, "ctx")
        value = value + self.flip(value, "ctx", 1)
        return value + self.flip(value, "ctx", 2)

    def ctx_collect(self, parts):
        if not self.direct:
            low = lax.psum_scatter(parts.astype(BF16), "ctx", scatter_dimension=0, tiled=False)
            return low.astype(F32)
        own, away = self.ctx_halves(parts)
        return own + self.flip(away, "ctx", 2).astype(F32)

    def ctx_halves(self, parts):
        pairs = parts.reshape((2, 2) + parts.shape[1:])
        away = lax.dynamic_index_in_dim(pairs, 1 - self.core, 1, False).astype(BF16)
        here = lax.dynamic_index_in_dim(pairs, self.core, 1, False)
        got = self.flip(away, "ctx", 1)

        def half(which):
            return lax.dynamic_index_in_dim(here, which, 0, False).astype(
                F32
            ) + lax.dynamic_index_in_dim(got, which, 0, False).astype(F32)

        return half(self.x), half(1 - self.x).astype(BF16)

    def over_cores(self, value):
        value = lax.psum(value, "ctx", axis_index_groups=self.by_core)
        return lax.all_gather(value, "ctx", axis=0)[:2].astype(F32)

    def rows_out(self, shard):
        per = self.m // self.n
        got = lax.all_gather(shard, "fsdp", axis=0, tiled=False)
        return lax.dynamic_slice_in_dim(got, self.c * per, per, 0)

    def rows_back(self, sums):
        wide = jnp.zeros((self.m,) + sums.shape[1:], BF16)
        wide = lax.dynamic_update_slice_in_dim(
            wide, sums.astype(BF16), self.c * (self.m // self.n), 0
        )
        out = lax.psum_scatter(wide, "fsdp", scatter_dimension=0, tiled=False)
        return lax.psum(out, "ctx")


def put_kernel(counts, cuts, places, *refs):
    parts, outs = refs[: len(counts)], refs[len(counts) :]
    start = 0
    for part, count in zip(parts, counts):

        @pl.when((pl.program_id(0) >= start) & (pl.program_id(0) < start + count))
        def _(part=part):
            for out, low, high in zip(outs, cuts[:-1], cuts[1:]):
                out[...] = part[..., low:high]

        start += count


def put(parts, places, columns=None):
    counts = [part.shape[0] for part in parts]
    total = sum(counts)
    shape = parts[0].shape[1:]
    zeros = (0,) * len(shape)
    sizes = columns or [shape[-1]]
    cuts = [0]
    for size in sizes:
        cuts.append(cuts[-1] + size)
    places = jnp.stack([jnp.asarray(p, jnp.int32) for p in places])
    size = parts[0][0].size * parts[0].dtype.itemsize
    specs = []
    for p in range(len(parts)):
        start = sum(counts[:p])

        def at(i, at, start=start, last=counts[p] - 1):
            return (jnp.clip(i - start, 0, last),) + zeros

        specs.append(pl.BlockSpec((1,) + shape, at))
    out = pl.pallas_call(
        functools.partial(put_kernel, counts, cuts),
        grid_spec=pltpu.PrefetchScalarGridSpec(
            num_scalar_prefetch=1,
            grid=(total,),
            in_specs=specs,
            out_specs=[
                pl.BlockSpec((1,) + shape[:-1] + (w,), lambda i, at: (at[i],) + zeros)
                for w in sizes
            ],
        ),
        out_shape=[
            jax.ShapeDtypeStruct((total,) + shape[:-1] + (w,), parts[0].dtype) for w in sizes
        ],
        compiler_params=pltpu.CompilerParams(vmem_limit_bytes=40 * 1024 * 1024),
        cost_estimate=pl.CostEstimate(
            flops=0, bytes_accessed=2 * total * size, transcendentals=0
        ),
        name="put",
    )(places, *parts)
    return out if columns else out[0]


def rms_scale(values):
    return lax.rsqrt(jnp.mean(values * values, axis=-1, keepdims=True) + EPSILON)


def rms_back(values, gain, scale, grad):
    scaled = grad * gain
    inner = jnp.mean(values * scaled, axis=-1, keepdims=True)
    return scale * scaled - values * (scale * scale * scale * inner)


def columns_of(w, start, size):
    return lax.dynamic_slice_in_dim(w, start, size, 1)


def rotary_tables(length, q_heads, slab):
    half = HD // 2
    freq = (ROPE_BASE ** (-(np.arange(half) * 2.0 / HD))).astype(np.float32)
    angle = np.arange(length, dtype=np.float32)[:, None] * freq[None, :]
    one = np.concatenate([np.cos(angle), np.cos(angle)], axis=1)
    two = np.concatenate([-np.sin(angle), np.sin(angle)], axis=1)
    room = slab - (q_heads + 1) * HD
    cosine = np.concatenate([one] * (q_heads + 1) + [np.ones((length, room))], axis=1)
    sine = np.concatenate([two] * (q_heads + 1) + [np.zeros((length, room))], axis=1)
    return jnp.asarray(cosine, F32), jnp.asarray(sine, F32)


def per_device(
    tokens,
    teacher,
    segment_ids,
    valid_mask,
    gain_in,
    w_in,
    conv_w,
    conv_b,
    dt_bias,
    a_log,
    d_skip,
    gain_m,
    w_out,
    w_qkv,
    w_o,
    gain_ffn,
    w_gate,
    w_up,
    w_down,
):
    net = Net()
    n, m, c, f = net.n, net.m, net.c, net.f
    rows, dim = tokens.shape[1:]
    length = segment_ids.shape[1]
    shard = w_in.shape[0]
    wide = MH * HP
    conv_full = wide + 2 * NS
    heads = MH // n
    q_heads = QH // n
    width = heads * HP
    conv_width = width + 2 * NS
    q_width = q_heads * HD
    slab = q_width + 2 * HD
    slab += -slab % 128
    group = QH // KVH
    kv_at = (c * q_heads) // group
    ff = w_gate.shape[1]
    ff_shard = w_down.shape[0]
    per = m // n
    seg = segment_ids[0]
    seg_c, seg_r = seg[:, None], seg[None, :]
    ends = jnp.concatenate([jnp.full((1,), -1, jnp.int32), seg[SPAN - 1 :: SPAN]])
    valid = valid_mask[0].astype(F32)

    def lay(values):
        values = values.reshape((-1, values.shape[-1]))
        room = -values.shape[1] % 128
        return jnp.pad(values, ((0, 0), (0, room))).reshape(-1, 128)

    def unlay(small, start, lead, size):
        room = size + -size % 128
        count = lead * room // 128
        return small[..., start : start + count, :].reshape(small.shape[:-2] + (lead, room))[
            ..., :size
        ]

    shapes = [(1, shard), (1, shard), (1, w_out.shape[0]), (1, conv_b.shape[0])]
    shapes += [(KW, conv_b.shape[0])]
    starts = [0]
    for lead, size in shapes:
        starts.append(starts[-1] + lead * (size + -size % 128) // 128)
    laid = [lay(p) for p in (gain_in[None], gain_ffn[None], gain_m[None], conv_b[None], conv_w)]
    laid.append(jnp.full((1, 128), jnp.sum(valid), F32).astype(BF16))
    laid.append(jnp.zeros((-(starts[-1] + 1) % 16, 128), BF16))
    at_small = 64
    packed = jnp.concatenate(laid, axis=0)
    first = jnp.concatenate(
        [
            columns_of(w_in, wide + c * width, width),
            w_in[:, 2 * wide : 2 * wide + 2 * NS],
            columns_of(w_in, wide + conv_full + c * heads, heads),
            jnp.zeros((shard, at_small - heads), BF16),
            packed.T if net.direct else jnp.zeros((shard, packed.shape[0]), BF16),
            jnp.zeros((shard, 128 - at_small - packed.shape[0]), BF16),
        ],
        axis=1,
    )
    second = jnp.concatenate(
        [
            columns_of(w_in, c * width, width),
            columns_of(w_qkv, c * q_width, q_width),
            columns_of(w_qkv, QH * HD + kv_at * HD, HD),
            columns_of(w_qkv, (QH + KVH) * HD + kv_at * HD, HD),
            jnp.zeros((shard, slab - q_width - 2 * HD), BF16),
        ],
        axis=1,
    )
    both_out = jnp.concatenate([w_out, w_o], axis=0)
    out_rows, mamba_rows = both_out.shape[0], w_out.shape[0]
    ff_half = ff_shard // 2
    size = m * ff_half

    def ff_cut(w):
        w = w.reshape(shard, m, 2, ff_half)
        return lax.dynamic_index_in_dim(w, net.core, 2, False).reshape(shard, size)

    places_x = n // 2

    def quarter_x(w):
        size = w.shape[0] // places_x
        return lax.dynamic_slice_in_dim(w, net.x * size, size, 0)

    w_ff = jnp.concatenate(
        [
            quarter_x(ff_cut(w_gate).reshape(-1, dim)),
            quarter_x(ff_cut(w_up).reshape(-1, dim)),
            quarter_x(lax.dynamic_slice_in_dim(w_down, net.core * ff_half, ff_half, 0)),
        ],
        axis=0,
    )
    groups = [[d * m + i for d in net.by_core[k] for i in range(m)] for k in range(2)]
    w_ff = lax.all_gather(
        w_ff, ("ctx", "fsdp"), axis=0, tiled=False, axis_index_groups=groups
    ).reshape((places_x, m) + w_ff.shape)
    if net.direct:
        both_cols = jnp.concatenate([first, second], axis=1)
        pair = jnp.stack([tokens[0], net.flip_x(tokens[0])])
        near = net.along_z(both_cols)
        far = net.along_y([tie(near[0], pair)] + near[1:])
        all_tokens = put([pair, net.flip_core(pair)], [c, c ^ 2, c ^ 1, c ^ 3])
        w_first, w_second = net.in_order(
            [tie(near[0], all_tokens)[None]] + [p[None] for p in near[1:]],
            [p[None] for p in far],
            [first.shape[1], second.shape[1]],
        )
        at = conv_width + at_small
        small = jnp.swapaxes(w_first[:, :, at : at + packed.shape[0]], 1, 2)
        crossed = net.cross(tie(both_out, *near[1:]))
    else:
        small = lax.all_gather(packed, "fsdp", axis=0, tiled=False)
        w_first = lax.all_gather(first, "fsdp", axis=0, tiled=False)
        w_second = lax.all_gather(second, "fsdp", axis=0, tiled=False)
        w_outs = net.rows_out(both_out)
        all_tokens = net.ctx_all(tokens[0])
    all_tokens = all_tokens.reshape(length, dim)
    w_first = w_first.reshape(dim, first.shape[1])
    cuts = [
        jnp.transpose(unlay(small, start, *shape), (1, 0, 2)).reshape(shape[0], -1)
        for start, shape in zip(starts, shapes)
    ]
    gain_input = cuts[0].astype(F32)
    gain_second = cuts[1].astype(F32)
    gain_mamba = lax.dynamic_slice_in_dim(cuts[2], c * width, width, 1).astype(F32)
    count_ctx = jnp.sum(small[:, starts[-1], 0].astype(F32))

    def conv_cut(values):
        own = lax.dynamic_slice_in_dim(values, c * width, width, 1)
        return jnp.concatenate([own, values[:, wide:]], axis=1).astype(F32)

    bias, taps = conv_cut(cuts[3]), conv_cut(cuts[4])
    rate = jnp.exp(a_log)
    params = jnp.stack(
        [lax.dynamic_slice_in_dim(v, c * heads, heads) for v in (dt_bias, rate)]
    )
    params = jnp.pad(params, ((0, 6), (0, 128 - heads)))
    skip = lax.dynamic_slice_in_dim(d_skip, c * heads, heads)

    def shifted(by):
        return jnp.concatenate([jnp.full((by,), -1, jnp.int32), seg[: length - by]]) == seg

    same = jnp.stack([shifted(by) for by in range(KW)], axis=1).astype(F32)
    up = jnp.stack(
        [
            jnp.concatenate([seg[by:], jnp.full((by,), -1, jnp.int32)]) == seg
            for by in range(KW)
        ],
        axis=1,
    ).astype(F32)
    cosine, sine = rotary_tables(length, q_heads, slab)
    conv_args = (all_tokens, gain_input, w_first, taps, bias, same, params)

    def square_rows(square):
        return jnp.concatenate([square[0].reshape(-1, 128), jnp.full((8, 128), count_ctx)])

    def ssm(act, steps, step_rows):
        return ssm_forward(heads, (ends, skip, act, steps, step_rows, seg_c, seg_r))

    def attend(qkv):
        return attn_forward(q_heads, (qkv, seg_c, seg_r))

    w_second = w_second.reshape(dim, second.shape[1])
    if net.direct:
        normed, cin, pre, act, steps, step_rows = project_conv(*conv_args)
        ssm_y, states = ssm(act, steps, step_rows)
        gate_z, qkv, square = project_gate(normed, w_second, ssm_y, cosine, sine)
        mated = net.flip_y(tie(crossed, ssm_y))
        (attended, lse), (square,) = stage(
            attend, (qkv,), [(net.ctx_sum, square_rows(square))]
        )
        w_outs = jnp.where(
            net.y == 0, jnp.stack([crossed, mated]), jnp.stack([mated, crossed])
        )
    else:
        normed, cin, pre, act, steps, step_rows = project_conv(*conv_args)
        ssm_y, states = ssm(act, steps, step_rows)
        gate_z, qkv, square = project_gate(normed, w_second, ssm_y, cosine, sine)
        square = net.ctx_sum(square_rows(square))
        attended, lse = attend(qkv)
    w_mamba = w_outs[:, :mamba_rows].reshape(per * mamba_rows, dim)
    w_attn = w_outs[:, mamba_rows:].reshape(per * (out_rows - mamba_rows), dim)
    ssm_in = (ends, skip, act, steps, step_rows, seg_c, seg_r)
    count = square[-1, 0]
    scale_m = lax.rsqrt(square[:-8].reshape(length, 1) / wide + EPSILON)
    gated = ssm_y * (gate_z * jax.nn.sigmoid(gate_z))
    ym = (gated * scale_m * gain_mamba).astype(BF16)
    outs = nn(ym, w_mamba) + nn(attended, w_attn)
    ff_rows = shard * size // dim
    part_rows = ff_rows // places_x

    def plus(here, got):
        return (here.astype(F32) + got.astype(F32)).astype(BF16)

    def ff_weights(w_ff):
        def part(low, high, columns):
            return jnp.swapaxes(w_ff[:, :, low:high], 0, 1).reshape(-1, columns)

        return (
            part(0, part_rows, size),
            part(part_rows, 2 * part_rows, size),
            part(2 * part_rows, w_ff.shape[2], dim),
        )

    if net.direct:
        own, away = net.ctx_halves(outs.reshape(n, rows, dim))
        (w_g, w_u, w_d), (across,) = stage(ff_weights, (w_ff,), [(net.flip_x, away)])
        mixed = tokens[0].astype(F32) + own + across.astype(F32)
    else:
        w_g, w_u, w_d = ff_weights(w_ff)
        mixed = tokens[0].astype(F32) + net.ctx_collect(outs.reshape(n, rows, dim))

    scale2 = rms_scale(mixed)
    normed2 = (mixed * scale2 * gain_second).astype(BF16)
    mate = [(i, i ^ 1) for i in range(n)]
    both = jnp.concatenate([normed2, lax.ppermute(normed2, "ctx", mate)], axis=0)
    gate_v, up_v = nn(both, w_g), nn(both, w_u)
    sig = jax.nn.sigmoid(gate_v)
    product = (gate_v * sig * up_v).astype(BF16)
    down_out = nn(product, w_d)
    from_mate = lax.ppermute(down_out[rows:].astype(BF16), "ctx", mate)
    layer_out = mixed + down_out[:rows] + from_mate.astype(F32)
    diff = layer_out - teacher[0].astype(F32)
    squared = jnp.sum(valid[:, None] * diff * diff)
    token_total = length * m * tokens.shape[0]
    grad_out = token_total * valid[:, None] * diff / count

    gb = grad_out.astype(BF16)
    gb_both = jnp.concatenate([gb, lax.ppermute(gb, "ctx", mate)], axis=0)
    g_prod = nt(gb_both, w_d)
    g_gate = (g_prod * up_v * (sig * (1.0 + gate_v * (1.0 - sig)))).astype(BF16)
    g_up = (g_prod * gate_v * sig).astype(BF16)
    if net.direct:
        g_ff = ff_gradients(m, both, product, g_gate, g_up, gb_both)
    else:
        g_ff = jnp.concatenate(
            [
                tn(both, g_gate).reshape(m, ff_rows, dim),
                tn(both, g_up).reshape(m, ff_rows, dim),
                tn(product, gb_both).reshape(m, ff_half, dim),
            ],
            axis=1,
        ).astype(BF16)
    g_n2 = nt(tie(g_gate, g_ff), w_g) + nt(g_up, w_u)
    from_mate = lax.ppermute(g_n2[rows:].astype(BF16), "ctx", mate)
    grad_n2 = g_n2[:rows] + from_mate.astype(F32)
    part = rms_back(mixed, gain_second, scale2, grad_n2)
    grad_mixed = grad_out + part

    gm = net.ctx_all(grad_mixed.astype(BF16))
    gm = gm.reshape(length, dim)
    g_ff = lax.psum_scatter(g_ff, "fsdp", scatter_dimension=0, tiled=False)

    g_ym = nt(gm, w_mamba)
    inner = jnp.sum(gated * (g_ym * gain_mamba), axis=1).reshape(-1, 128)

    def outs_back(gm):
        g_ob = nt(gm, w_attn).astype(BF16)
        g_outs = jnp.concatenate(
            [
                tn(ym, gm).reshape(per, mamba_rows, dim),
                tn(attended, gm).reshape(per, out_rows - mamba_rows, dim),
            ],
            axis=1,
        )
        return g_ob, g_outs.astype(BF16)

    def attend_back(qkv, g_ob):
        return attn_backward(q_heads, (qkv, seg_c, seg_r), lse, g_ob, cosine, sine)

    def plus(here, got):
        return (here.astype(F32) + got.astype(F32)).astype(BF16)

    if net.direct:
        (g_ob, g_outs), (got,) = stage(outs_back, (gm,), [(net.flip_core, inner)])
        inner = inner + got
        here = lax.dynamic_index_in_dim(g_outs, net.y, 0, False)
        away = lax.dynamic_index_in_dim(g_outs, 1 - net.y, 0, False)
        got = net.flip_y(away)
        g_qkv, (got_x,) = stage(attend_back, (qkv, g_ob), [(net.flip_x, inner)])
        inner = inner + got_x
        out_both = plus(here, got).reshape(4, out_rows // 4, dim)
    else:
        g_ob, g_outs = outs_back(gm)
        inner = net.ctx_sum(inner)
        g_qkv = attend_back(qkv, g_ob)
    inner = inner.reshape(length, 1) / wide
    stats = jnp.concatenate([scale_m, scale_m * scale_m * scale_m * inner], axis=1)
    g_gated = stats[:, :1] * (g_ym * gain_mamba) - gated * stats[:, 1:]
    sig_z = jax.nn.sigmoid(gate_z)
    g_z = (g_gated * ssm_y * (sig_z + gate_z * sig_z * (1.0 - sig_z))).astype(BF16)
    early = jnp.concatenate([g_z, g_qkv], axis=1)
    grad_early = tn(normed, early).reshape(m, shard, width + slab)

    def ssm_back(states):
        return ssm_backward(
            heads,
            ssm_in,
            states,
            gate_z,
            g_ym,
            ssm_y,
            stats,
            gain_mamba,
            pre,
            cin,
            up,
            taps,
            params,
        )

    if net.direct:
        here, away = net.halves_y(grad_early)
        (g_late, g_conv, g_wide, g_steps), (got, out_parts) = stage(
            ssm_back, (states,), [(net.flip_y, away), (net.shifts_z, out_both)]
        )
        grad_early = plus(here, got)
        out_quarter = sum(p.astype(F32) for p in out_parts).astype(BF16)
    else:
        g_late, g_conv, g_wide, g_steps = ssm_back(states)

    def to_wide(values, at, size):
        out = jnp.zeros(values.shape[:-1] + (size,), F32)
        return lax.dynamic_update_slice_in_dim(out, values, at, values.ndim - 1)

    def for_shards(values):
        values = jnp.concatenate(
            [to_wide(values[:, :width], c * width, wide), values[:, width:]], axis=1
        )
        values = values.reshape((-1, m, values.shape[-1] // m))
        return jnp.transpose(values, (1, 0, 2))

    conv_rows = (conv_b.shape[0] + 127) // 128
    heads_grads = jnp.stack(
        [
            to_wide(g_steps[0, :heads], c * heads, MH),
            to_wide(g_steps[1, :heads], c * heads, MH),
            to_wide(jnp.sum(g_wide[0].reshape(heads, HP), axis=1), c * heads, MH),
            jnp.full((MH,), squared),
        ]
    )
    laid = [jax.vmap(lay)(for_shards(g_conv[: KW + 1]))]
    laid.append(jnp.broadcast_to(lay(heads_grads)[None], (m, 4, 128)))
    laid = jnp.concatenate(laid, axis=1)
    late_size = conv_width + 128
    grad_late = tn(normed, g_late).reshape(m, shard, late_size)
    if net.direct:
        laid = jnp.swapaxes(laid, 1, 2)
        ends_at = conv_width + at_small
        grad_late = jnp.concatenate(
            [grad_late[..., :ends_at], laid, grad_late[..., ends_at + laid.shape[2] :]], axis=2
        )
    grad_late = grad_late.astype(BF16)
    resid = tokens[0].astype(F32)

    def normed_back(early, g_late):
        return (nt(early, w_second) + nt(g_late, w_first)).reshape(n, rows, dim)

    def tokens_back(grad_normed):
        return grad_mixed + rms_back(resid, gain_input, rms_scale(resid), grad_normed)

    if net.direct:
        g_normed = normed_back(early, g_late)
        here, away = net.halves_y(grad_late)
        _, (grad_normed, got, early_parts) = stage(
            tuple,
            (),
            [
                (net.ctx_collect, g_normed),
                (net.flip_y, away),
                (net.shifts_z, grad_early),
            ],
        )
        grad_early = sum(p.astype(F32) for p in early_parts).astype(BF16)
        blocks = net.blocks_z(plus(here, got))
        g_ff = tie(g_ff, grad_early, *blocks)
        got_ff = net.flip_x(g_ff)
        grad_tokens, (late_parts, out_quarter), (got_ff,) = stage(
            tokens_back,
            (grad_normed,),
            [(net.send_z, blocks), (net.cross, out_quarter)],
            (got_ff,),
        )
        g_ff = plus(g_ff, got_ff)
        grad_late = sum(p.astype(F32) for p in late_parts).astype(BF16)
        joined = jnp.concatenate([out_quarter[:, : dim // 2], out_quarter[:, dim // 2 :]], axis=0)
        joined = jnp.concatenate([grad_early, joined], axis=1)
        joined = jnp.concatenate([grad_late, joined], axis=1)
        def finish_halves(g_ff, got_ff):
            return finish_ff(net.core, g_ff, got_ff, w_gate, w_up, gain_ffn)

        ff_out, (across,) = stage(
            finish_halves, (g_ff, net.flip_core(g_ff)), [(net.flip_x, joined)]
        )
        out_gate, out_up, out_down, out_gain_ffn = ff_out
        joined = jnp.stack([joined, across])
        mates = net.flip_core(joined)
        place = jnp.stack([net.x, net.core]).astype(jnp.int32)
        out_w_in, out_w_qkv, out_mamba, out_attn, out_gain_in, out_gain_m, totals = finish(
            place, joined, mates, w_in, w_qkv, w_out, w_o, gain_in, gain_m
        )
        totals = totals[at_small : at_small + laid.shape[2]]
    else:
        grad_tokens = tokens_back(net.ctx_collect(normed_back(early, g_late)))
        got_early = net.ctx_all(net.collect(grad_early)).astype(F32)
        got_late = net.ctx_all(net.collect(grad_late))
        out_outs = net.rows_back(g_outs).astype(F32)
        got_ff = net.over_cores(g_ff)
        got_late = got_late.astype(F32)
        totals = lax.psum_scatter(laid, "fsdp", scatter_dimension=0, tiled=False)
        totals = lax.psum(totals, "ctx")
        def side(got, start, size):
            return [got[j][:, start : start + size] for j in range(n)]

        shared = n // KVH
        out_w_in = jnp.concatenate(
            side(got_early, 0, width)
            + side(got_late, 0, width)
            + [sum(side(got_late, width, 2 * NS))]
            + side(got_late, conv_width, heads),
            axis=1,
        )
        out_w_qkv = jnp.concatenate(
            side(got_early, width, q_width)
            + [
                sum(side(got_early, width + q_width + i * HD, HD)[k * shared : (k + 1) * shared])
                for i in range(2)
                for k in range(KVH)
            ],
            axis=1,
        )

        def ff_wide(values):
            values = values.reshape(2, shard, m, ff_half)
            return jnp.transpose(values, (1, 2, 0, 3)).reshape(shard, ff)

        out_gate = ff_wide(got_ff[:, :ff_rows])
        out_up = ff_wide(got_ff[:, ff_rows : 2 * ff_rows])
        out_mamba = out_outs[:mamba_rows]

        def along(*pairs):
            return sum(jnp.sum(w.astype(F32) * g, axis=1) for w, g in pairs)

        out_attn = out_outs[mamba_rows:]
        out_down = got_ff[:, 2 * ff_rows :].reshape(ff_shard, dim)
        out_gain_in = along((w_in, out_w_in), (w_qkv, out_w_qkv)) / gain_in.astype(F32)
        out_gain_m = along((w_out, out_mamba)) / gain_m.astype(F32)
        out_gain_ffn = along((w_gate, out_gate), (w_up, out_up)) / gain_ffn.astype(F32)
    grad_conv = unlay(totals, 0, KW + 1, conv_b.shape[0])
    head_totals = totals[(KW + 1) * conv_rows : (KW + 1) * conv_rows + 4, :MH]
    loss = head_totals[3, 0] / (2.0 * count)
    return (
        loss,
        layer_out[None],
        grad_tokens[None],
        out_gain_in,
        out_w_in,
        grad_conv[:KW],
        grad_conv[KW],
        head_totals[0],
        head_totals[1],
        head_totals[2],
        out_gain_m,
        out_mamba,
        out_w_qkv,
        out_attn,
        out_gain_ffn,
        out_gate,
        out_up,
        out_down,
    )


def solution(mesh):
    in_specs = (
        P("fsdp", "ctx", None),
        P("fsdp", "ctx", None),
        P("fsdp", None),
        P("fsdp", "ctx"),
        P("fsdp"),
        P("fsdp", None),
        P(None, "fsdp"),
        P("fsdp"),
        P(),
        P(),
        P(),
        P("fsdp"),
        P("fsdp", None),
        P("fsdp", None),
        P("fsdp", None),
        P("fsdp"),
        P("fsdp", None),
        P("fsdp", None),
        P("fsdp", None),
    )
    out_specs = (
        P(),
        P("fsdp", "ctx", None),
        P("fsdp", "ctx", None),
        P("fsdp"),
        P("fsdp", None),
        P(None, "fsdp"),
        P("fsdp"),
        P(),
        P(),
        P(),
        P("fsdp"),
        P("fsdp", None),
        P("fsdp", None),
        P("fsdp", None),
        P("fsdp"),
        P("fsdp", None),
        P("fsdp", None),
        P("fsdp", None),
    )
    return jax.shard_map(
        per_device, mesh=mesh, in_specs=in_specs, out_specs=out_specs, check_vma=False
    )
```

```python
import functools

import jax
import jax.numpy as jnp
import numpy as np
from jax import lax
from jax.experimental import pallas as pl
from jax.experimental.pallas import tpu as pltpu
from jax.sharding import PartitionSpec as P

MH = 24
HP = 64
NS = 128
KW = 4
QH = 8
KVH = 2
HD = 64
SPAN = 128
QBLK = 256

EPSILON = 1e-05
ROPE_BASE = 100000000000.0
MASKED = -1e30

F32 = jnp.float32
BF16 = jnp.bfloat16
HIGH = lax.Precision.HIGHEST


def nn(left, right, precision=None):
    return lax.dot_general(
        left, right, (((1,), (0,)), ((), ())), precision=precision, preferred_element_type=F32
    )


def nt(left, right):
    return lax.dot_general(left, right, (((1,), (1,)), ((), ())), preferred_element_type=F32)


def tn(left, right):
    return lax.dot_general(left, right, (((0,), (0,)), ((), ())), preferred_element_type=F32)


def swap_halves(values):
    lane = lax.broadcasted_iota(jnp.int32, values.shape, 1) % HD
    size = values.shape[1]
    return jnp.where(
        lane < HD // 2,
        pltpu.roll(values, size - HD // 2, 1),
        pltpu.roll(values, HD // 2, 1),
    )


def conv_kernel(
    tok, gain, weight, taps, bias, same, params, normed_ref, cin_ref, pre_ref, act_ref, step_ref,
    row_ref, halo,
):
    conv = taps.shape[1]
    block = tok.shape[0]

    @pl.when(pl.program_id(0) == 0)
    def _():
        halo[...] = jnp.zeros_like(halo)

    values = tok[...].astype(F32)
    scale = lax.rsqrt(jnp.mean(values * values, axis=-1, keepdims=True) + EPSILON)
    normed = (values * scale * gain[...]).astype(BF16)
    normed_ref[...] = normed
    cin = nn(normed, weight[:, :conv])
    cin_ref[...] = cin.astype(BF16)
    halo[8 : 8 + block, :] = cin
    pre = bias[...] + taps[KW - 1 : KW, :] * cin
    for by in range(1, KW):
        tap = taps[KW - 1 - by : KW - by, :]
        pre = pre + tap * halo[8 - by : 8 - by + block, :] * same[:, by : by + 1]
    halo[0:8, :] = halo[block : block + 8, :]
    pre_ref[...] = pre.astype(BF16)
    act_ref[...] = (pre * jax.nn.sigmoid(pre)).astype(BF16)
    raw = nn(normed, weight[:, conv:]) + params[0:1, :]
    dt = jnp.maximum(raw, 0.0) + jnp.log1p(jnp.exp(-jnp.abs(raw)))
    loga = -dt * params[1:2, :]
    step_ref[:, :128] = dt
    step_ref[:, 128:] = loga
    row_ref[0:8, :] = jnp.transpose(dt)[0:8, :]
    row_ref[8:16, :] = jnp.transpose(loga)[0:8, :]


def by_rows(size):
    return pl.BlockSpec((QBLK, size), lambda i: (i, 0))


def whole(a):
    return pl.BlockSpec(a.shape, lambda i: (0, 0))


def project_conv(tokens, gain, weight, taps, bias, same, params):
    length, dim = tokens.shape
    conv = taps.shape[1]
    sizes = [(dim, BF16), (conv, BF16), (conv, BF16), (conv, BF16), (256, F32)]
    return pl.pallas_call(
        conv_kernel,
        grid=(length // QBLK,),
        in_specs=[
            by_rows(dim),
            whole(gain),
            whole(weight),
            whole(taps),
            whole(bias),
            by_rows(same.shape[1]),
            whole(params),
        ],
        out_specs=[by_rows(size) for size, _ in sizes]
        + [pl.BlockSpec((16, QBLK), lambda i: (0, i))],
        out_shape=[jax.ShapeDtypeStruct((length, size), kind) for size, kind in sizes]
        + [jax.ShapeDtypeStruct((16, length), F32)],
        scratch_shapes=[pltpu.VMEM((QBLK + 8, conv), F32)],
        compiler_params=pltpu.CompilerParams(vmem_limit_bytes=40 * 1024 * 1024),
        cost_estimate=pl.CostEstimate(
            flops=2 * length * dim * weight.shape[1], bytes_accessed=10**7, transcendentals=10**6
        ),
        name="project_conv",
    )(tokens, gain, weight, taps, bias, same, params)


def gate_kernel(normed_ref, weight, y_ref, cosine, sine, z_ref, qkv_ref, sq_ref):
    width = y_ref.shape[1]
    normed = normed_ref[...]
    gate = nn(normed, weight[:, :width])
    z_ref[...] = gate
    qkv = nn(normed, weight[:, width:])
    qkv_ref[...] = (qkv * cosine[...] + swap_halves(qkv) * sine[...]).astype(BF16)
    gated = y_ref[...] * (gate * jax.nn.sigmoid(gate))
    sq_ref[...] = lax.dot_general(
        jnp.ones((8, width), F32),
        gated * gated,
        (((1,), (1,)), ((), ())),
        precision=HIGH,
        preferred_element_type=F32,
    )


def project_gate(normed, weight, y, cosine, sine):
    length, dim = normed.shape
    width = y.shape[1]
    slab = cosine.shape[1]
    return pl.pallas_call(
        gate_kernel,
        grid=(length // QBLK,),
        in_specs=[by_rows(dim), whole(weight), by_rows(width), by_rows(slab), by_rows(slab)],
        out_specs=[
            by_rows(width),
            by_rows(slab),
            pl.BlockSpec((8, QBLK), lambda i: (0, i)),
        ],
        out_shape=[
            jax.ShapeDtypeStruct((length, width), F32),
            jax.ShapeDtypeStruct((length, slab), BF16),
            jax.ShapeDtypeStruct((8, length), F32),
        ],
        compiler_params=pltpu.CompilerParams(vmem_limit_bytes=40 * 1024 * 1024),
        cost_estimate=pl.CostEstimate(
            flops=2 * length * dim * weight.shape[1], bytes_accessed=10**7, transcendentals=10**6
        ),
        name="project_gate",
    )(normed, weight, y, cosine, sine)


def decays(seg_c, seg_r, loga_c, loga_r, before, end):
    row = lax.broadcasted_iota(jnp.int32, (SPAN, SPAN), 0)
    col = lax.broadcasted_iota(jnp.int32, (SPAN, SPAN), 1)
    lower = row >= col
    same = (seg_c == seg_r) & lower
    run_c = nn(lower.astype(F32), loga_c, HIGH)
    run_r = nn(loga_r, (row <= col).astype(F32), HIGH)
    keep = (seg_c == before).astype(F32)
    tail = (seg_c == end).astype(F32)
    return row, col, same, run_c, run_r, keep, tail


def head_groups(heads):
    return [tuple(range(g, min(g + 2, heads))) for g in range(0, heads, 2)]


def by_lane(columns, group, size):
    first = columns[:, group[0] : group[0] + 1]
    if len(group) == 1:
        return first
    lane = lax.broadcasted_iota(jnp.int32, (columns.shape[0], size), 1)
    return jnp.where(lane < HP, first, columns[:, group[1] : group[1] + 1])


def stacked(values, group):
    if len(group) == 1:
        return values
    lane = lax.broadcasted_iota(jnp.int32, values.shape, 1)
    zero = jnp.zeros_like(values)
    return jnp.concatenate(
        [jnp.where(lane < HP, values, zero), jnp.where(lane < HP, zero, values)], axis=0
    )


def ssm_fwd_kernel(
    heads, ends, skip, act, steps, rows, seg_c, seg_r, y_ref, st_ref, state, weighted
):
    step = pl.program_id(0)

    @pl.when(step == 0)
    def _():
        state[...] = jnp.zeros_like(state)

    before, end = ends[step], ends[step + 1]
    link = (before == end).astype(F32)
    _, _, same, run_c, run_r, keep, tail = decays(
        seg_c[...], seg_r[...], steps[:, 128:], rows[8:16, :], before, end
    )
    width = heads * HP
    b_in = act[:, width : width + NS]
    c_in = act[:, width + NS : width + 2 * NS]
    gram = nt(c_in, b_in)
    last = run_c[SPAN - 1 :, :]
    carry_w = jnp.exp(run_c) * keep
    end_w = jnp.exp(last - run_c) * tail * steps[:, :128]
    prior = state[...]
    st_ref[0] = prior
    from_state = nt(c_in, prior.astype(BF16))
    for group in head_groups(heads):
        size = len(group) * HP
        lanes = slice(group[0] * HP, group[0] * HP + size)
        x_in = act[:, lanes]
        x_wide = x_in.astype(F32)
        mixing = []
        for h in group:
            decay = jnp.where(same, jnp.exp(run_c[:, h : h + 1] - run_r[h : h + 1, :]), 0.0)
            mixing.append((gram * decay * rows[h : h + 1, :]).astype(BF16))
        y_in = nn(jnp.concatenate(mixing, axis=1), stacked(x_in, group))
        skips = [skip[h] for h in group]
        lane = lax.broadcasted_iota(jnp.int32, (1, size), 1)
        skip_w = jnp.where(lane < HP, skips[0], skips[-1])
        y_ref[:, lanes] = (
            y_in + from_state[:, lanes] * by_lane(carry_w, group, size) + skip_w * x_wide
        )
        weighted[:, lanes] = (x_wide * by_lane(end_w, group, size)).astype(BF16)
    local = tn(weighted[...], b_in)
    for h in range(heads):
        part = slice(h * HP, (h + 1) * HP)
        state[part, :] = (jnp.exp(last[:, h : h + 1]) * link) * prior[part, :] + local[part, :]


def ssm_bwd_kernel(
    heads,
    ends,
    skip,
    act,
    steps,
    rows,
    seg_c,
    seg_r,
    st_ref,
    z_ref,
    gym_ref,
    y_ref,
    stat_ref,
    gain_ref,
    pre_ref,
    cin_ref,
    up_ref,
    taps,
    params,
    first_ref,
    gconv_ref,
    gwide_ref,
    gstep_ref,
    gstate,
    gbuf,
    grow,
    carried,
    ended,
):
    step = pl.num_programs(0) - 1 - pl.program_id(0)
    width = heads * HP
    conv = width + 2 * NS

    @pl.when(pl.program_id(0) == 0)
    def _():
        gstate[...] = jnp.zeros_like(gstate)
        gbuf[...] = jnp.zeros_like(gbuf)
        grow[...] = jnp.zeros_like(grow)
        gconv_ref[...] = jnp.zeros_like(gconv_ref)
        gwide_ref[...] = jnp.zeros_like(gwide_ref)
        gstep_ref[...] = jnp.zeros_like(gstep_ref)

    before, end = ends[step], ends[step + 1]
    link = (before == end).astype(F32)
    row, col, same, run_c, run_r, keep, tail = decays(
        seg_c[...], seg_r[...], steps[:, 128:], rows[8:16, :], before, end
    )
    gate = z_ref[...]
    silu = gate * jax.nn.sigmoid(gate)
    gated = y_ref[...] * silu
    g_gated = stat_ref[:, 0:1] * (gym_ref[...] * gain_ref[...]) - gated * stat_ref[:, 1:2]
    g_all = g_gated * silu
    x_all = act[:, :width].astype(F32)
    gwide_ref[0:1, :] += jnp.sum(g_all * x_all, axis=0, keepdims=True)

    b_in = act[:, width : width + NS]
    c_in = act[:, width + NS : width + 2 * NS]
    gram = nt(c_in, b_in)
    last = run_c[SPAN - 1 :, :]
    carry_w = jnp.exp(run_c) * keep
    tail_w = jnp.exp(last - run_c) * tail
    end_w = tail_w * steps[:, :128]
    prior = st_ref[0]
    prior_low = prior.astype(BF16)
    after = gstate[...]
    after_low = after.astype(BF16)
    from_prior = nt(c_in, prior_low)
    from_after = nt(b_in, after_low)
    g_gram = jnp.zeros((SPAN, SPAN), F32)
    row_sums = jnp.zeros((SPAN, SPAN), F32)
    for group in head_groups(heads):
        size = len(group) * HP
        lanes = slice(group[0] * HP, group[0] * HP + size)
        gy = g_all[:, lanes]
        gy_parts = stacked(gy.astype(BF16), group)
        g_mixes = nt(gy_parts, act[:, lanes])
        mixing = []
        for i, h in enumerate(group):
            dt_row = rows[h : h + 1, :]
            decay = jnp.where(same, jnp.exp(run_c[:, h : h + 1] - run_r[h : h + 1, :]), 0.0)
            mixing.append((gram * decay * dt_row).astype(BF16))
            g_mix = g_mixes[i * SPAN : (i + 1) * SPAN, :] * decay
            g_gram_h = g_mix * dt_row
            g_gram = g_gram + g_gram_h
            sums = jnp.sum(g_gram_h * gram, axis=1, keepdims=True)
            row_sums = jnp.where(col == h, sums, row_sums)
            by_key = jnp.sum(g_mix * gram, axis=0, keepdims=True)
            grow[h : h + 1, :] = by_key * dt_row
            grow[128 + h : 128 + h + 1, :] = by_key
        skips = [skip[h] for h in group]
        lane = lax.broadcasted_iota(jnp.int32, (1, size), 1)
        skip_w = jnp.where(lane < HP, skips[0], skips[-1])
        end_l = by_lane(end_w, group, size)
        gbuf[0:SPAN, lanes] = (
            tn(jnp.concatenate(mixing, axis=0), gy_parts)
            + from_after[:, lanes] * end_l
            + skip_w * gy
        )
        carried[:, lanes] = (gy * by_lane(carry_w, group, size)).astype(BF16)
        ended[:, lanes] = (x_all[:, lanes] * end_l).astype(BF16)
    of_head = (
        lax.broadcasted_iota(jnp.int32, (width, 128), 0) // HP
        == lax.broadcasted_iota(jnp.int32, (width, 128), 1)
    ).astype(BF16)

    def head_sums(values):
        high = values.astype(BF16)
        return nn(high, of_head) + nn((values - high.astype(F32)).astype(BF16), of_head)

    g_carry = head_sums(g_all * from_prior)
    g_tail = head_sums(x_all * from_after)
    state_sums = jnp.sum(after * prior, axis=1, keepdims=True)
    of_head_t = (
        lax.broadcasted_iota(jnp.int32, (width, 128), 0) // HP
        == lax.broadcasted_iota(jnp.int32, (width, 128), 1)
    )
    state_sums = jnp.sum(jnp.where(of_head_t, state_sums, 0.0), axis=0, keepdims=True)
    g_end = g_tail * end_w
    g_link = jnp.exp(last) * link
    total_last = jnp.sum(g_end, axis=0, keepdims=True) + g_link * state_sums
    g_run = row_sums + g_carry * carry_w - g_end + jnp.where(row == SPAN - 1, total_last, 0.0)
    weighted = carried[...]
    g_gram_low = g_gram.astype(BF16)
    gbuf[0:SPAN, width : width + NS] = nn(ended[...], after_low) + tn(g_gram_low, c_in)
    gbuf[0:SPAN, width + NS :] = nn(weighted, prior_low) + nn(g_gram_low, b_in)
    to_state = tn(weighted, c_in)
    for h in range(heads):
        part = slice(h * HP, (h + 1) * HP)
        gstate[part, :] = g_link[:, h : h + 1] * after[part, :] + to_state[part, :]

    pre = pre_ref[...].astype(F32)
    sig = jax.nn.sigmoid(pre)
    g_pre = gbuf[0:SPAN, :] * (sig + pre * sig * (1.0 - sig))
    gbuf[0:SPAN, :] = g_pre
    cin = cin_ref[...].astype(F32)
    g_conv = taps[KW - 1 : KW, :] * g_pre
    gconv_ref[KW - 1 : KW, :] += jnp.sum(g_pre * cin, axis=0, keepdims=True)
    gconv_ref[KW : KW + 1, :] += jnp.sum(g_pre, axis=0, keepdims=True)
    for by in range(1, KW):
        ahead = gbuf[by : by + SPAN, :] * up_ref[:, by : by + 1]
        tap = KW - 1 - by
        g_conv = g_conv + taps[tap : tap + 1, :] * ahead
        gconv_ref[tap : tap + 1, :] += jnp.sum(ahead * cin, axis=0, keepdims=True)
    gbuf[SPAN : SPAN + 8, :] = gbuf[0:8, :]
    first_ref[:, :conv] = g_conv.astype(BF16)

    later = (col >= row).astype(F32)
    eye = (col == row).astype(F32)

    def across(left, right):
        return lax.dot_general(
            left, right, (((1,), (1,)), ((), ())), precision=HIGH, preferred_element_type=F32
        )

    g_loga = nn(later, g_run, HIGH) - across(later, grow[:128, :])
    g_dt = g_tail * tail_w + across(eye, grow[128:, :]) - g_loga * params[1:2, :]
    g_step = g_dt * (1.0 - jnp.exp(-steps[:, :128]))
    first_ref[:, conv:] = g_step.astype(BF16)
    gstep_ref[0:1, :] += jnp.sum(g_step, axis=0, keepdims=True)
    gstep_ref[1:2, :] += jnp.sum(g_loga * steps[:, 128:], axis=0, keepdims=True)


def ssm_specs(heads, at):
    width = heads * HP
    return [
        pl.BlockSpec(memory_space=pltpu.SMEM),
        pl.BlockSpec(memory_space=pltpu.SMEM),
        pl.BlockSpec((SPAN, width + 2 * NS), lambda i: (at(i), 0)),
        pl.BlockSpec((SPAN, 256), lambda i: (at(i), 0)),
        pl.BlockSpec((16, SPAN), lambda i: (0, at(i))),
        pl.BlockSpec((SPAN, 1), lambda i: (at(i), 0)),
        pl.BlockSpec((1, SPAN), lambda i: (0, at(i))),
    ]


def ssm_forward(heads, inputs):
    length = inputs[2].shape[0]
    steps = length // SPAN
    width = heads * HP
    return pl.pallas_call(
        functools.partial(ssm_fwd_kernel, heads),
        grid=(steps,),
        in_specs=ssm_specs(heads, lambda i: i),
        out_specs=[
            pl.BlockSpec((SPAN, width), lambda i: (i, 0)),
            pl.BlockSpec((1, width, NS), lambda i: (i, 0, 0)),
        ],
        out_shape=[
            jax.ShapeDtypeStruct((length, width), F32),
            jax.ShapeDtypeStruct((steps, width, NS), F32),
        ],
        scratch_shapes=[pltpu.VMEM((width, NS), F32), pltpu.VMEM((SPAN, width), BF16)],
        compiler_params=pltpu.CompilerParams(vmem_limit_bytes=32 * 1024 * 1024),
        cost_estimate=pl.CostEstimate(
            flops=10**9, bytes_accessed=4 * 10**7, transcendentals=10**6
        ),
        name="ssm_forward",
    )(*inputs)


def ssm_backward(heads, inputs, states, gate_z, g_ym, ssm_y, stats, gain, pre, cin, up, taps, params):
    length = inputs[2].shape[0]
    steps = length // SPAN
    width = heads * HP
    conv = width + 2 * NS
    total = conv + 128

    def at(i):
        return steps - 1 - i

    def part(size):
        return pl.BlockSpec((SPAN, size), lambda i: (at(i), 0))

    def fixed(shape):
        return pl.BlockSpec(shape, lambda i: (0, 0))

    return pl.pallas_call(
        functools.partial(ssm_bwd_kernel, heads),
        grid=(steps,),
        in_specs=ssm_specs(heads, at)
        + [
            pl.BlockSpec((1, width, NS), lambda i: (at(i), 0, 0)),
            part(width),
            part(width),
            part(width),
            part(stats.shape[1]),
            fixed(gain.shape),
            part(conv),
            part(conv),
            part(up.shape[1]),
            fixed(taps.shape),
            fixed(params.shape),
        ],
        out_specs=[part(total), fixed((8, conv)), fixed((8, width)), fixed((8, 128))],
        out_shape=[
            jax.ShapeDtypeStruct((length, total), BF16),
            jax.ShapeDtypeStruct((8, conv), F32),
            jax.ShapeDtypeStruct((8, width), F32),
            jax.ShapeDtypeStruct((8, 128), F32),
        ],
        scratch_shapes=[
            pltpu.VMEM((width, NS), F32),
            pltpu.VMEM((SPAN + 8, conv), F32),
            pltpu.VMEM((256, SPAN), F32),
            pltpu.VMEM((SPAN, width), BF16),
            pltpu.VMEM((SPAN, width), BF16),
        ],
        compiler_params=pltpu.CompilerParams(vmem_limit_bytes=56 * 1024 * 1024),
        cost_estimate=pl.CostEstimate(
            flops=10**7, bytes_accessed=10**6, transcendentals=10**4
        ),
        name="ssm_backward",
    )(*inputs, states, gate_z, g_ym, ssm_y, stats, gain, pre, cin, up, taps, params)


def allowed_keys(index, reach, seg_c, seg_r):
    row = lax.broadcasted_iota(jnp.int32, (QBLK, reach), 0) + index * QBLK
    col = lax.broadcasted_iota(jnp.int32, (QBLK, reach), 1)
    return (seg_c[...] == seg_r[:, :reach]) & (col <= row)


def attn_fwd_kernel(heads, blocks, qkv_ref, seg_c, seg_r, out_ref, lse_ref):
    wide = heads * HD
    for index in range(blocks):

        @pl.when(pl.program_id(0) == index)
        def _(index=index):
            reach = (index + 1) * QBLK
            allowed = allowed_keys(index, reach, seg_c, seg_r)
            own = slice(index * QBLK, reach)
            keys = qkv_ref[:reach, wide : wide + HD]
            values = qkv_ref[:reach, wide + HD : wide + 2 * HD]
            for h in range(heads):
                lanes = slice(h * HD, (h + 1) * HD)
                scores = nt(qkv_ref[own, lanes], keys) * (HD**-0.5)
                scores = jnp.where(allowed, scores, MASKED)
                top = jnp.max(scores, axis=1, keepdims=True)
                expo = jnp.exp(scores - top)
                total = jnp.sum(expo, axis=1, keepdims=True)
                probs = (expo * (1.0 / total)).astype(BF16)
                out_ref[:, lanes] = nn(probs, values).astype(BF16)
                lse_ref[:, h : h + 1] = top + jnp.log(total)


def attn_bwd_kernel(
    heads, blocks, qkv_ref, seg_c, seg_r, lse_ref, go_ref, cosine, sine, out_ref, grads
):
    wide = heads * HD

    @pl.when(pl.program_id(0) == 0)
    def _():
        grads[...] = jnp.zeros_like(grads)

    for index in range(blocks):

        @pl.when(pl.program_id(0) == index)
        def _(index=index):
            reach = (index + 1) * QBLK
            allowed = allowed_keys(index, reach, seg_c, seg_r)
            own = slice(index * QBLK, reach)
            keys = qkv_ref[:reach, wide : wide + HD]
            values = qkv_ref[:reach, wide + HD : wide + 2 * HD]
            for h in range(heads):
                lanes = slice(h * HD, (h + 1) * HD)
                query = qkv_ref[own, lanes]
                g_out = go_ref[:, lanes]
                scores = nt(query, keys) * (HD**-0.5)
                probs = jnp.where(allowed, jnp.exp(scores - lse_ref[:, h : h + 1]), 0.0)
                g_probs = nt(g_out, values)
                delta = jnp.sum(probs * g_probs, axis=1, keepdims=True)
                g_scores = (probs * (g_probs - delta)).astype(BF16)
                grads[own, lanes] = nn(g_scores, keys) * (HD**-0.5)
                grads[:reach, wide : wide + HD] += tn(g_scores, query) * (HD**-0.5)
                grads[:reach, wide + HD : wide + 2 * HD] += tn(probs.astype(BF16), g_out)
            if index == blocks - 1:
                for b in range(blocks):
                    part = slice(b * QBLK, (b + 1) * QBLK)
                    slab = grads[part, :]
                    out_ref[part, :] = (
                        slab * cosine[part, :] - swap_halves(slab) * sine[part, :]
                    ).astype(BF16)


def attn_specs(length, slab):
    return [
        pl.BlockSpec((length, slab), lambda i: (0, 0)),
        pl.BlockSpec((QBLK, 1), lambda i: (i, 0)),
        pl.BlockSpec((1, length), lambda i: (0, 0)),
    ]


def attn_forward(heads, inputs):
    length, slab = inputs[0].shape
    blocks = length // QBLK
    return pl.pallas_call(
        functools.partial(attn_fwd_kernel, heads, blocks),
        grid=(blocks,),
        in_specs=attn_specs(length, slab),
        out_specs=[
            pl.BlockSpec((QBLK, heads * HD), lambda i: (i, 0)),
            pl.BlockSpec((QBLK, heads), lambda i: (i, 0)),
        ],
        out_shape=[
            jax.ShapeDtypeStruct((length, heads * HD), BF16),
            jax.ShapeDtypeStruct((length, heads), F32),
        ],
        compiler_params=pltpu.CompilerParams(vmem_limit_bytes=32 * 1024 * 1024),
        cost_estimate=pl.CostEstimate(
            flops=10**9, bytes_accessed=2 * 10**7, transcendentals=10**6
        ),
        name="attn_forward",
    )(*inputs)


def attn_backward(heads, inputs, lse, g_out, cosine, sine):
    length, slab = inputs[0].shape
    blocks = length // QBLK
    full = pl.BlockSpec((length, slab), lambda i: (0, 0))
    return pl.pallas_call(
        functools.partial(attn_bwd_kernel, heads, blocks),
        grid=(blocks,),
        in_specs=attn_specs(length, slab)
        + [
            pl.BlockSpec((QBLK, heads), lambda i: (i, 0)),
            pl.BlockSpec((QBLK, heads * HD), lambda i: (i, 0)),
            full,
            full,
        ],
        out_specs=full,
        out_shape=jax.ShapeDtypeStruct((length, slab), BF16),
        scratch_shapes=[pltpu.VMEM((length, slab), F32)],
        compiler_params=pltpu.CompilerParams(vmem_limit_bytes=56 * 1024 * 1024),
        cost_estimate=pl.CostEstimate(
            flops=10**7, bytes_accessed=10**6, transcendentals=10**4
        ),
        name="attn_backward",
    )(*inputs, lse, g_out, cosine, sine)


def ff_kernel(both, product, g_gate, g_up, gb, out):
    rows = both.shape[1]
    out[0, :rows] = tn(both[...], g_gate[...]).astype(BF16)
    out[0, rows : 2 * rows] = tn(both[...], g_up[...]).astype(BF16)
    out[0, 2 * rows :] = tn(product[...], gb[...]).astype(BF16)


def ff_gradients(m, both, product, g_gate, g_up, gb):
    tokens, dim = both.shape
    rows, down = dim // m, product.shape[1] // m
    full = pl.BlockSpec((tokens, dim), lambda i: (0, 0))
    return pl.pallas_call(
        ff_kernel,
        grid=(m,),
        in_specs=[
            pl.BlockSpec((tokens, rows), lambda i: (0, i)),
            pl.BlockSpec((tokens, down), lambda i: (0, i)),
            full,
            full,
            full,
        ],
        out_specs=pl.BlockSpec((1, 2 * rows + down, dim), lambda i: (i, 0, 0)),
        out_shape=jax.ShapeDtypeStruct((m, 2 * rows + down, dim), BF16),
        compiler_params=pltpu.CompilerParams(vmem_limit_bytes=40 * 1024 * 1024),
        cost_estimate=pl.CostEstimate(
            flops=6 * tokens * dim * dim, bytes_accessed=10**7, transcendentals=0
        ),
        name="ff_gradients",
    )(both, product, g_gate, g_up, gb)


def row_totals(values):
    ones = jnp.ones((8, values.shape[1]), F32)
    return lax.dot_general(
        ones, values, (((1,), (1,)), ((), ())), precision=HIGH, preferred_element_type=F32
    )


def finish_ff_kernel(core, own, mate, w_gate, w_up, gain, gate_ref, up_ref, down_ref, gain_ref):
    rows = w_gate.shape[0]
    tiles = own.shape[1] // 128
    total = jnp.zeros((rows, 128), F32)
    for half in range(2):
        mine = core[0] == half

        def pick(low, high, lanes, mine=mine):
            return jnp.where(mine, own[low:high, lanes], mate[low:high, lanes]).astype(F32)

        for f in range(tiles):
            lanes = slice(f * 128, (f + 1) * 128)
            to = slice((2 * f + half) * 128, (2 * f + half + 1) * 128)
            gate_ref[:, to] = pick(0, rows, lanes)
            up_ref[:, to] = pick(rows, 2 * rows, lanes)
        down = down_ref.shape[0] // 2
        down_ref[half * down : (half + 1) * down, :] = pick(2 * rows, 2 * rows + down, slice(None))
    for t in range(2 * tiles):
        lanes = slice(t * 128, (t + 1) * 128)
        total = total + gate_ref[:, lanes] * w_gate[:, lanes].astype(F32)
        total = total + up_ref[:, lanes] * w_up[:, lanes].astype(F32)
    gain_ref[...] = row_totals(total) / gain[...]


def finish_ff(core, own, mate, w_gate, w_up, gain):
    shard, ff = w_gate.shape
    down = own.shape[0] - 2 * shard
    vmem = pl.BlockSpec(memory_space=pltpu.VMEM)
    out = pl.pallas_call(
        finish_ff_kernel,
        in_specs=[pl.BlockSpec(memory_space=pltpu.SMEM)] + [vmem] * 5,
        out_specs=[vmem] * 4,
        out_shape=[
            jax.ShapeDtypeStruct((shard, ff), F32),
            jax.ShapeDtypeStruct((shard, ff), F32),
            jax.ShapeDtypeStruct((2 * down, own.shape[1]), F32),
            jax.ShapeDtypeStruct((8, shard), F32),
        ],
        compiler_params=pltpu.CompilerParams(vmem_limit_bytes=40 * 1024 * 1024),
        name="finish_ff",
    )(core.astype(jnp.int32)[None], own, mate, w_gate, w_up, gain.astype(F32)[None])
    return out[0], out[1], out[2], out[3][0]


def finish_kernel(
    place,
    own,
    mates,
    w_in,
    w_qkv,
    w_out,
    gain_in,
    gain_m,
    in_ref,
    qkv_ref,
    out_ref,
    o_ref,
    gain_in_ref,
    gain_m_ref,
    small_ref,
    steps,
):
    count = 2 * own.shape[0]
    shard = w_qkv.shape[0]
    heads = MH // count
    width = heads * HP
    conv = width + 2 * NS
    late = conv + 128
    q_width = QH * HD // count
    wide = count * width
    steps[...] = jnp.zeros_like(steps)
    shared = jnp.zeros((shard, 2 * NS), F32)
    gain = jnp.zeros((1, shard), F32)
    small = jnp.zeros((shard, 128), F32)
    pairs = []

    def lay(at, values, gain):
        flat = jnp.transpose(values)
        rows = slice(at, at + flat.shape[0])
        in_ref[rows, :] = flat
        return gain + jnp.sum(flat * w_in[rows, :].astype(F32), axis=0, keepdims=True)

    for j in range(count):

        at_x = (place[0] + j // 2) % 2
        mine = place[1] == j % 2

        def pick(rows, lanes, at_x=at_x, mine=mine):
            return jnp.where(mine, own[at_x, rows, lanes], mates[at_x, rows, lanes]).astype(F32)

        def part(low, high, pick=pick):
            return pick(slice(None), slice(low, high))

        gain = lay(j * width, part(late, late + width), gain)
        gain = lay(wide + j * width, part(0, width), gain)
        shared = shared + part(width, conv)
        steps[:, j * heads : (j + 1) * heads] = part(conv, conv + heads)
        at = late + width
        qkv_ref[:, j * q_width : (j + 1) * q_width] = part(at, at + q_width)
        pairs.append(part(at + q_width, at + q_width + 128))
        at = at + q_width + 128
        lanes = slice(at, own.shape[2])
        rows = pick(slice(0, shard // 2), lanes), pick(slice(shard // 2, shard), lanes)
        rows = jnp.concatenate(rows, axis=1)
        low = j * (shard // 2)
        if low < out_ref.shape[0]:
            out_ref[low : low + shard // 2, :] = rows
        else:
            low -= out_ref.shape[0]
            o_ref[low : low + shard // 2, :] = rows
        small = small + part(conv, late)
    gain = lay(2 * wide, shared, gain)
    at = 2 * wide + 2 * NS
    flat = jnp.transpose(steps[...])[: in_ref.shape[0] - at, :]
    in_ref[at:, :] = flat
    gain = gain + jnp.sum(flat * w_in[at:, :].astype(F32), axis=0, keepdims=True)
    one, two = pairs[0] + pairs[1], pairs[2] + pairs[3]
    low = lax.broadcasted_iota(jnp.int32, one.shape, 1) < HD
    at = QH * HD
    qkv_ref[:, at : at + 128] = jnp.where(low, one, pltpu.roll(two, HD, 1))
    qkv_ref[:, at + 128 :] = jnp.where(low, pltpu.roll(one, HD, 1), two)
    gain = row_totals(qkv_ref[...] * w_qkv[...].astype(F32)) + gain
    gain_in_ref[...] = gain / gain_in[...]
    gain_m_ref[...] = row_totals(out_ref[...] * w_out[...].astype(F32)) / gain_m[...]
    small_ref[...] = jnp.transpose(small)


def finish(place, own, mates, w_in, w_qkv, w_out, w_o, gain_in, gain_m):
    shard = w_qkv.shape[0]
    vmem = pl.BlockSpec(memory_space=pltpu.VMEM)
    shapes = [w_in.shape[::-1], w_qkv.shape, w_out.shape, w_o.shape]
    shapes += [(8, shard), (8, w_out.shape[0]), (128, shard)]
    out = pl.pallas_call(
        finish_kernel,
        in_specs=[pl.BlockSpec(memory_space=pltpu.SMEM)] + [vmem] * 7,
        out_specs=[vmem] * 7,
        out_shape=[jax.ShapeDtypeStruct(shape, F32) for shape in shapes],
        scratch_shapes=[pltpu.VMEM((shard, 128), F32)],
        compiler_params=pltpu.CompilerParams(vmem_limit_bytes=40 * 1024 * 1024),
        name="finish",
    )(place, own, mates, w_in.T, w_qkv, w_out, gain_in.astype(F32)[None], gain_m.astype(F32)[None])
    return out[0].T, out[1], out[2], out[3], out[4][0], out[5][0], out[6]


def tie(value, *after):
    return lax.optimization_barrier((value,) + after)[0]


def stage(compute, inputs, sends, late=()):
    inputs, operands = lax.optimization_barrier((inputs, [operand for _, operand in sends]))
    got = [send(operand) for (send, _), operand in zip(sends, operands)]
    out, got, late = lax.optimization_barrier((compute(*inputs), got, late))
    return (out, got, late) if late else (out, got)


class Net:
    def __init__(self):
        self.n = lax.axis_size("ctx")
        self.m = lax.axis_size("fsdp")
        self.c = lax.axis_index("ctx")
        self.f = lax.axis_index("fsdp")
        self.direct = self.n == 4 and self.m == 8
        self.x, self.core = self.c // 2, self.c % 2
        self.z, self.y = self.f // 2, self.f % 2
        self.by_core = [[i * 2 + k for i in range(self.n // 2)] for k in range(2)]

    def flip(self, value, axis, bit):
        size = lax.axis_size(axis)
        return lax.ppermute(value, axis, [(i, i ^ bit) for i in range(size)])

    def shift_z(self, value, by):
        return lax.ppermute(value, "fsdp", [(i, (i + 2 * by) % self.m) for i in range(self.m)])

    def cross(self, value):
        pairs = [
            (c * 8 + z * 2 + y, z * 8 + c * 2 + y)
            for c in range(4)
            for z in range(4)
            for y in range(2)
        ]
        return lax.ppermute(value, ("ctx", "fsdp"), pairs)

    def along_z(self, block):
        return [block] + [self.shift_z(block, k) for k in range(1, 4)]

    def along_y(self, pieces):
        return [self.flip(piece, "fsdp", 1) for piece in pieces]

    def in_order(self, own, mate, columns=None):
        places = [2 * ((self.z - k) % 4) + (self.y ^ o) for o in range(2) for k in range(4)]
        return put(own + mate, places, columns)

    def flip_y(self, value):
        return self.flip(value, "fsdp", 1)

    def flip_x(self, value):
        return self.flip(value, "ctx", 2)

    def flip_core(self, value):
        return self.flip(value, "ctx", 1)

    def halves_y(self, sums):
        low = sums.astype(BF16)
        low = low.reshape((4, 2) + low.shape[1:])
        away = lax.dynamic_index_in_dim(low, 1 - self.y, 1, False)
        return lax.dynamic_index_in_dim(low, self.y, 1, False), away

    def shifts_z(self, both):
        return self.send_z(self.blocks_z(both))

    def blocks_z(self, both):
        return [lax.dynamic_index_in_dim(both, (self.z + k) % 4, 0, False) for k in range(4)]

    def send_z(self, blocks):
        return [blocks[0]] + [self.shift_z(blocks[k], k) for k in range(1, 4)]

    def collect(self, sums):
        return lax.psum_scatter(sums.astype(BF16), "fsdp", scatter_dimension=0, tiled=False)

    def ctx_all(self, value):
        if not self.direct:
            return lax.all_gather(value, "ctx", axis=0, tiled=False)
        pair = jnp.stack([value, self.flip(value, "ctx", 2)])
        mates = self.flip(pair, "ctx", 1)
        return put([pair, mates], [self.c, self.c ^ 2, self.c ^ 1, self.c ^ 3])

    def ctx_sum(self, value):
        if not self.direct:
            return lax.psum(value, "ctx")
        value = value + self.flip(value, "ctx", 1)
        return value + self.flip(value, "ctx", 2)

    def ctx_collect(self, parts):
        if not self.direct:
            low = lax.psum_scatter(parts.astype(BF16), "ctx", scatter_dimension=0, tiled=False)
            return low.astype(F32)
        own, away = self.ctx_halves(parts)
        return own + self.flip(away, "ctx", 2).astype(F32)

    def ctx_halves(self, parts):
        pairs = parts.reshape((2, 2) + parts.shape[1:])
        away = lax.dynamic_index_in_dim(pairs, 1 - self.core, 1, False).astype(BF16)
        here = lax.dynamic_index_in_dim(pairs, self.core, 1, False)
        got = self.flip(away, "ctx", 1)

        def half(which):
            return lax.dynamic_index_in_dim(here, which, 0, False).astype(
                F32
            ) + lax.dynamic_index_in_dim(got, which, 0, False).astype(F32)

        return half(self.x), half(1 - self.x).astype(BF16)

    def over_cores(self, value):
        value = lax.psum(value, "ctx", axis_index_groups=self.by_core)
        return lax.all_gather(value, "ctx", axis=0)[:2].astype(F32)

    def rows_out(self, shard):
        per = self.m // self.n
        got = lax.all_gather(shard, "fsdp", axis=0, tiled=False)
        return lax.dynamic_slice_in_dim(got, self.c * per, per, 0)

    def rows_back(self, sums):
        wide = jnp.zeros((self.m,) + sums.shape[1:], BF16)
        wide = lax.dynamic_update_slice_in_dim(
            wide, sums.astype(BF16), self.c * (self.m // self.n), 0
        )
        out = lax.psum_scatter(wide, "fsdp", scatter_dimension=0, tiled=False)
        return lax.psum(out, "ctx")


def put_kernel(counts, cuts, places, *refs):
    parts, outs = refs[: len(counts)], refs[len(counts) :]
    start = 0
    for part, count in zip(parts, counts):

        @pl.when((pl.program_id(0) >= start) & (pl.program_id(0) < start + count))
        def _(part=part):
            for out, low, high in zip(outs, cuts[:-1], cuts[1:]):
                out[...] = part[..., low:high]

        start += count


def put(parts, places, columns=None):
    counts = [part.shape[0] for part in parts]
    total = sum(counts)
    shape = parts[0].shape[1:]
    zeros = (0,) * len(shape)
    sizes = columns or [shape[-1]]
    cuts = [0]
    for size in sizes:
        cuts.append(cuts[-1] + size)
    places = jnp.stack([jnp.asarray(p, jnp.int32) for p in places])
    size = parts[0][0].size * parts[0].dtype.itemsize
    specs = []
    for p in range(len(parts)):
        start = sum(counts[:p])

        def at(i, at, start=start, last=counts[p] - 1):
            return (jnp.clip(i - start, 0, last),) + zeros

        specs.append(pl.BlockSpec((1,) + shape, at))
    out = pl.pallas_call(
        functools.partial(put_kernel, counts, cuts),
        grid_spec=pltpu.PrefetchScalarGridSpec(
            num_scalar_prefetch=1,
            grid=(total,),
            in_specs=specs,
            out_specs=[
                pl.BlockSpec((1,) + shape[:-1] + (w,), lambda i, at: (at[i],) + zeros)
                for w in sizes
            ],
        ),
        out_shape=[
            jax.ShapeDtypeStruct((total,) + shape[:-1] + (w,), parts[0].dtype) for w in sizes
        ],
        compiler_params=pltpu.CompilerParams(vmem_limit_bytes=40 * 1024 * 1024),
        cost_estimate=pl.CostEstimate(
            flops=0, bytes_accessed=2 * total * size, transcendentals=0
        ),
        name="put",
    )(places, *parts)
    return out if columns else out[0]


def rms_scale(values):
    return lax.rsqrt(jnp.mean(values * values, axis=-1, keepdims=True) + EPSILON)


def rms_back(values, gain, scale, grad):
    scaled = grad * gain
    inner = jnp.mean(values * scaled, axis=-1, keepdims=True)
    return scale * scaled - values * (scale * scale * scale * inner)


def columns_of(w, start, size):
    return lax.dynamic_slice_in_dim(w, start, size, 1)


def rotary_tables(length, q_heads, slab):
    half = HD // 2
    freq = (ROPE_BASE ** (-(np.arange(half) * 2.0 / HD))).astype(np.float32)
    angle = np.arange(length, dtype=np.float32)[:, None] * freq[None, :]
    one = np.concatenate([np.cos(angle), np.cos(angle)], axis=1)
    two = np.concatenate([-np.sin(angle), np.sin(angle)], axis=1)
    room = slab - (q_heads + 1) * HD
    cosine = np.concatenate([one] * (q_heads + 1) + [np.ones((length, room))], axis=1)
    sine = np.concatenate([two] * (q_heads + 1) + [np.zeros((length, room))], axis=1)
    return jnp.asarray(cosine, F32), jnp.asarray(sine, F32)


def per_device(
    tokens,
    teacher,
    segment_ids,
    valid_mask,
    gain_in,
    w_in,
    conv_w,
    conv_b,
    dt_bias,
    a_log,
    d_skip,
    gain_m,
    w_out,
    w_qkv,
    w_o,
    gain_ffn,
    w_gate,
    w_up,
    w_down,
):
    net = Net()
    n, m, c, f = net.n, net.m, net.c, net.f
    rows, dim = tokens.shape[1:]
    length = segment_ids.shape[1]
    shard = w_in.shape[0]
    wide = MH * HP
    conv_full = wide + 2 * NS
    heads = MH // n
    q_heads = QH // n
    width = heads * HP
    conv_width = width + 2 * NS
    q_width = q_heads * HD
    slab = q_width + 2 * HD
    slab += -slab % 128
    group = QH // KVH
    kv_at = (c * q_heads) // group
    ff = w_gate.shape[1]
    ff_shard = w_down.shape[0]
    per = m // n
    seg = segment_ids[0]
    seg_c, seg_r = seg[:, None], seg[None, :]
    ends = jnp.concatenate([jnp.full((1,), -1, jnp.int32), seg[SPAN - 1 :: SPAN]])
    valid = valid_mask[0].astype(F32)

    def lay(values):
        values = values.reshape((-1, values.shape[-1]))
        room = -values.shape[1] % 128
        return jnp.pad(values, ((0, 0), (0, room))).reshape(-1, 128)

    def unlay(small, start, lead, size):
        room = size + -size % 128
        count = lead * room // 128
        return small[..., start : start + count, :].reshape(small.shape[:-2] + (lead, room))[
            ..., :size
        ]

    shapes = [(1, shard), (1, shard), (1, w_out.shape[0]), (1, conv_b.shape[0])]
    shapes += [(KW, conv_b.shape[0])]
    starts = [0]
    for lead, size in shapes:
        starts.append(starts[-1] + lead * (size + -size % 128) // 128)
    laid = [lay(p) for p in (gain_in[None], gain_ffn[None], gain_m[None], conv_b[None], conv_w)]
    laid.append(jnp.full((1, 128), jnp.sum(valid), F32).astype(BF16))
    laid.append(jnp.zeros((-(starts[-1] + 1) % 16, 128), BF16))
    at_small = 64
    packed = jnp.concatenate(laid, axis=0)
    first = jnp.concatenate(
        [
            columns_of(w_in, wide + c * width, width),
            w_in[:, 2 * wide : 2 * wide + 2 * NS],
            columns_of(w_in, wide + conv_full + c * heads, heads),
            jnp.zeros((shard, at_small - heads), BF16),
            packed.T if net.direct else jnp.zeros((shard, packed.shape[0]), BF16),
            jnp.zeros((shard, 128 - at_small - packed.shape[0]), BF16),
        ],
        axis=1,
    )
    second = jnp.concatenate(
        [
            columns_of(w_in, c * width, width),
            columns_of(w_qkv, c * q_width, q_width),
            columns_of(w_qkv, QH * HD + kv_at * HD, HD),
            columns_of(w_qkv, (QH + KVH) * HD + kv_at * HD, HD),
            jnp.zeros((shard, slab - q_width - 2 * HD), BF16),
        ],
        axis=1,
    )
    both_out = jnp.concatenate([w_out, w_o], axis=0)
    out_rows, mamba_rows = both_out.shape[0], w_out.shape[0]
    ff_half = ff_shard // 2
    size = m * ff_half

    def ff_cut(w):
        w = w.reshape(shard, m, 2, ff_half)
        return lax.dynamic_index_in_dim(w, net.core, 2, False).reshape(shard, size)

    places_x = n // 2

    def quarter_x(w):
        size = w.shape[0] // places_x
        return lax.dynamic_slice_in_dim(w, net.x * size, size, 0)

    w_ff = jnp.concatenate(
        [
            quarter_x(ff_cut(w_gate).reshape(-1, dim)),
            quarter_x(ff_cut(w_up).reshape(-1, dim)),
            quarter_x(lax.dynamic_slice_in_dim(w_down, net.core * ff_half, ff_half, 0)),
        ],
        axis=0,
    )
    groups = [[d * m + i for d in net.by_core[k] for i in range(m)] for k in range(2)]
    w_ff = lax.all_gather(
        w_ff, ("ctx", "fsdp"), axis=0, tiled=False, axis_index_groups=groups
    ).reshape((places_x, m) + w_ff.shape)
    if net.direct:
        both_cols = jnp.concatenate([first, second], axis=1)
        near = net.along_z(both_cols)
        own_tokens = tie(tokens[0], near[1])
        pair = jnp.stack([own_tokens, net.flip_x(own_tokens)])
        far = net.along_y(near)
        all_tokens = put([pair, net.flip_core(pair)], [c, c ^ 2, c ^ 1, c ^ 3])
        w_first, w_second = net.in_order(
            [tie(near[0], all_tokens)[None]] + [p[None] for p in near[1:]],
            [p[None] for p in far],
            [first.shape[1], second.shape[1]],
        )
        at = conv_width + at_small
        small = jnp.swapaxes(w_first[:, :, at : at + packed.shape[0]], 1, 2)
        crossed = net.cross(tie(both_out, *near[1:]))
    else:
        small = lax.all_gather(packed, "fsdp", axis=0, tiled=False)
        w_first = lax.all_gather(first, "fsdp", axis=0, tiled=False)
        w_second = lax.all_gather(second, "fsdp", axis=0, tiled=False)
        w_outs = net.rows_out(both_out)
        all_tokens = net.ctx_all(tokens[0])
    all_tokens = all_tokens.reshape(length, dim)
    w_first = w_first.reshape(dim, first.shape[1])
    cuts = [
        jnp.transpose(unlay(small, start, *shape), (1, 0, 2)).reshape(shape[0], -1)
        for start, shape in zip(starts, shapes)
    ]
    gain_input = cuts[0].astype(F32)
    gain_second = cuts[1].astype(F32)
    gain_mamba = lax.dynamic_slice_in_dim(cuts[2], c * width, width, 1).astype(F32)
    count_ctx = jnp.sum(small[:, starts[-1], 0].astype(F32))

    def conv_cut(values):
        own = lax.dynamic_slice_in_dim(values, c * width, width, 1)
        return jnp.concatenate([own, values[:, wide:]], axis=1).astype(F32)

    bias, taps = conv_cut(cuts[3]), conv_cut(cuts[4])
    rate = jnp.exp(a_log)
    params = jnp.stack(
        [lax.dynamic_slice_in_dim(v, c * heads, heads) for v in (dt_bias, rate)]
    )
    params = jnp.pad(params, ((0, 6), (0, 128 - heads)))
    skip = lax.dynamic_slice_in_dim(d_skip, c * heads, heads)

    def shifted(by):
        return jnp.concatenate([jnp.full((by,), -1, jnp.int32), seg[: length - by]]) == seg

    same = jnp.stack([shifted(by) for by in range(KW)], axis=1).astype(F32)
    up = jnp.stack(
        [
            jnp.concatenate([seg[by:], jnp.full((by,), -1, jnp.int32)]) == seg
            for by in range(KW)
        ],
        axis=1,
    ).astype(F32)
    cosine, sine = rotary_tables(length, q_heads, slab)
    conv_args = (all_tokens, gain_input, w_first, taps, bias, same, params)

    def square_rows(square):
        return jnp.concatenate([square[0].reshape(-1, 128), jnp.full((8, 128), count_ctx)])

    def ssm(act, steps, step_rows):
        return ssm_forward(heads, (ends, skip, act, steps, step_rows, seg_c, seg_r))

    def attend(qkv):
        return attn_forward(q_heads, (qkv, seg_c, seg_r))

    w_second = w_second.reshape(dim, second.shape[1])
    if net.direct:
        normed, cin, pre, act, steps, step_rows = project_conv(*conv_args)
        ssm_y, states = ssm(act, steps, step_rows)
        gate_z, qkv, square = project_gate(normed, w_second, ssm_y, cosine, sine)
        mated = net.flip_y(tie(crossed, ssm_y))
        (attended, lse), (square,) = stage(
            attend, (qkv,), [(net.ctx_sum, square_rows(square))]
        )
        w_outs = jnp.where(
            net.y == 0, jnp.stack([crossed, mated]), jnp.stack([mated, crossed])
        )
    else:
        normed, cin, pre, act, steps, step_rows = project_conv(*conv_args)
        ssm_y, states = ssm(act, steps, step_rows)
        gate_z, qkv, square = project_gate(normed, w_second, ssm_y, cosine, sine)
        square = net.ctx_sum(square_rows(square))
        attended, lse = attend(qkv)
    w_mamba = w_outs[:, :mamba_rows].reshape(per * mamba_rows, dim)
    w_attn = w_outs[:, mamba_rows:].reshape(per * (out_rows - mamba_rows), dim)
    ssm_in = (ends, skip, act, steps, step_rows, seg_c, seg_r)
    count = square[-1, 0]
    scale_m = lax.rsqrt(square[:-8].reshape(length, 1) / wide + EPSILON)
    gated = ssm_y * (gate_z * jax.nn.sigmoid(gate_z))
    ym = (gated * scale_m * gain_mamba).astype(BF16)
    outs = nn(ym, w_mamba) + nn(attended, w_attn)
    ff_rows = shard * size // dim
    part_rows = ff_rows // places_x

    def plus(here, got):
        return (here.astype(F32) + got.astype(F32)).astype(BF16)

    def ff_weights(w_ff):
        def part(low, high, columns):
            return jnp.swapaxes(w_ff[:, :, low:high], 0, 1).reshape(-1, columns)

        return (
            part(0, part_rows, size),
            part(part_rows, 2 * part_rows, size),
            part(2 * part_rows, w_ff.shape[2], dim),
        )

    if net.direct:
        own, away = net.ctx_halves(outs.reshape(n, rows, dim))
        (w_g, w_u, w_d), (across,) = stage(ff_weights, (w_ff,), [(net.flip_x, away)])
        mixed = tokens[0].astype(F32) + own + across.astype(F32)
    else:
        w_g, w_u, w_d = ff_weights(w_ff)
        mixed = tokens[0].astype(F32) + net.ctx_collect(outs.reshape(n, rows, dim))

    scale2 = rms_scale(mixed)
    normed2 = (mixed * scale2 * gain_second).astype(BF16)
    mate = [(i, i ^ 1) for i in range(n)]
    both = jnp.concatenate([normed2, lax.ppermute(normed2, "ctx", mate)], axis=0)
    gate_v, up_v = nn(both, w_g), nn(both, w_u)
    sig = jax.nn.sigmoid(gate_v)
    product = (gate_v * sig * up_v).astype(BF16)
    down_out = nn(product, w_d)
    from_mate = lax.ppermute(down_out[rows:].astype(BF16), "ctx", mate)
    layer_out = mixed + down_out[:rows] + from_mate.astype(F32)
    diff = layer_out - teacher[0].astype(F32)
    squared = jnp.sum(valid[:, None] * diff * diff)
    token_total = length * m * tokens.shape[0]
    grad_out = token_total * valid[:, None] * diff / count

    gb = grad_out.astype(BF16)
    gb_both = jnp.concatenate([gb, lax.ppermute(gb, "ctx", mate)], axis=0)
    g_prod = nt(gb_both, w_d)
    g_gate = (g_prod * up_v * (sig * (1.0 + gate_v * (1.0 - sig)))).astype(BF16)
    g_up = (g_prod * gate_v * sig).astype(BF16)
    if net.direct:
        g_ff = ff_gradients(m, both, product, g_gate, g_up, gb_both)
    else:
        g_ff = jnp.concatenate(
            [
                tn(both, g_gate).reshape(m, ff_rows, dim),
                tn(both, g_up).reshape(m, ff_rows, dim),
                tn(product, gb_both).reshape(m, ff_half, dim),
            ],
            axis=1,
        ).astype(BF16)
    g_n2 = nt(tie(g_gate, g_ff), w_g) + nt(g_up, w_u)
    from_mate = lax.ppermute(g_n2[rows:].astype(BF16), "ctx", mate)
    grad_n2 = g_n2[:rows] + from_mate.astype(F32)
    part = rms_back(mixed, gain_second, scale2, grad_n2)
    grad_mixed = grad_out + part

    gm = net.ctx_all(grad_mixed.astype(BF16))
    gm = gm.reshape(length, dim)
    g_ff = lax.psum_scatter(g_ff, "fsdp", scatter_dimension=0, tiled=False)

    g_ym = nt(gm, w_mamba)
    inner = jnp.sum(gated * (g_ym * gain_mamba), axis=1).reshape(-1, 128)

    def outs_back(gm):
        g_ob = nt(gm, w_attn).astype(BF16)
        g_outs = jnp.concatenate(
            [
                tn(ym, gm).reshape(per, mamba_rows, dim),
                tn(attended, gm).reshape(per, out_rows - mamba_rows, dim),
            ],
            axis=1,
        )
        return g_ob, g_outs.astype(BF16)

    def attend_back(qkv, g_ob):
        return attn_backward(q_heads, (qkv, seg_c, seg_r), lse, g_ob, cosine, sine)

    def plus(here, got):
        return (here.astype(F32) + got.astype(F32)).astype(BF16)

    if net.direct:
        (g_ob, g_outs), (got,) = stage(outs_back, (gm,), [(net.flip_core, inner)])
        inner = inner + got
        here = lax.dynamic_index_in_dim(g_outs, net.y, 0, False)
        away = lax.dynamic_index_in_dim(g_outs, 1 - net.y, 0, False)
        got = net.flip_y(away)
        g_qkv, (got_x,) = stage(attend_back, (qkv, g_ob), [(net.flip_x, inner)])
        inner = inner + got_x
        out_both = plus(here, got).reshape(4, out_rows // 4, dim)
    else:
        g_ob, g_outs = outs_back(gm)
        inner = net.ctx_sum(inner)
        g_qkv = attend_back(qkv, g_ob)
    inner = inner.reshape(length, 1) / wide
    stats = jnp.concatenate([scale_m, scale_m * scale_m * scale_m * inner], axis=1)
    g_gated = stats[:, :1] * (g_ym * gain_mamba) - gated * stats[:, 1:]
    sig_z = jax.nn.sigmoid(gate_z)
    g_z = (g_gated * ssm_y * (sig_z + gate_z * sig_z * (1.0 - sig_z))).astype(BF16)
    early = jnp.concatenate([g_z, g_qkv], axis=1)
    grad_early = tn(normed, early).reshape(m, shard, width + slab)

    def ssm_back(states):
        return ssm_backward(
            heads,
            ssm_in,
            states,
            gate_z,
            g_ym,
            ssm_y,
            stats,
            gain_mamba,
            pre,
            cin,
            up,
            taps,
            params,
        )

    if net.direct:
        here, away = net.halves_y(grad_early)
        (g_late, g_conv, g_wide, g_steps), (got, out_parts) = stage(
            ssm_back, (states,), [(net.flip_y, away), (net.shifts_z, out_both)]
        )
        grad_early = plus(here, got)
        out_quarter = sum(p.astype(F32) for p in out_parts).astype(BF16)
    else:
        g_late, g_conv, g_wide, g_steps = ssm_back(states)

    def to_wide(values, at, size):
        out = jnp.zeros(values.shape[:-1] + (size,), F32)
        return lax.dynamic_update_slice_in_dim(out, values, at, values.ndim - 1)

    def for_shards(values):
        values = jnp.concatenate(
            [to_wide(values[:, :width], c * width, wide), values[:, width:]], axis=1
        )
        values = values.reshape((-1, m, values.shape[-1] // m))
        return jnp.transpose(values, (1, 0, 2))

    conv_rows = (conv_b.shape[0] + 127) // 128
    heads_grads = jnp.stack(
        [
            to_wide(g_steps[0, :heads], c * heads, MH),
            to_wide(g_steps[1, :heads], c * heads, MH),
            to_wide(jnp.sum(g_wide[0].reshape(heads, HP), axis=1), c * heads, MH),
            jnp.full((MH,), squared),
        ]
    )
    laid = [jax.vmap(lay)(for_shards(g_conv[: KW + 1]))]
    laid.append(jnp.broadcast_to(lay(heads_grads)[None], (m, 4, 128)))
    laid = jnp.concatenate(laid, axis=1)
    late_size = conv_width + 128
    grad_late = tn(normed, g_late).reshape(m, shard, late_size)
    if net.direct:
        laid = jnp.swapaxes(laid, 1, 2)
        ends_at = conv_width + at_small
        grad_late = jnp.concatenate(
            [grad_late[..., :ends_at], laid, grad_late[..., ends_at + laid.shape[2] :]], axis=2
        )
    grad_late = grad_late.astype(BF16)
    resid = tokens[0].astype(F32)

    def normed_back(early, g_late):
        return (nt(early, w_second) + nt(g_late, w_first)).reshape(n, rows, dim)

    def tokens_back(grad_normed):
        return grad_mixed + rms_back(resid, gain_input, rms_scale(resid), grad_normed)

    if net.direct:
        g_normed = normed_back(early, g_late)
        here, away = net.halves_y(grad_late)
        _, (grad_normed, got, early_parts) = stage(
            tuple,
            (),
            [
                (net.ctx_collect, g_normed),
                (net.flip_y, away),
                (net.shifts_z, grad_early),
            ],
        )
        grad_early = sum(p.astype(F32) for p in early_parts).astype(BF16)
        blocks = net.blocks_z(plus(here, got))
        g_ff = tie(g_ff, grad_early, *blocks)
        got_ff = net.flip_x(g_ff)
        grad_tokens, (late_parts, out_quarter), (got_ff,) = stage(
            tokens_back,
            (grad_normed,),
            [(net.send_z, blocks), (net.cross, out_quarter)],
            (got_ff,),
        )
        g_ff = plus(g_ff, got_ff)
        grad_late = sum(p.astype(F32) for p in late_parts).astype(BF16)
        joined = jnp.concatenate([out_quarter[:, : dim // 2], out_quarter[:, dim // 2 :]], axis=0)
        joined = jnp.concatenate([grad_early, joined], axis=1)
        joined = jnp.concatenate([grad_late, joined], axis=1)
        def finish_halves(g_ff, got_ff):
            return finish_ff(net.core, g_ff, got_ff, w_gate, w_up, gain_ffn)

        ff_out, (across,) = stage(
            finish_halves, (g_ff, net.flip_core(g_ff)), [(net.flip_x, joined)]
        )
        out_gate, out_up, out_down, out_gain_ffn = ff_out
        joined = jnp.stack([joined, across])
        mates = net.flip_core(joined)
        place = jnp.stack([net.x, net.core]).astype(jnp.int32)
        out_w_in, out_w_qkv, out_mamba, out_attn, out_gain_in, out_gain_m, totals = finish(
            place, joined, mates, w_in, w_qkv, w_out, w_o, gain_in, gain_m
        )
        totals = totals[at_small : at_small + laid.shape[2]]
    else:
        grad_tokens = tokens_back(net.ctx_collect(normed_back(early, g_late)))
        got_early = net.ctx_all(net.collect(grad_early)).astype(F32)
        got_late = net.ctx_all(net.collect(grad_late))
        out_outs = net.rows_back(g_outs).astype(F32)
        got_ff = net.over_cores(g_ff)
        got_late = got_late.astype(F32)
        totals = lax.psum_scatter(laid, "fsdp", scatter_dimension=0, tiled=False)
        totals = lax.psum(totals, "ctx")
        def side(got, start, size):
            return [got[j][:, start : start + size] for j in range(n)]

        shared = n // KVH
        out_w_in = jnp.concatenate(
            side(got_early, 0, width)
            + side(got_late, 0, width)
            + [sum(side(got_late, width, 2 * NS))]
            + side(got_late, conv_width, heads),
            axis=1,
        )
        out_w_qkv = jnp.concatenate(
            side(got_early, width, q_width)
            + [
                sum(side(got_early, width + q_width + i * HD, HD)[k * shared : (k + 1) * shared])
                for i in range(2)
                for k in range(KVH)
            ],
            axis=1,
        )

        def ff_wide(values):
            values = values.reshape(2, shard, m, ff_half)
            return jnp.transpose(values, (1, 2, 0, 3)).reshape(shard, ff)

        out_gate = ff_wide(got_ff[:, :ff_rows])
        out_up = ff_wide(got_ff[:, ff_rows : 2 * ff_rows])
        out_mamba = out_outs[:mamba_rows]

        def along(*pairs):
            return sum(jnp.sum(w.astype(F32) * g, axis=1) for w, g in pairs)

        out_attn = out_outs[mamba_rows:]
        out_down = got_ff[:, 2 * ff_rows :].reshape(ff_shard, dim)
        out_gain_in = along((w_in, out_w_in), (w_qkv, out_w_qkv)) / gain_in.astype(F32)
        out_gain_m = along((w_out, out_mamba)) / gain_m.astype(F32)
        out_gain_ffn = along((w_gate, out_gate), (w_up, out_up)) / gain_ffn.astype(F32)
    grad_conv = unlay(totals, 0, KW + 1, conv_b.shape[0])
    head_totals = totals[(KW + 1) * conv_rows : (KW + 1) * conv_rows + 4, :MH]
    loss = head_totals[3, 0] / (2.0 * count)
    return (
        loss,
        layer_out[None],
        grad_tokens[None],
        out_gain_in,
        out_w_in,
        grad_conv[:KW],
        grad_conv[KW],
        head_totals[0],
        head_totals[1],
        head_totals[2],
        out_gain_m,
        out_mamba,
        out_w_qkv,
        out_attn,
        out_gain_ffn,
        out_gate,
        out_up,
        out_down,
    )


def solution(mesh):
    in_specs = (
        P("fsdp", "ctx", None),
        P("fsdp", "ctx", None),
        P("fsdp", None),
        P("fsdp", "ctx"),
        P("fsdp"),
        P("fsdp", None),
        P(None, "fsdp"),
        P("fsdp"),
        P(),
        P(),
        P(),
        P("fsdp"),
        P("fsdp", None),
        P("fsdp", None),
        P("fsdp", None),
        P("fsdp"),
        P("fsdp", None),
        P("fsdp", None),
        P("fsdp", None),
    )
    out_specs = (
        P(),
        P("fsdp", "ctx", None),
        P("fsdp", "ctx", None),
        P("fsdp"),
        P("fsdp", None),
        P(None, "fsdp"),
        P("fsdp"),
        P(),
        P(),
        P(),
        P("fsdp"),
        P("fsdp", None),
        P("fsdp", None),
        P("fsdp", None),
        P("fsdp"),
        P("fsdp", None),
        P("fsdp", None),
        P("fsdp", None),
    )
    return jax.shard_map(
        per_device, mesh=mesh, in_specs=in_specs, out_specs=out_specs, check_vma=False
    )
```

```python
import functools

import jax
import jax.numpy as jnp
import numpy as np
from jax import lax
from jax.experimental import pallas as pl
from jax.experimental.pallas import tpu as pltpu
from jax.sharding import PartitionSpec as P

MH = 24
HP = 64
NS = 128
KW = 4
QH = 8
KVH = 2
HD = 64
SPAN = 128
QBLK = 256

EPSILON = 1e-05
ROPE_BASE = 100000000000.0
MASKED = -1e30

F32 = jnp.float32
BF16 = jnp.bfloat16
HIGH = lax.Precision.HIGHEST


def nn(left, right, precision=None):
    return lax.dot_general(
        left, right, (((1,), (0,)), ((), ())), precision=precision, preferred_element_type=F32
    )


def nt(left, right):
    return lax.dot_general(left, right, (((1,), (1,)), ((), ())), preferred_element_type=F32)


def tn(left, right):
    return lax.dot_general(left, right, (((0,), (0,)), ((), ())), preferred_element_type=F32)


def swap_halves(values):
    lane = lax.broadcasted_iota(jnp.int32, values.shape, 1) % HD
    size = values.shape[1]
    return jnp.where(
        lane < HD // 2,
        pltpu.roll(values, size - HD // 2, 1),
        pltpu.roll(values, HD // 2, 1),
    )


def conv_kernel(
    tok, gain, weight, taps, bias, same, params, normed_ref, cin_ref, pre_ref, act_ref, step_ref,
    row_ref, halo,
):
    conv = taps.shape[1]
    block = tok.shape[0]

    @pl.when(pl.program_id(0) == 0)
    def _():
        halo[...] = jnp.zeros_like(halo)

    values = tok[...].astype(F32)
    scale = lax.rsqrt(jnp.mean(values * values, axis=-1, keepdims=True) + EPSILON)
    normed = (values * scale * gain[...]).astype(BF16)
    normed_ref[...] = normed
    cin = nn(normed, weight[:, :conv])
    cin_ref[...] = cin.astype(BF16)
    halo[8 : 8 + block, :] = cin
    pre = bias[...] + taps[KW - 1 : KW, :] * cin
    for by in range(1, KW):
        tap = taps[KW - 1 - by : KW - by, :]
        pre = pre + tap * halo[8 - by : 8 - by + block, :] * same[:, by : by + 1]
    halo[0:8, :] = halo[block : block + 8, :]
    pre_ref[...] = pre.astype(BF16)
    act_ref[...] = (pre * jax.nn.sigmoid(pre)).astype(BF16)
    raw = nn(normed, weight[:, conv:]) + params[0:1, :]
    dt = jnp.maximum(raw, 0.0) + jnp.log1p(jnp.exp(-jnp.abs(raw)))
    loga = -dt * params[1:2, :]
    step_ref[:, :128] = dt
    step_ref[:, 128:] = loga
    row_ref[0:8, :] = jnp.transpose(dt)[0:8, :]
    row_ref[8:16, :] = jnp.transpose(loga)[0:8, :]


def by_rows(size):
    return pl.BlockSpec((QBLK, size), lambda i: (i, 0))


def whole(a):
    return pl.BlockSpec(a.shape, lambda i: (0, 0))


def project_conv(tokens, gain, weight, taps, bias, same, params):
    length, dim = tokens.shape
    conv = taps.shape[1]
    sizes = [(dim, BF16), (conv, BF16), (conv, BF16), (conv, BF16), (256, F32)]
    return pl.pallas_call(
        conv_kernel,
        grid=(length // QBLK,),
        in_specs=[
            by_rows(dim),
            whole(gain),
            whole(weight),
            whole(taps),
            whole(bias),
            by_rows(same.shape[1]),
            whole(params),
        ],
        out_specs=[by_rows(size) for size, _ in sizes]
        + [pl.BlockSpec((16, QBLK), lambda i: (0, i))],
        out_shape=[jax.ShapeDtypeStruct((length, size), kind) for size, kind in sizes]
        + [jax.ShapeDtypeStruct((16, length), F32)],
        scratch_shapes=[pltpu.VMEM((QBLK + 8, conv), F32)],
        compiler_params=pltpu.CompilerParams(vmem_limit_bytes=40 * 1024 * 1024),
        cost_estimate=pl.CostEstimate(
            flops=2 * length * dim * weight.shape[1], bytes_accessed=10**7, transcendentals=10**6
        ),
        name="project_conv",
    )(tokens, gain, weight, taps, bias, same, params)


def gate_kernel(normed_ref, weight, y_ref, cosine, sine, z_ref, qkv_ref, sq_ref):
    width = y_ref.shape[1]
    normed = normed_ref[...]
    gate = nn(normed, weight[:, :width])
    z_ref[...] = gate
    qkv = nn(normed, weight[:, width:])
    qkv_ref[...] = (qkv * cosine[...] + swap_halves(qkv) * sine[...]).astype(BF16)
    gated = y_ref[...] * (gate * jax.nn.sigmoid(gate))
    sq_ref[...] = lax.dot_general(
        jnp.ones((8, width), F32),
        gated * gated,
        (((1,), (1,)), ((), ())),
        precision=HIGH,
        preferred_element_type=F32,
    )


def project_gate(normed, weight, y, cosine, sine):
    length, dim = normed.shape
    width = y.shape[1]
    slab = cosine.shape[1]
    return pl.pallas_call(
        gate_kernel,
        grid=(length // QBLK,),
        in_specs=[by_rows(dim), whole(weight), by_rows(width), by_rows(slab), by_rows(slab)],
        out_specs=[
            by_rows(width),
            by_rows(slab),
            pl.BlockSpec((8, QBLK), lambda i: (0, i)),
        ],
        out_shape=[
            jax.ShapeDtypeStruct((length, width), F32),
            jax.ShapeDtypeStruct((length, slab), BF16),
            jax.ShapeDtypeStruct((8, length), F32),
        ],
        compiler_params=pltpu.CompilerParams(vmem_limit_bytes=40 * 1024 * 1024),
        cost_estimate=pl.CostEstimate(
            flops=2 * length * dim * weight.shape[1], bytes_accessed=10**7, transcendentals=10**6
        ),
        name="project_gate",
    )(normed, weight, y, cosine, sine)


def decays(seg_c, seg_r, loga_c, loga_r, before, end):
    row = lax.broadcasted_iota(jnp.int32, (SPAN, SPAN), 0)
    col = lax.broadcasted_iota(jnp.int32, (SPAN, SPAN), 1)
    lower = row >= col
    same = (seg_c == seg_r) & lower
    run_c = nn(lower.astype(F32), loga_c, HIGH)
    run_r = nn(loga_r, (row <= col).astype(F32), HIGH)
    keep = (seg_c == before).astype(F32)
    tail = (seg_c == end).astype(F32)
    return row, col, same, run_c, run_r, keep, tail


def head_groups(heads):
    return [tuple(range(g, min(g + 2, heads))) for g in range(0, heads, 2)]


def by_lane(columns, group, size):
    first = columns[:, group[0] : group[0] + 1]
    if len(group) == 1:
        return first
    lane = lax.broadcasted_iota(jnp.int32, (columns.shape[0], size), 1)
    return jnp.where(lane < HP, first, columns[:, group[1] : group[1] + 1])


def stacked(values, group):
    if len(group) == 1:
        return values
    lane = lax.broadcasted_iota(jnp.int32, values.shape, 1)
    zero = jnp.zeros_like(values)
    return jnp.concatenate(
        [jnp.where(lane < HP, values, zero), jnp.where(lane < HP, zero, values)], axis=0
    )


def ssm_fwd_kernel(
    heads, ends, skip, act, steps, rows, seg_c, seg_r, y_ref, st_ref, state, weighted
):
    step = pl.program_id(0)

    @pl.when(step == 0)
    def _():
        state[...] = jnp.zeros_like(state)

    before, end = ends[step], ends[step + 1]
    link = (before == end).astype(F32)
    _, _, same, run_c, run_r, keep, tail = decays(
        seg_c[...], seg_r[...], steps[:, 128:], rows[8:16, :], before, end
    )
    width = heads * HP
    b_in = act[:, width : width + NS]
    c_in = act[:, width + NS : width + 2 * NS]
    gram = nt(c_in, b_in)
    last = run_c[SPAN - 1 :, :]
    carry_w = jnp.exp(run_c) * keep
    end_w = jnp.exp(last - run_c) * tail * steps[:, :128]
    prior = state[...]
    st_ref[0] = prior
    from_state = nt(c_in, prior.astype(BF16))
    for group in head_groups(heads):
        size = len(group) * HP
        lanes = slice(group[0] * HP, group[0] * HP + size)
        x_in = act[:, lanes]
        x_wide = x_in.astype(F32)
        mixing = []
        for h in group:
            decay = jnp.where(same, jnp.exp(run_c[:, h : h + 1] - run_r[h : h + 1, :]), 0.0)
            mixing.append((gram * decay * rows[h : h + 1, :]).astype(BF16))
        y_in = nn(jnp.concatenate(mixing, axis=1), stacked(x_in, group))
        skips = [skip[h] for h in group]
        lane = lax.broadcasted_iota(jnp.int32, (1, size), 1)
        skip_w = jnp.where(lane < HP, skips[0], skips[-1])
        y_ref[:, lanes] = (
            y_in + from_state[:, lanes] * by_lane(carry_w, group, size) + skip_w * x_wide
        )
        weighted[:, lanes] = (x_wide * by_lane(end_w, group, size)).astype(BF16)
    local = tn(weighted[...], b_in)
    for h in range(heads):
        part = slice(h * HP, (h + 1) * HP)
        state[part, :] = (jnp.exp(last[:, h : h + 1]) * link) * prior[part, :] + local[part, :]


def ssm_bwd_kernel(
    heads,
    ends,
    skip,
    act,
    steps,
    rows,
    seg_c,
    seg_r,
    st_ref,
    z_ref,
    gym_ref,
    y_ref,
    stat_ref,
    gain_ref,
    pre_ref,
    cin_ref,
    up_ref,
    taps,
    params,
    first_ref,
    gconv_ref,
    gwide_ref,
    gstep_ref,
    gstate,
    gbuf,
    grow,
    carried,
    ended,
):
    step = pl.num_programs(0) - 1 - pl.program_id(0)
    width = heads * HP
    conv = width + 2 * NS

    @pl.when(pl.program_id(0) == 0)
    def _():
        gstate[...] = jnp.zeros_like(gstate)
        gbuf[...] = jnp.zeros_like(gbuf)
        grow[...] = jnp.zeros_like(grow)
        gconv_ref[...] = jnp.zeros_like(gconv_ref)
        gwide_ref[...] = jnp.zeros_like(gwide_ref)
        gstep_ref[...] = jnp.zeros_like(gstep_ref)

    before, end = ends[step], ends[step + 1]
    link = (before == end).astype(F32)
    row, col, same, run_c, run_r, keep, tail = decays(
        seg_c[...], seg_r[...], steps[:, 128:], rows[8:16, :], before, end
    )
    gate = z_ref[...]
    silu = gate * jax.nn.sigmoid(gate)
    gated = y_ref[...] * silu
    g_gated = stat_ref[:, 0:1] * (gym_ref[...] * gain_ref[...]) - gated * stat_ref[:, 1:2]
    g_all = g_gated * silu
    x_all = act[:, :width].astype(F32)
    gwide_ref[0:1, :] += jnp.sum(g_all * x_all, axis=0, keepdims=True)

    b_in = act[:, width : width + NS]
    c_in = act[:, width + NS : width + 2 * NS]
    gram = nt(c_in, b_in)
    last = run_c[SPAN - 1 :, :]
    carry_w = jnp.exp(run_c) * keep
    tail_w = jnp.exp(last - run_c) * tail
    end_w = tail_w * steps[:, :128]
    prior = st_ref[0]
    prior_low = prior.astype(BF16)
    after = gstate[...]
    after_low = after.astype(BF16)
    from_prior = nt(c_in, prior_low)
    from_after = nt(b_in, after_low)
    g_gram = jnp.zeros((SPAN, SPAN), F32)
    row_sums = jnp.zeros((SPAN, SPAN), F32)
    for group in head_groups(heads):
        size = len(group) * HP
        lanes = slice(group[0] * HP, group[0] * HP + size)
        gy = g_all[:, lanes]
        gy_parts = stacked(gy.astype(BF16), group)
        g_mixes = nt(gy_parts, act[:, lanes])
        mixing = []
        for i, h in enumerate(group):
            dt_row = rows[h : h + 1, :]
            decay = jnp.where(same, jnp.exp(run_c[:, h : h + 1] - run_r[h : h + 1, :]), 0.0)
            mixing.append((gram * decay * dt_row).astype(BF16))
            g_mix = g_mixes[i * SPAN : (i + 1) * SPAN, :] * decay
            g_gram_h = g_mix * dt_row
            g_gram = g_gram + g_gram_h
            sums = jnp.sum(g_gram_h * gram, axis=1, keepdims=True)
            row_sums = jnp.where(col == h, sums, row_sums)
            by_key = jnp.sum(g_mix * gram, axis=0, keepdims=True)
            grow[h : h + 1, :] = by_key * dt_row
            grow[128 + h : 128 + h + 1, :] = by_key
        skips = [skip[h] for h in group]
        lane = lax.broadcasted_iota(jnp.int32, (1, size), 1)
        skip_w = jnp.where(lane < HP, skips[0], skips[-1])
        end_l = by_lane(end_w, group, size)
        gbuf[0:SPAN, lanes] = (
            tn(jnp.concatenate(mixing, axis=0), gy_parts)
            + from_after[:, lanes] * end_l
            + skip_w * gy
        )
        carried[:, lanes] = (gy * by_lane(carry_w, group, size)).astype(BF16)
        ended[:, lanes] = (x_all[:, lanes] * end_l).astype(BF16)
    of_head = (
        lax.broadcasted_iota(jnp.int32, (width, 128), 0) // HP
        == lax.broadcasted_iota(jnp.int32, (width, 128), 1)
    ).astype(BF16)

    def head_sums(values):
        high = values.astype(BF16)
        return nn(high, of_head) + nn((values - high.astype(F32)).astype(BF16), of_head)

    g_carry = head_sums(g_all * from_prior)
    g_tail = head_sums(x_all * from_after)
    state_sums = jnp.sum(after * prior, axis=1, keepdims=True)
    of_head_t = (
        lax.broadcasted_iota(jnp.int32, (width, 128), 0) // HP
        == lax.broadcasted_iota(jnp.int32, (width, 128), 1)
    )
    state_sums = jnp.sum(jnp.where(of_head_t, state_sums, 0.0), axis=0, keepdims=True)
    g_end = g_tail * end_w
    g_link = jnp.exp(last) * link
    total_last = jnp.sum(g_end, axis=0, keepdims=True) + g_link * state_sums
    g_run = row_sums + g_carry * carry_w - g_end + jnp.where(row == SPAN - 1, total_last, 0.0)
    weighted = carried[...]
    g_gram_low = g_gram.astype(BF16)
    gbuf[0:SPAN, width : width + NS] = nn(ended[...], after_low) + tn(g_gram_low, c_in)
    gbuf[0:SPAN, width + NS :] = nn(weighted, prior_low) + nn(g_gram_low, b_in)
    to_state = tn(weighted, c_in)
    for h in range(heads):
        part = slice(h * HP, (h + 1) * HP)
        gstate[part, :] = g_link[:, h : h + 1] * after[part, :] + to_state[part, :]

    pre = pre_ref[...].astype(F32)
    sig = jax.nn.sigmoid(pre)
    g_pre = gbuf[0:SPAN, :] * (sig + pre * sig * (1.0 - sig))
    gbuf[0:SPAN, :] = g_pre
    cin = cin_ref[...].astype(F32)
    g_conv = taps[KW - 1 : KW, :] * g_pre
    gconv_ref[KW - 1 : KW, :] += jnp.sum(g_pre * cin, axis=0, keepdims=True)
    gconv_ref[KW : KW + 1, :] += jnp.sum(g_pre, axis=0, keepdims=True)
    for by in range(1, KW):
        ahead = gbuf[by : by + SPAN, :] * up_ref[:, by : by + 1]
        tap = KW - 1 - by
        g_conv = g_conv + taps[tap : tap + 1, :] * ahead
        gconv_ref[tap : tap + 1, :] += jnp.sum(ahead * cin, axis=0, keepdims=True)
    gbuf[SPAN : SPAN + 8, :] = gbuf[0:8, :]
    first_ref[:, :conv] = g_conv.astype(BF16)

    later = (col >= row).astype(F32)
    eye = (col == row).astype(F32)

    def across(left, right):
        return lax.dot_general(
            left, right, (((1,), (1,)), ((), ())), precision=HIGH, preferred_element_type=F32
        )

    g_loga = nn(later, g_run, HIGH) - across(later, grow[:128, :])
    g_dt = g_tail * tail_w + across(eye, grow[128:, :]) - g_loga * params[1:2, :]
    g_step = g_dt * (1.0 - jnp.exp(-steps[:, :128]))
    first_ref[:, conv:] = g_step.astype(BF16)
    gstep_ref[0:1, :] += jnp.sum(g_step, axis=0, keepdims=True)
    gstep_ref[1:2, :] += jnp.sum(g_loga * steps[:, 128:], axis=0, keepdims=True)


def ssm_specs(heads, at):
    width = heads * HP
    return [
        pl.BlockSpec(memory_space=pltpu.SMEM),
        pl.BlockSpec(memory_space=pltpu.SMEM),
        pl.BlockSpec((SPAN, width + 2 * NS), lambda i: (at(i), 0)),
        pl.BlockSpec((SPAN, 256), lambda i: (at(i), 0)),
        pl.BlockSpec((16, SPAN), lambda i: (0, at(i))),
        pl.BlockSpec((SPAN, 1), lambda i: (at(i), 0)),
        pl.BlockSpec((1, SPAN), lambda i: (0, at(i))),
    ]


def ssm_forward(heads, inputs):
    length = inputs[2].shape[0]
    steps = length // SPAN
    width = heads * HP
    return pl.pallas_call(
        functools.partial(ssm_fwd_kernel, heads),
        grid=(steps,),
        in_specs=ssm_specs(heads, lambda i: i),
        out_specs=[
            pl.BlockSpec((SPAN, width), lambda i: (i, 0)),
            pl.BlockSpec((1, width, NS), lambda i: (i, 0, 0)),
        ],
        out_shape=[
            jax.ShapeDtypeStruct((length, width), F32),
            jax.ShapeDtypeStruct((steps, width, NS), F32),
        ],
        scratch_shapes=[pltpu.VMEM((width, NS), F32), pltpu.VMEM((SPAN, width), BF16)],
        compiler_params=pltpu.CompilerParams(vmem_limit_bytes=32 * 1024 * 1024),
        cost_estimate=pl.CostEstimate(
            flops=10**9, bytes_accessed=4 * 10**7, transcendentals=10**6
        ),
        name="ssm_forward",
    )(*inputs)


def ssm_backward(heads, inputs, states, gate_z, g_ym, ssm_y, stats, gain, pre, cin, up, taps, params):
    length = inputs[2].shape[0]
    steps = length // SPAN
    width = heads * HP
    conv = width + 2 * NS
    total = conv + 128

    def at(i):
        return steps - 1 - i

    def part(size):
        return pl.BlockSpec((SPAN, size), lambda i: (at(i), 0))

    def fixed(shape):
        return pl.BlockSpec(shape, lambda i: (0, 0))

    return pl.pallas_call(
        functools.partial(ssm_bwd_kernel, heads),
        grid=(steps,),
        in_specs=ssm_specs(heads, at)
        + [
            pl.BlockSpec((1, width, NS), lambda i: (at(i), 0, 0)),
            part(width),
            part(width),
            part(width),
            part(stats.shape[1]),
            fixed(gain.shape),
            part(conv),
            part(conv),
            part(up.shape[1]),
            fixed(taps.shape),
            fixed(params.shape),
        ],
        out_specs=[part(total), fixed((8, conv)), fixed((8, width)), fixed((8, 128))],
        out_shape=[
            jax.ShapeDtypeStruct((length, total), BF16),
            jax.ShapeDtypeStruct((8, conv), F32),
            jax.ShapeDtypeStruct((8, width), F32),
            jax.ShapeDtypeStruct((8, 128), F32),
        ],
        scratch_shapes=[
            pltpu.VMEM((width, NS), F32),
            pltpu.VMEM((SPAN + 8, conv), F32),
            pltpu.VMEM((256, SPAN), F32),
            pltpu.VMEM((SPAN, width), BF16),
            pltpu.VMEM((SPAN, width), BF16),
        ],
        compiler_params=pltpu.CompilerParams(vmem_limit_bytes=56 * 1024 * 1024),
        cost_estimate=pl.CostEstimate(
            flops=10**7, bytes_accessed=10**6, transcendentals=10**4
        ),
        name="ssm_backward",
    )(*inputs, states, gate_z, g_ym, ssm_y, stats, gain, pre, cin, up, taps, params)


def allowed_keys(index, reach, seg_c, seg_r):
    row = lax.broadcasted_iota(jnp.int32, (QBLK, reach), 0) + index * QBLK
    col = lax.broadcasted_iota(jnp.int32, (QBLK, reach), 1)
    return (seg_c[...] == seg_r[:, :reach]) & (col <= row)


def attn_fwd_kernel(heads, blocks, qkv_ref, seg_c, seg_r, out_ref, lse_ref):
    wide = heads * HD
    for index in range(blocks):

        @pl.when(pl.program_id(0) == index)
        def _(index=index):
            reach = (index + 1) * QBLK
            allowed = allowed_keys(index, reach, seg_c, seg_r)
            own = slice(index * QBLK, reach)
            keys = qkv_ref[:reach, wide : wide + HD]
            values = qkv_ref[:reach, wide + HD : wide + 2 * HD]
            for h in range(heads):
                lanes = slice(h * HD, (h + 1) * HD)
                scores = nt(qkv_ref[own, lanes], keys) * (HD**-0.5)
                scores = jnp.where(allowed, scores, MASKED)
                top = jnp.max(scores, axis=1, keepdims=True)
                expo = jnp.exp(scores - top)
                total = jnp.sum(expo, axis=1, keepdims=True)
                probs = (expo * (1.0 / total)).astype(BF16)
                out_ref[:, lanes] = nn(probs, values).astype(BF16)
                lse_ref[:, h : h + 1] = top + jnp.log(total)


def attn_bwd_kernel(
    heads, blocks, qkv_ref, seg_c, seg_r, lse_ref, go_ref, cosine, sine, out_ref, grads
):
    wide = heads * HD

    @pl.when(pl.program_id(0) == 0)
    def _():
        grads[...] = jnp.zeros_like(grads)

    for index in range(blocks):

        @pl.when(pl.program_id(0) == index)
        def _(index=index):
            reach = (index + 1) * QBLK
            allowed = allowed_keys(index, reach, seg_c, seg_r)
            own = slice(index * QBLK, reach)
            keys = qkv_ref[:reach, wide : wide + HD]
            values = qkv_ref[:reach, wide + HD : wide + 2 * HD]
            for h in range(heads):
                lanes = slice(h * HD, (h + 1) * HD)
                query = qkv_ref[own, lanes]
                g_out = go_ref[:, lanes]
                scores = nt(query, keys) * (HD**-0.5)
                probs = jnp.where(allowed, jnp.exp(scores - lse_ref[:, h : h + 1]), 0.0)
                g_probs = nt(g_out, values)
                delta = jnp.sum(probs * g_probs, axis=1, keepdims=True)
                g_scores = (probs * (g_probs - delta)).astype(BF16)
                grads[own, lanes] = nn(g_scores, keys) * (HD**-0.5)
                grads[:reach, wide : wide + HD] += tn(g_scores, query) * (HD**-0.5)
                grads[:reach, wide + HD : wide + 2 * HD] += tn(probs.astype(BF16), g_out)
            if index == blocks - 1:
                for b in range(blocks):
                    part = slice(b * QBLK, (b + 1) * QBLK)
                    slab = grads[part, :]
                    out_ref[part, :] = (
                        slab * cosine[part, :] - swap_halves(slab) * sine[part, :]
                    ).astype(BF16)


def attn_specs(length, slab):
    return [
        pl.BlockSpec((length, slab), lambda i: (0, 0)),
        pl.BlockSpec((QBLK, 1), lambda i: (i, 0)),
        pl.BlockSpec((1, length), lambda i: (0, 0)),
    ]


def attn_forward(heads, inputs):
    length, slab = inputs[0].shape
    blocks = length // QBLK
    return pl.pallas_call(
        functools.partial(attn_fwd_kernel, heads, blocks),
        grid=(blocks,),
        in_specs=attn_specs(length, slab),
        out_specs=[
            pl.BlockSpec((QBLK, heads * HD), lambda i: (i, 0)),
            pl.BlockSpec((QBLK, heads), lambda i: (i, 0)),
        ],
        out_shape=[
            jax.ShapeDtypeStruct((length, heads * HD), BF16),
            jax.ShapeDtypeStruct((length, heads), F32),
        ],
        compiler_params=pltpu.CompilerParams(vmem_limit_bytes=32 * 1024 * 1024),
        cost_estimate=pl.CostEstimate(
            flops=10**9, bytes_accessed=2 * 10**7, transcendentals=10**6
        ),
        name="attn_forward",
    )(*inputs)


def attn_backward(heads, inputs, lse, g_out, cosine, sine):
    length, slab = inputs[0].shape
    blocks = length // QBLK
    full = pl.BlockSpec((length, slab), lambda i: (0, 0))
    return pl.pallas_call(
        functools.partial(attn_bwd_kernel, heads, blocks),
        grid=(blocks,),
        in_specs=attn_specs(length, slab)
        + [
            pl.BlockSpec((QBLK, heads), lambda i: (i, 0)),
            pl.BlockSpec((QBLK, heads * HD), lambda i: (i, 0)),
            full,
            full,
        ],
        out_specs=full,
        out_shape=jax.ShapeDtypeStruct((length, slab), BF16),
        scratch_shapes=[pltpu.VMEM((length, slab), F32)],
        compiler_params=pltpu.CompilerParams(vmem_limit_bytes=56 * 1024 * 1024),
        cost_estimate=pl.CostEstimate(
            flops=10**7, bytes_accessed=10**6, transcendentals=10**4
        ),
        name="attn_backward",
    )(*inputs, lse, g_out, cosine, sine)


def ff_kernel(both, product, g_gate, g_up, gb, out):
    rows = both.shape[1]
    out[0, :rows] = tn(both[...], g_gate[...]).astype(BF16)
    out[0, rows : 2 * rows] = tn(both[...], g_up[...]).astype(BF16)
    out[0, 2 * rows :] = tn(product[...], gb[...]).astype(BF16)


def ff_gradients(m, both, product, g_gate, g_up, gb):
    tokens, dim = both.shape
    rows, down = dim // m, product.shape[1] // m
    full = pl.BlockSpec((tokens, dim), lambda i: (0, 0))
    return pl.pallas_call(
        ff_kernel,
        grid=(m,),
        in_specs=[
            pl.BlockSpec((tokens, rows), lambda i: (0, i)),
            pl.BlockSpec((tokens, down), lambda i: (0, i)),
            full,
            full,
            full,
        ],
        out_specs=pl.BlockSpec((1, 2 * rows + down, dim), lambda i: (i, 0, 0)),
        out_shape=jax.ShapeDtypeStruct((m, 2 * rows + down, dim), BF16),
        compiler_params=pltpu.CompilerParams(vmem_limit_bytes=40 * 1024 * 1024),
        cost_estimate=pl.CostEstimate(
            flops=6 * tokens * dim * dim, bytes_accessed=10**7, transcendentals=0
        ),
        name="ff_gradients",
    )(both, product, g_gate, g_up, gb)


def row_totals(values):
    ones = jnp.ones((8, values.shape[1]), F32)
    return lax.dot_general(
        ones, values, (((1,), (1,)), ((), ())), precision=HIGH, preferred_element_type=F32
    )


def finish_ff_kernel(core, own, mate, w_gate, w_up, gain, gate_ref, up_ref, down_ref, gain_ref):
    rows = w_gate.shape[0]
    tiles = own.shape[1] // 128
    total = jnp.zeros((rows, 128), F32)
    for half in range(2):
        mine = core[0] == half

        def pick(low, high, lanes, mine=mine):
            return jnp.where(mine, own[low:high, lanes], mate[low:high, lanes]).astype(F32)

        for f in range(tiles):
            lanes = slice(f * 128, (f + 1) * 128)
            to = slice((2 * f + half) * 128, (2 * f + half + 1) * 128)
            gate_ref[:, to] = pick(0, rows, lanes)
            up_ref[:, to] = pick(rows, 2 * rows, lanes)
        down = down_ref.shape[0] // 2
        down_ref[half * down : (half + 1) * down, :] = pick(2 * rows, 2 * rows + down, slice(None))
    for t in range(2 * tiles):
        lanes = slice(t * 128, (t + 1) * 128)
        total = total + gate_ref[:, lanes] * w_gate[:, lanes].astype(F32)
        total = total + up_ref[:, lanes] * w_up[:, lanes].astype(F32)
    gain_ref[...] = row_totals(total) / gain[...]


def finish_ff(core, own, mate, w_gate, w_up, gain):
    shard, ff = w_gate.shape
    down = own.shape[0] - 2 * shard
    vmem = pl.BlockSpec(memory_space=pltpu.VMEM)
    out = pl.pallas_call(
        finish_ff_kernel,
        in_specs=[pl.BlockSpec(memory_space=pltpu.SMEM)] + [vmem] * 5,
        out_specs=[vmem] * 4,
        out_shape=[
            jax.ShapeDtypeStruct((shard, ff), F32),
            jax.ShapeDtypeStruct((shard, ff), F32),
            jax.ShapeDtypeStruct((2 * down, own.shape[1]), F32),
            jax.ShapeDtypeStruct((8, shard), F32),
        ],
        compiler_params=pltpu.CompilerParams(vmem_limit_bytes=40 * 1024 * 1024),
        name="finish_ff",
    )(core.astype(jnp.int32)[None], own, mate, w_gate, w_up, gain.astype(F32)[None])
    return out[0], out[1], out[2], out[3][0]


def finish_kernel(
    place,
    own,
    mates,
    w_in,
    w_qkv,
    w_out,
    gain_in,
    gain_m,
    in_ref,
    qkv_ref,
    out_ref,
    o_ref,
    gain_in_ref,
    gain_m_ref,
    small_ref,
    steps,
):
    count = 2 * own.shape[0]
    shard = w_qkv.shape[0]
    heads = MH // count
    width = heads * HP
    conv = width + 2 * NS
    late = conv + 128
    q_width = QH * HD // count
    wide = count * width
    steps[...] = jnp.zeros_like(steps)
    shared = jnp.zeros((shard, 2 * NS), F32)
    gain = jnp.zeros((1, shard), F32)
    small = jnp.zeros((shard, 128), F32)
    pairs = []

    def lay(at, values, gain):
        flat = jnp.transpose(values)
        rows = slice(at, at + flat.shape[0])
        in_ref[rows, :] = flat
        return gain + jnp.sum(flat * w_in[rows, :].astype(F32), axis=0, keepdims=True)

    for j in range(count):

        at_x = (place[0] + j // 2) % 2
        mine = place[1] == j % 2

        def pick(rows, lanes, at_x=at_x, mine=mine):
            return jnp.where(mine, own[at_x, rows, lanes], mates[at_x, rows, lanes]).astype(F32)

        def part(low, high, pick=pick):
            return pick(slice(None), slice(low, high))

        gain = lay(j * width, part(late, late + width), gain)
        gain = lay(wide + j * width, part(0, width), gain)
        shared = shared + part(width, conv)
        steps[:, j * heads : (j + 1) * heads] = part(conv, conv + heads)
        at = late + width
        qkv_ref[:, j * q_width : (j + 1) * q_width] = part(at, at + q_width)
        pairs.append(part(at + q_width, at + q_width + 128))
        at = at + q_width + 128
        lanes = slice(at, own.shape[2])
        rows = pick(slice(0, shard // 2), lanes), pick(slice(shard // 2, shard), lanes)
        rows = jnp.concatenate(rows, axis=1)
        low = j * (shard // 2)
        if low < out_ref.shape[0]:
            out_ref[low : low + shard // 2, :] = rows
        else:
            low -= out_ref.shape[0]
            o_ref[low : low + shard // 2, :] = rows
        small = small + part(conv, late)
    gain = lay(2 * wide, shared, gain)
    at = 2 * wide + 2 * NS
    flat = jnp.transpose(steps[...])[: in_ref.shape[0] - at, :]
    in_ref[at:, :] = flat
    gain = gain + jnp.sum(flat * w_in[at:, :].astype(F32), axis=0, keepdims=True)
    one, two = pairs[0] + pairs[1], pairs[2] + pairs[3]
    low = lax.broadcasted_iota(jnp.int32, one.shape, 1) < HD
    at = QH * HD
    qkv_ref[:, at : at + 128] = jnp.where(low, one, pltpu.roll(two, HD, 1))
    qkv_ref[:, at + 128 :] = jnp.where(low, pltpu.roll(one, HD, 1), two)
    gain = row_totals(qkv_ref[...] * w_qkv[...].astype(F32)) + gain
    gain_in_ref[...] = gain / gain_in[...]
    gain_m_ref[...] = row_totals(out_ref[...] * w_out[...].astype(F32)) / gain_m[...]
    small_ref[...] = jnp.transpose(small)


def finish(place, own, mates, w_in, w_qkv, w_out, w_o, gain_in, gain_m):
    shard = w_qkv.shape[0]
    vmem = pl.BlockSpec(memory_space=pltpu.VMEM)
    shapes = [w_in.shape[::-1], w_qkv.shape, w_out.shape, w_o.shape]
    shapes += [(8, shard), (8, w_out.shape[0]), (128, shard)]
    out = pl.pallas_call(
        finish_kernel,
        in_specs=[pl.BlockSpec(memory_space=pltpu.SMEM)] + [vmem] * 7,
        out_specs=[vmem] * 7,
        out_shape=[jax.ShapeDtypeStruct(shape, F32) for shape in shapes],
        scratch_shapes=[pltpu.VMEM((shard, 128), F32)],
        compiler_params=pltpu.CompilerParams(vmem_limit_bytes=40 * 1024 * 1024),
        name="finish",
    )(place, own, mates, w_in.T, w_qkv, w_out, gain_in.astype(F32)[None], gain_m.astype(F32)[None])
    return out[0].T, out[1], out[2], out[3], out[4][0], out[5][0], out[6]


def tie(value, *after):
    return lax.optimization_barrier((value,) + after)[0]


def stage(compute, inputs, sends, late=()):
    inputs, operands = lax.optimization_barrier((inputs, [operand for _, operand in sends]))
    got = [send(operand) for (send, _), operand in zip(sends, operands)]
    out, got, late = lax.optimization_barrier((compute(*inputs), got, late))
    return (out, got, late) if late else (out, got)


class Net:
    def __init__(self):
        self.n = lax.axis_size("ctx")
        self.m = lax.axis_size("fsdp")
        self.c = lax.axis_index("ctx")
        self.f = lax.axis_index("fsdp")
        self.direct = self.n == 4 and self.m == 8
        self.x, self.core = self.c // 2, self.c % 2
        self.z, self.y = self.f // 2, self.f % 2
        self.by_core = [[i * 2 + k for i in range(self.n // 2)] for k in range(2)]

    def flip(self, value, axis, bit):
        size = lax.axis_size(axis)
        return lax.ppermute(value, axis, [(i, i ^ bit) for i in range(size)])

    def shift_z(self, value, by):
        return lax.ppermute(value, "fsdp", [(i, (i + 2 * by) % self.m) for i in range(self.m)])

    def cross(self, value):
        pairs = [
            (c * 8 + z * 2 + y, z * 8 + c * 2 + y)
            for c in range(4)
            for z in range(4)
            for y in range(2)
        ]
        return lax.ppermute(value, ("ctx", "fsdp"), pairs)

    def along_z(self, block):
        return [block] + [self.shift_z(block, k) for k in range(1, 4)]

    def along_y(self, pieces):
        return [self.flip(piece, "fsdp", 1) for piece in pieces]

    def in_order(self, own, mate, columns=None):
        places = [2 * ((self.z - k) % 4) + (self.y ^ o) for o in range(2) for k in range(4)]
        return put(own + mate, places, columns)

    def flip_y(self, value):
        return self.flip(value, "fsdp", 1)

    def flip_x(self, value):
        return self.flip(value, "ctx", 2)

    def flip_core(self, value):
        return self.flip(value, "ctx", 1)

    def halves_y(self, sums):
        low = sums.astype(BF16)
        low = low.reshape((4, 2) + low.shape[1:])
        away = lax.dynamic_index_in_dim(low, 1 - self.y, 1, False)
        return lax.dynamic_index_in_dim(low, self.y, 1, False), away

    def shifts_z(self, both):
        return self.send_z(self.blocks_z(both))

    def blocks_z(self, both):
        return [lax.dynamic_index_in_dim(both, (self.z + k) % 4, 0, False) for k in range(4)]

    def send_z(self, blocks):
        return [blocks[0]] + [self.shift_z(blocks[k], k) for k in range(1, 4)]

    def collect(self, sums):
        return lax.psum_scatter(sums.astype(BF16), "fsdp", scatter_dimension=0, tiled=False)

    def ctx_all(self, value):
        if not self.direct:
            return lax.all_gather(value, "ctx", axis=0, tiled=False)
        pair = jnp.stack([value, self.flip(value, "ctx", 2)])
        mates = self.flip(pair, "ctx", 1)
        return put([pair, mates], [self.c, self.c ^ 2, self.c ^ 1, self.c ^ 3])

    def ctx_sum(self, value):
        if not self.direct:
            return lax.psum(value, "ctx")
        value = value + self.flip(value, "ctx", 1)
        return value + self.flip(value, "ctx", 2)

    def ctx_collect(self, parts):
        if not self.direct:
            low = lax.psum_scatter(parts.astype(BF16), "ctx", scatter_dimension=0, tiled=False)
            return low.astype(F32)
        own, away = self.ctx_halves(parts)
        return own + self.flip(away, "ctx", 2).astype(F32)

    def ctx_halves(self, parts):
        pairs = parts.reshape((2, 2) + parts.shape[1:])
        away = lax.dynamic_index_in_dim(pairs, 1 - self.core, 1, False).astype(BF16)
        here = lax.dynamic_index_in_dim(pairs, self.core, 1, False)
        got = self.flip(away, "ctx", 1)

        def half(which):
            return lax.dynamic_index_in_dim(here, which, 0, False).astype(
                F32
            ) + lax.dynamic_index_in_dim(got, which, 0, False).astype(F32)

        return half(self.x), half(1 - self.x).astype(BF16)

    def over_cores(self, value):
        value = lax.psum(value, "ctx", axis_index_groups=self.by_core)
        return lax.all_gather(value, "ctx", axis=0)[:2].astype(F32)

    def rows_out(self, shard):
        per = self.m // self.n
        got = lax.all_gather(shard, "fsdp", axis=0, tiled=False)
        return lax.dynamic_slice_in_dim(got, self.c * per, per, 0)

    def rows_back(self, sums):
        wide = jnp.zeros((self.m,) + sums.shape[1:], BF16)
        wide = lax.dynamic_update_slice_in_dim(
            wide, sums.astype(BF16), self.c * (self.m // self.n), 0
        )
        out = lax.psum_scatter(wide, "fsdp", scatter_dimension=0, tiled=False)
        return lax.psum(out, "ctx")


def put_kernel(counts, cuts, places, *refs):
    parts, outs = refs[: len(counts)], refs[len(counts) :]
    start = 0
    for part, count in zip(parts, counts):

        @pl.when((pl.program_id(0) >= start) & (pl.program_id(0) < start + count))
        def _(part=part):
            for out, low, high in zip(outs, cuts[:-1], cuts[1:]):
                out[...] = part[..., low:high]

        start += count


def put(parts, places, columns=None):
    counts = [part.shape[0] for part in parts]
    total = sum(counts)
    shape = parts[0].shape[1:]
    zeros = (0,) * len(shape)
    sizes = columns or [shape[-1]]
    cuts = [0]
    for size in sizes:
        cuts.append(cuts[-1] + size)
    places = jnp.stack([jnp.asarray(p, jnp.int32) for p in places])
    size = parts[0][0].size * parts[0].dtype.itemsize
    specs = []
    for p in range(len(parts)):
        start = sum(counts[:p])

        def at(i, at, start=start, last=counts[p] - 1):
            return (jnp.clip(i - start, 0, last),) + zeros

        specs.append(pl.BlockSpec((1,) + shape, at))
    out = pl.pallas_call(
        functools.partial(put_kernel, counts, cuts),
        grid_spec=pltpu.PrefetchScalarGridSpec(
            num_scalar_prefetch=1,
            grid=(total,),
            in_specs=specs,
            out_specs=[
                pl.BlockSpec((1,) + shape[:-1] + (w,), lambda i, at: (at[i],) + zeros)
                for w in sizes
            ],
        ),
        out_shape=[
            jax.ShapeDtypeStruct((total,) + shape[:-1] + (w,), parts[0].dtype) for w in sizes
        ],
        compiler_params=pltpu.CompilerParams(vmem_limit_bytes=40 * 1024 * 1024),
        cost_estimate=pl.CostEstimate(
            flops=0, bytes_accessed=2 * total * size, transcendentals=0
        ),
        name="put",
    )(places, *parts)
    return out if columns else out[0]


def rms_scale(values):
    return lax.rsqrt(jnp.mean(values * values, axis=-1, keepdims=True) + EPSILON)


def rms_back(values, gain, scale, grad):
    scaled = grad * gain
    inner = jnp.mean(values * scaled, axis=-1, keepdims=True)
    return scale * scaled - values * (scale * scale * scale * inner)


def columns_of(w, start, size):
    return lax.dynamic_slice_in_dim(w, start, size, 1)


def rotary_tables(length, q_heads, slab):
    half = HD // 2
    freq = (ROPE_BASE ** (-(np.arange(half) * 2.0 / HD))).astype(np.float32)
    angle = np.arange(length, dtype=np.float32)[:, None] * freq[None, :]
    one = np.concatenate([np.cos(angle), np.cos(angle)], axis=1)
    two = np.concatenate([-np.sin(angle), np.sin(angle)], axis=1)
    room = slab - (q_heads + 1) * HD
    cosine = np.concatenate([one] * (q_heads + 1) + [np.ones((length, room))], axis=1)
    sine = np.concatenate([two] * (q_heads + 1) + [np.zeros((length, room))], axis=1)
    return jnp.asarray(cosine, F32), jnp.asarray(sine, F32)


def per_device(
    tokens,
    teacher,
    segment_ids,
    valid_mask,
    gain_in,
    w_in,
    conv_w,
    conv_b,
    dt_bias,
    a_log,
    d_skip,
    gain_m,
    w_out,
    w_qkv,
    w_o,
    gain_ffn,
    w_gate,
    w_up,
    w_down,
):
    net = Net()
    n, m, c, f = net.n, net.m, net.c, net.f
    rows, dim = tokens.shape[1:]
    length = segment_ids.shape[1]
    shard = w_in.shape[0]
    wide = MH * HP
    conv_full = wide + 2 * NS
    heads = MH // n
    q_heads = QH // n
    width = heads * HP
    conv_width = width + 2 * NS
    q_width = q_heads * HD
    slab = q_width + 2 * HD
    slab += -slab % 128
    group = QH // KVH
    kv_at = (c * q_heads) // group
    ff = w_gate.shape[1]
    ff_shard = w_down.shape[0]
    per = m // n
    seg = segment_ids[0]
    seg_c, seg_r = seg[:, None], seg[None, :]
    ends = jnp.concatenate([jnp.full((1,), -1, jnp.int32), seg[SPAN - 1 :: SPAN]])
    valid = valid_mask[0].astype(F32)

    def lay(values):
        values = values.reshape((-1, values.shape[-1]))
        room = -values.shape[1] % 128
        return jnp.pad(values, ((0, 0), (0, room))).reshape(-1, 128)

    def unlay(small, start, lead, size):
        room = size + -size % 128
        count = lead * room // 128
        return small[..., start : start + count, :].reshape(small.shape[:-2] + (lead, room))[
            ..., :size
        ]

    shapes = [(1, shard), (1, shard), (1, w_out.shape[0]), (1, conv_b.shape[0])]
    shapes += [(KW, conv_b.shape[0])]
    starts = [0]
    for lead, size in shapes:
        starts.append(starts[-1] + lead * (size + -size % 128) // 128)
    laid = [lay(p) for p in (gain_in[None], gain_ffn[None], gain_m[None], conv_b[None], conv_w)]
    laid.append(jnp.full((1, 128), jnp.sum(valid), F32).astype(BF16))
    laid.append(jnp.zeros((-(starts[-1] + 1) % 16, 128), BF16))
    at_small = 64
    packed = jnp.concatenate(laid, axis=0)
    first = jnp.concatenate(
        [
            columns_of(w_in, wide + c * width, width),
            w_in[:, 2 * wide : 2 * wide + 2 * NS],
            columns_of(w_in, wide + conv_full + c * heads, heads),
            jnp.zeros((shard, at_small - heads), BF16),
            packed.T if net.direct else jnp.zeros((shard, packed.shape[0]), BF16),
            jnp.zeros((shard, 128 - at_small - packed.shape[0]), BF16),
        ],
        axis=1,
    )
    second = jnp.concatenate(
        [
            columns_of(w_in, c * width, width),
            columns_of(w_qkv, c * q_width, q_width),
            columns_of(w_qkv, QH * HD + kv_at * HD, HD),
            columns_of(w_qkv, (QH + KVH) * HD + kv_at * HD, HD),
            jnp.zeros((shard, slab - q_width - 2 * HD), BF16),
        ],
        axis=1,
    )
    both_out = jnp.concatenate([w_out, w_o], axis=0)
    out_rows, mamba_rows = both_out.shape[0], w_out.shape[0]
    ff_half = ff_shard // 2
    size = m * ff_half

    def ff_cut(w):
        w = w.reshape(shard, m, 2, ff_half)
        return lax.dynamic_index_in_dim(w, net.core, 2, False).reshape(shard, size)

    places_x = n // 2

    def quarter_x(w):
        size = w.shape[0] // places_x
        return lax.dynamic_slice_in_dim(w, net.x * size, size, 0)

    w_ff = jnp.concatenate(
        [
            quarter_x(ff_cut(w_gate).reshape(-1, dim)),
            quarter_x(ff_cut(w_up).reshape(-1, dim)),
            quarter_x(lax.dynamic_slice_in_dim(w_down, net.core * ff_half, ff_half, 0)),
        ],
        axis=0,
    )
    groups = [[d * m + i for d in net.by_core[k] for i in range(m)] for k in range(2)]
    w_ff = lax.all_gather(
        w_ff, ("ctx", "fsdp"), axis=0, tiled=False, axis_index_groups=groups
    ).reshape((places_x, m) + w_ff.shape)
    if net.direct:
        both_cols = jnp.concatenate([first, second], axis=1)
        near = net.along_z(both_cols)
        own_tokens = tie(tokens[0], near[1])
        pair = jnp.stack([own_tokens, net.flip_x(own_tokens)])
        far = net.along_y(near)
        all_tokens = put([pair, net.flip_core(pair)], [c, c ^ 2, c ^ 1, c ^ 3])
        w_first, w_second = net.in_order(
            [tie(near[0], all_tokens)[None]] + [p[None] for p in near[1:]],
            [p[None] for p in far],
            [first.shape[1], second.shape[1]],
        )
        at = conv_width + at_small
        small = jnp.swapaxes(w_first[:, :, at : at + packed.shape[0]], 1, 2)
        crossed = net.cross(tie(both_out, *near[1:]))
    else:
        small = lax.all_gather(packed, "fsdp", axis=0, tiled=False)
        w_first = lax.all_gather(first, "fsdp", axis=0, tiled=False)
        w_second = lax.all_gather(second, "fsdp", axis=0, tiled=False)
        w_outs = net.rows_out(both_out)
        all_tokens = net.ctx_all(tokens[0])
    all_tokens = all_tokens.reshape(length, dim)
    w_first = w_first.reshape(dim, first.shape[1])
    cuts = [
        jnp.transpose(unlay(small, start, *shape), (1, 0, 2)).reshape(shape[0], -1)
        for start, shape in zip(starts, shapes)
    ]
    gain_input = cuts[0].astype(F32)
    gain_second = cuts[1].astype(F32)
    gain_mamba = lax.dynamic_slice_in_dim(cuts[2], c * width, width, 1).astype(F32)
    count_ctx = jnp.sum(small[:, starts[-1], 0].astype(F32))

    def conv_cut(values):
        own = lax.dynamic_slice_in_dim(values, c * width, width, 1)
        return jnp.concatenate([own, values[:, wide:]], axis=1).astype(F32)

    bias, taps = conv_cut(cuts[3]), conv_cut(cuts[4])
    rate = jnp.exp(a_log)
    params = jnp.stack(
        [lax.dynamic_slice_in_dim(v, c * heads, heads) for v in (dt_bias, rate)]
    )
    params = jnp.pad(params, ((0, 6), (0, 128 - heads)))
    skip = lax.dynamic_slice_in_dim(d_skip, c * heads, heads)

    def shifted(by):
        return jnp.concatenate([jnp.full((by,), -1, jnp.int32), seg[: length - by]]) == seg

    same = jnp.stack([shifted(by) for by in range(KW)], axis=1).astype(F32)
    up = jnp.stack(
        [
            jnp.concatenate([seg[by:], jnp.full((by,), -1, jnp.int32)]) == seg
            for by in range(KW)
        ],
        axis=1,
    ).astype(F32)
    cosine, sine = rotary_tables(length, q_heads, slab)
    conv_args = (all_tokens, gain_input, w_first, taps, bias, same, params)

    def square_rows(square):
        return jnp.concatenate([square[0].reshape(-1, 128), jnp.full((8, 128), count_ctx)])

    def ssm(act, steps, step_rows):
        return ssm_forward(heads, (ends, skip, act, steps, step_rows, seg_c, seg_r))

    def attend(qkv):
        return attn_forward(q_heads, (qkv, seg_c, seg_r))

    w_second = w_second.reshape(dim, second.shape[1])
    if net.direct:
        normed, cin, pre, act, steps, step_rows = project_conv(*conv_args)
        ssm_y, states = ssm(act, steps, step_rows)
        gate_z, qkv, square = project_gate(normed, w_second, ssm_y, cosine, sine)
        mated = net.flip_y(tie(crossed, ssm_y))
        (attended, lse), (square,) = stage(
            attend, (qkv,), [(net.ctx_sum, square_rows(square))]
        )
        w_outs = jnp.where(
            net.y == 0, jnp.stack([crossed, mated]), jnp.stack([mated, crossed])
        )
    else:
        normed, cin, pre, act, steps, step_rows = project_conv(*conv_args)
        ssm_y, states = ssm(act, steps, step_rows)
        gate_z, qkv, square = project_gate(normed, w_second, ssm_y, cosine, sine)
        square = net.ctx_sum(square_rows(square))
        attended, lse = attend(qkv)
    w_mamba = w_outs[:, :mamba_rows].reshape(per * mamba_rows, dim)
    w_attn = w_outs[:, mamba_rows:].reshape(per * (out_rows - mamba_rows), dim)
    ssm_in = (ends, skip, act, steps, step_rows, seg_c, seg_r)
    count = square[-1, 0]
    scale_m = lax.rsqrt(square[:-8].reshape(length, 1) / wide + EPSILON)
    gated = ssm_y * (gate_z * jax.nn.sigmoid(gate_z))
    ym = (gated * scale_m * gain_mamba).astype(BF16)
    outs = nn(ym, w_mamba) + nn(attended, w_attn)
    ff_rows = shard * size // dim
    part_rows = ff_rows // places_x

    def plus(here, got):
        return (here.astype(F32) + got.astype(F32)).astype(BF16)

    def ff_weights(w_ff):
        def part(low, high, columns):
            return jnp.swapaxes(w_ff[:, :, low:high], 0, 1).reshape(-1, columns)

        return (
            part(0, part_rows, size),
            part(part_rows, 2 * part_rows, size),
            part(2 * part_rows, w_ff.shape[2], dim),
        )

    if net.direct:
        own, away = net.ctx_halves(outs.reshape(n, rows, dim))
        laid_out = ff_weights(w_ff)
        _, (across,), (w_g, w_u, w_d) = stage(tuple, (), [(net.flip_x, away)], laid_out)
        mixed = tokens[0].astype(F32) + own + across.astype(F32)
    else:
        w_g, w_u, w_d = ff_weights(w_ff)
        mixed = tokens[0].astype(F32) + net.ctx_collect(outs.reshape(n, rows, dim))

    scale2 = rms_scale(mixed)
    normed2 = (mixed * scale2 * gain_second).astype(BF16)
    mate = [(i, i ^ 1) for i in range(n)]
    both = jnp.concatenate([normed2, lax.ppermute(normed2, "ctx", mate)], axis=0)
    gate_v, up_v = nn(both, w_g), nn(both, w_u)
    sig = jax.nn.sigmoid(gate_v)
    product = (gate_v * sig * up_v).astype(BF16)
    down_out = nn(product, w_d)
    from_mate = lax.ppermute(down_out[rows:].astype(BF16), "ctx", mate)
    layer_out = mixed + down_out[:rows] + from_mate.astype(F32)
    diff = layer_out - teacher[0].astype(F32)
    squared = jnp.sum(valid[:, None] * diff * diff)
    token_total = length * m * tokens.shape[0]
    grad_out = token_total * valid[:, None] * diff / count

    gb = grad_out.astype(BF16)
    gb_both = jnp.concatenate([gb, lax.ppermute(gb, "ctx", mate)], axis=0)
    g_prod = nt(gb_both, w_d)
    g_gate = (g_prod * up_v * (sig * (1.0 + gate_v * (1.0 - sig)))).astype(BF16)
    g_up = (g_prod * gate_v * sig).astype(BF16)
    if net.direct:
        g_ff = ff_gradients(m, both, product, g_gate, g_up, gb_both)
    else:
        g_ff = jnp.concatenate(
            [
                tn(both, g_gate).reshape(m, ff_rows, dim),
                tn(both, g_up).reshape(m, ff_rows, dim),
                tn(product, gb_both).reshape(m, ff_half, dim),
            ],
            axis=1,
        ).astype(BF16)
    g_n2 = nt(tie(g_gate, g_ff), w_g) + nt(g_up, w_u)
    from_mate = lax.ppermute(g_n2[rows:].astype(BF16), "ctx", mate)
    grad_n2 = g_n2[:rows] + from_mate.astype(F32)
    part = rms_back(mixed, gain_second, scale2, grad_n2)
    grad_mixed = grad_out + part

    gm = net.ctx_all(grad_mixed.astype(BF16))
    gm = gm.reshape(length, dim)
    g_ff = lax.psum_scatter(g_ff, "fsdp", scatter_dimension=0, tiled=False)

    g_ym = nt(gm, w_mamba)
    inner = jnp.sum(gated * (g_ym * gain_mamba), axis=1).reshape(-1, 128)

    def outs_back(gm):
        g_ob = nt(gm, w_attn).astype(BF16)
        g_outs = jnp.concatenate(
            [
                tn(ym, gm).reshape(per, mamba_rows, dim),
                tn(attended, gm).reshape(per, out_rows - mamba_rows, dim),
            ],
            axis=1,
        )
        return g_ob, g_outs.astype(BF16)

    def attend_back(qkv, g_ob):
        return attn_backward(q_heads, (qkv, seg_c, seg_r), lse, g_ob, cosine, sine)

    def plus(here, got):
        return (here.astype(F32) + got.astype(F32)).astype(BF16)

    if net.direct:
        (g_ob, g_outs), (got,) = stage(outs_back, (gm,), [(net.flip_core, inner)])
        inner = inner + got
        here = lax.dynamic_index_in_dim(g_outs, net.y, 0, False)
        away = lax.dynamic_index_in_dim(g_outs, 1 - net.y, 0, False)
        got = net.flip_y(away)
        g_qkv, (got_x,) = stage(attend_back, (qkv, g_ob), [(net.flip_x, inner)])
        inner = inner + got_x
        out_both = plus(here, got).reshape(4, out_rows // 4, dim)
    else:
        g_ob, g_outs = outs_back(gm)
        inner = net.ctx_sum(inner)
        g_qkv = attend_back(qkv, g_ob)
    inner = inner.reshape(length, 1) / wide
    stats = jnp.concatenate([scale_m, scale_m * scale_m * scale_m * inner], axis=1)
    g_gated = stats[:, :1] * (g_ym * gain_mamba) - gated * stats[:, 1:]
    sig_z = jax.nn.sigmoid(gate_z)
    g_z = (g_gated * ssm_y * (sig_z + gate_z * sig_z * (1.0 - sig_z))).astype(BF16)
    early = jnp.concatenate([g_z, g_qkv], axis=1)
    grad_early = tn(normed, early).reshape(m, shard, width + slab)

    def ssm_back(states):
        return ssm_backward(
            heads,
            ssm_in,
            states,
            gate_z,
            g_ym,
            ssm_y,
            stats,
            gain_mamba,
            pre,
            cin,
            up,
            taps,
            params,
        )

    if net.direct:
        here, away = net.halves_y(grad_early)
        (g_late, g_conv, g_wide, g_steps), (got, out_parts) = stage(
            ssm_back, (states,), [(net.flip_y, away), (net.shifts_z, out_both)]
        )
        grad_early = plus(here, got)
        out_quarter = sum(p.astype(F32) for p in out_parts).astype(BF16)
    else:
        g_late, g_conv, g_wide, g_steps = ssm_back(states)

    def to_wide(values, at, size):
        out = jnp.zeros(values.shape[:-1] + (size,), F32)
        return lax.dynamic_update_slice_in_dim(out, values, at, values.ndim - 1)

    def for_shards(values):
        values = jnp.concatenate(
            [to_wide(values[:, :width], c * width, wide), values[:, width:]], axis=1
        )
        values = values.reshape((-1, m, values.shape[-1] // m))
        return jnp.transpose(values, (1, 0, 2))

    conv_rows = (conv_b.shape[0] + 127) // 128
    heads_grads = jnp.stack(
        [
            to_wide(g_steps[0, :heads], c * heads, MH),
            to_wide(g_steps[1, :heads], c * heads, MH),
            to_wide(jnp.sum(g_wide[0].reshape(heads, HP), axis=1), c * heads, MH),
            jnp.full((MH,), squared),
        ]
    )
    laid = [jax.vmap(lay)(for_shards(g_conv[: KW + 1]))]
    laid.append(jnp.broadcast_to(lay(heads_grads)[None], (m, 4, 128)))
    laid = jnp.concatenate(laid, axis=1)
    late_size = conv_width + 128
    grad_late = tn(normed, g_late).reshape(m, shard, late_size)
    if net.direct:
        laid = jnp.swapaxes(laid, 1, 2)
        ends_at = conv_width + at_small
        grad_late = jnp.concatenate(
            [grad_late[..., :ends_at], laid, grad_late[..., ends_at + laid.shape[2] :]], axis=2
        )
    grad_late = grad_late.astype(BF16)
    resid = tokens[0].astype(F32)

    def normed_back(early, g_late):
        return (nt(early, w_second) + nt(g_late, w_first)).reshape(n, rows, dim)

    def tokens_back(grad_normed):
        return grad_mixed + rms_back(resid, gain_input, rms_scale(resid), grad_normed)

    if net.direct:
        g_normed = normed_back(early, g_late)
        here, away = net.halves_y(grad_late)
        _, (grad_normed, got, early_parts) = stage(
            tuple,
            (),
            [
                (net.ctx_collect, g_normed),
                (net.flip_y, away),
                (net.shifts_z, grad_early),
            ],
        )
        grad_early = sum(p.astype(F32) for p in early_parts).astype(BF16)
        blocks = net.blocks_z(plus(here, got))
        g_ff = tie(g_ff, grad_early, *blocks)
        got_ff = net.flip_x(g_ff)
        grad_tokens, (late_parts, out_quarter), (got_ff,) = stage(
            tokens_back,
            (grad_normed,),
            [(net.send_z, blocks), (net.cross, out_quarter)],
            (got_ff,),
        )
        g_ff = plus(g_ff, got_ff)
        grad_late = sum(p.astype(F32) for p in late_parts).astype(BF16)
        joined = jnp.concatenate([out_quarter[:, : dim // 2], out_quarter[:, dim // 2 :]], axis=0)
        joined = jnp.concatenate([grad_early, joined], axis=1)
        joined = jnp.concatenate([grad_late, joined], axis=1)
        def finish_halves(g_ff, got_ff):
            return finish_ff(net.core, g_ff, got_ff, w_gate, w_up, gain_ffn)

        ff_out, (across,) = stage(
            finish_halves, (g_ff, net.flip_core(g_ff)), [(net.flip_x, joined)]
        )
        out_gate, out_up, out_down, out_gain_ffn = ff_out
        joined = jnp.stack([joined, across])
        mates = net.flip_core(joined)
        place = jnp.stack([net.x, net.core]).astype(jnp.int32)
        out_w_in, out_w_qkv, out_mamba, out_attn, out_gain_in, out_gain_m, totals = finish(
            place, joined, mates, w_in, w_qkv, w_out, w_o, gain_in, gain_m
        )
        totals = totals[at_small : at_small + laid.shape[2]]
    else:
        grad_tokens = tokens_back(net.ctx_collect(normed_back(early, g_late)))
        got_early = net.ctx_all(net.collect(grad_early)).astype(F32)
        got_late = net.ctx_all(net.collect(grad_late))
        out_outs = net.rows_back(g_outs).astype(F32)
        got_ff = net.over_cores(g_ff)
        got_late = got_late.astype(F32)
        totals = lax.psum_scatter(laid, "fsdp", scatter_dimension=0, tiled=False)
        totals = lax.psum(totals, "ctx")
        def side(got, start, size):
            return [got[j][:, start : start + size] for j in range(n)]

        shared = n // KVH
        out_w_in = jnp.concatenate(
            side(got_early, 0, width)
            + side(got_late, 0, width)
            + [sum(side(got_late, width, 2 * NS))]
            + side(got_late, conv_width, heads),
            axis=1,
        )
        out_w_qkv = jnp.concatenate(
            side(got_early, width, q_width)
            + [
                sum(side(got_early, width + q_width + i * HD, HD)[k * shared : (k + 1) * shared])
                for i in range(2)
                for k in range(KVH)
            ],
            axis=1,
        )

        def ff_wide(values):
            values = values.reshape(2, shard, m, ff_half)
            return jnp.transpose(values, (1, 2, 0, 3)).reshape(shard, ff)

        out_gate = ff_wide(got_ff[:, :ff_rows])
        out_up = ff_wide(got_ff[:, ff_rows : 2 * ff_rows])
        out_mamba = out_outs[:mamba_rows]

        def along(*pairs):
            return sum(jnp.sum(w.astype(F32) * g, axis=1) for w, g in pairs)

        out_attn = out_outs[mamba_rows:]
        out_down = got_ff[:, 2 * ff_rows :].reshape(ff_shard, dim)
        out_gain_in = along((w_in, out_w_in), (w_qkv, out_w_qkv)) / gain_in.astype(F32)
        out_gain_m = along((w_out, out_mamba)) / gain_m.astype(F32)
        out_gain_ffn = along((w_gate, out_gate), (w_up, out_up)) / gain_ffn.astype(F32)
    grad_conv = unlay(totals, 0, KW + 1, conv_b.shape[0])
    head_totals = totals[(KW + 1) * conv_rows : (KW + 1) * conv_rows + 4, :MH]
    loss = head_totals[3, 0] / (2.0 * count)
    return (
        loss,
        layer_out[None],
        grad_tokens[None],
        out_gain_in,
        out_w_in,
        grad_conv[:KW],
        grad_conv[KW],
        head_totals[0],
        head_totals[1],
        head_totals[2],
        out_gain_m,
        out_mamba,
        out_w_qkv,
        out_attn,
        out_gain_ffn,
        out_gate,
        out_up,
        out_down,
    )


def solution(mesh):
    in_specs = (
        P("fsdp", "ctx", None),
        P("fsdp", "ctx", None),
        P("fsdp", None),
        P("fsdp", "ctx"),
        P("fsdp"),
        P("fsdp", None),
        P(None, "fsdp"),
        P("fsdp"),
        P(),
        P(),
        P(),
        P("fsdp"),
        P("fsdp", None),
        P("fsdp", None),
        P("fsdp", None),
        P("fsdp"),
        P("fsdp", None),
        P("fsdp", None),
        P("fsdp", None),
    )
    out_specs = (
        P(),
        P("fsdp", "ctx", None),
        P("fsdp", "ctx", None),
        P("fsdp"),
        P("fsdp", None),
        P(None, "fsdp"),
        P("fsdp"),
        P(),
        P(),
        P(),
        P("fsdp"),
        P("fsdp", None),
        P("fsdp", None),
        P("fsdp", None),
        P("fsdp"),
        P("fsdp", None),
        P("fsdp", None),
        P("fsdp", None),
    )
    return jax.shard_map(
        per_device, mesh=mesh, in_specs=in_specs, out_specs=out_specs, check_vma=False
    )
```
